32 devices in a mesh: dp: 2 (over core), fsdp: 16 (over z, y, x).
Axes of the slice: x: 2, y: 2, z: 4, core: 2. Of those that a mesh axis runs over, the one named last changes fastest.
Arguments:
- patches: bfloat16 [128, 576, 768], P(('dp', 'fsdp')), may hold values from -6 to 6
- resolution: int32 [128], P(('dp', 'fsdp')), may hold values 0 or 1
- labels: int32 [128], P(('dp', 'fsdp')), may hold values from 0 to 999
- dense_weights: float32 [384, 3840], P(None, ('dp', 'fsdp')), may hold values from -0.20412415 to 0.20412415
- attention: float32 [3, 384, 1536], P(None, None, ('dp', 'fsdp')), may hold values from -1.1547005 to 1.1547005
- router: float32 [2, 384, 128], P(None, 'dp', 'fsdp'), may hold values from -0.21875 to 0.21875
- expert_in: float32 [2, 128, 384, 1536], P(None, 'fsdp', None, 'dp'), may hold values from -4 to 4
- expert_out: float32 [2, 128, 1536, 384], P(None, 'fsdp', 'dp'), may hold values from -0.21875 to 0.21875
- classifier: float32 [385, 1000], replicated, may hold values from -0.3125 to 0.3125
- norm_table: float32 [210, 384], replicated, may hold values from -2 to 2
- dense_weights_first: float32 [384, 3840], P(None, ('dp', 'fsdp')), may hold values from -3.7252903e-08 to 3.7252903e-08
- dense_weights_second: float32 [384, 3840], P(None, ('dp', 'fsdp')), may hold values from 1.7200905e-16 to 6.8672815e-16
- attention_first: float32 [3, 384, 1536], P(None, None, ('dp', 'fsdp')), may hold values from -2.3841858e-07 to 2.3841858e-07
- attention_second: float32 [3, 384, 1536], P(None, None, ('dp', 'fsdp')), may hold values from 8.600452e-15 to 3.433641e-14
- router_first: float32 [2, 384, 128], P(None, 'dp', 'fsdp'), may hold values from -3.7252903e-08 to 3.7252903e-08
- router_second: float32 [2, 384, 128], P(None, 'dp', 'fsdp'), may hold values from 1.7200905e-16 to 6.8672815e-16
- expert_in_first: float32 [2, 128, 384, 1536], P(None, 'fsdp', None, 'dp'), may hold values from -1.6298145e-09 to 1.6298145e-09
- expert_in_second: float32 [2, 128, 384, 1536], P(None, 'fsdp', None, 'dp'), may hold values from 1.1870587e-18 to 4.741694e-18
- expert_out_first: float32 [2, 128, 1536, 384], P(None, 'fsdp', 'dp'), may hold values from -3.7252903e-08 to 3.7252903e-08
- expert_out_second: float32 [2, 128, 1536, 384], P(None, 'fsdp', 'dp'), may hold values from 1.7200905e-16 to 6.8672815e-16
- classifier_first: float32 [385, 1000], replicated, may hold values from -3.7252903e-08 to 3.7252903e-08
- classifier_second: float32 [385, 1000], replicated, may hold values from 1.7200905e-16 to 6.8672815e-16
- norm_table_first: float32 [210, 384], replicated, may hold values from -3.7252903e-08 to 3.7252903e-08
- norm_table_second: float32 [210, 384], replicated, may hold values from 1.7200905e-16 to 6.8672815e-16
Outputs:
- loss: float32 [], replicated
- grad_norm: float32 [], replicated
- new_dense_weights: float32 [384, 3840], P(None, ('dp', 'fsdp'))
- new_dense_weights_first: float32 [384, 3840], P(None, ('dp', 'fsdp'))
- new_dense_weights_second: float32 [384, 3840], P(None, ('dp', 'fsdp'))
- new_attention: float32 [3, 384, 1536], P(None, None, ('dp', 'fsdp'))
- new_attention_first: float32 [3, 384, 1536], P(None, None, ('dp', 'fsdp'))
- new_attention_second: float32 [3, 384, 1536], P(None, None, ('dp', 'fsdp'))
- new_router: float32 [2, 384, 128], P(None, 'dp', 'fsdp')
- new_router_first: float32 [2, 384, 128], P(None, 'dp', 'fsdp')
- new_router_second: float32 [2, 384, 128], P(None, 'dp', 'fsdp')
- new_expert_in: float32 [2, 128, 384, 1536], P(None, 'fsdp', None, 'dp')
- new_expert_in_first: float32 [2, 128, 384, 1536], P(None, 'fsdp', None, 'dp')
- new_expert_in_second: float32 [2, 128, 384, 1536], P(None, 'fsdp', None, 'dp')
- new_expert_out: float32 [2, 128, 1536, 384], P(None, 'fsdp', 'dp')
- new_expert_out_first: float32 [2, 128, 1536, 384], P(None, 'fsdp', 'dp')
- new_expert_out_second: float32 [2, 128, 1536, 384], P(None, 'fsdp', 'dp')
- new_classifier: float32 [385, 1000], replicated
- new_classifier_first: float32 [385, 1000], replicated
- new_classifier_second: float32 [385, 1000], replicated
- new_norm_table: float32 [210, 384], replicated
- new_norm_table_first: float32 [210, 384], replicated
- new_norm_table_second: float32 [210, 384], replicated
The draws below stay inside these ranges and needn't reach their ends.
All inputs are finite; a program needn't handle non-finite values. No bound on the sum of `resolution` on one device may be relied on, other than what follows from the above.
Results may differ from the reference program's by a relative error of at most 0.022.
Values may be sent and summed in bfloat16 or wider, within the bound.
A program may use at most 512 MiB of HBM per device.

```python
import math
import jax
import jax.numpy as jnp
from jax import lax

D = 384
HEADS = 6
FF = 1536
E = 128
C = 1000
PATCH = 768
G_LO = 14
G_HI = 24
LEN = 576
LEN_LO = 196
L = 2
STEP = 10
IMAGES = 128
NPARAMS = 305797864


def draw_dense_weights(key, part):
    shape = (D, PATCH + 2 * FF)
    noise = jax.random.truncated_normal(key, -4.0, 4.0, shape, jnp.float32)
    column = jnp.arange(PATCH + 2 * FF)[None, :]
    scale = jnp.where(column < PATCH, PATCH ** (-0.5), jnp.where(column < PATCH + FF, D ** (-0.5), (FF // 2) ** (-0.5)))
    return (noise * scale).astype(jnp.float32)


def draw_attention(key, part):
    shape = (L + 1, D, 4 * D)
    noise = jax.random.truncated_normal(key, -4.0, 4.0, shape, jnp.float32)
    column = jnp.arange(4 * D)[None, None, :]
    scale = jnp.where(column < 3 * D, D ** (-0.5), (D // 32) ** (-0.5))
    return (noise * scale).astype(jnp.float32)


def draw_norm_table(key, part):
    total_rows = LEN_LO + 4 * L + 6
    shape = (total_rows, D)
    noise = jax.random.truncated_normal(key, -4.0, 4.0, shape, jnp.float32)
    offset = jnp.arange(total_rows)[:, None] - LEN_LO
    is_gain = (offset >= 0) & (offset % 2 == 0)
    is_bias = (offset >= 0) & (offset % 2 == 1)
    return jnp.where(is_gain, 1.0 + 0.15 * noise, jnp.where(is_bias, 0.2 * noise, 0.5 * noise)).astype(jnp.float32)


def touch_ends(drawn, key, smallest, top_value):
    place = [jax.random.randint(jax.random.fold_in(key, axis), (), 0, length) for axis, length in enumerate(drawn.shape)]
    longest = drawn.shape.index(max(drawn.shape))
    next_to = place[:longest] + [(place[longest] + 1) % drawn.shape[longest]] + place[longest + 1:]
    return drawn.at[tuple(place)].set(smallest).at[tuple(next_to)].set(top_value)


def shard_levels(rng, shape, cuts, least, high):
    factor_of, own = 1.0, jax.random.fold_in(rng, 6)
    for dim, parts in cuts:
        draws = jnp.exp(jax.random.uniform(jax.random.fold_in(own, dim), (parts,), jnp.float32, least / len(cuts), high / len(cuts)))
        factor_of = factor_of * jnp.repeat(draws, shape[dim] // parts).reshape([-1 if axis == dim else 1 for axis in range(len(shape))])
    return factor_of


def centred(stream_key, shape, scale, reach, cuts=(), held_as=jnp.bfloat16):
    values = jax.random.normal(stream_key, shape, jnp.float32) * scale
    if len(cuts) > 0:
        values = shard_levels(stream_key, shape, cuts, -0.22, 0.18) * values
    return jnp.clip(values, min=-reach, max=reach).astype(held_as)


def setup_inputs(seed: int = 0) -> dict:
    streams_of = jax.random.split(jax.random.key(seed), 25)
    return {
        "patches": centred(streams_of[0], (IMAGES, LEN, PATCH), 1.0, 6.0, ((0, 32),)),
        "resolution": touch_ends((jax.random.randint(streams_of[1], (IMAGES,), 0, 6) < 1).astype(jnp.int32), jax.random.fold_in(streams_of[1], 1), 0, 1),
        "labels": touch_ends(jax.random.randint(streams_of[2], (IMAGES,), 0, C), jax.random.fold_in(streams_of[2], 1), 0, C - 1).astype(jnp.int32),
        "dense_weights": draw_dense_weights(jax.random.fold_in(streams_of[24], 71), 0),
        "attention": draw_attention(jax.random.fold_in(streams_of[24], 71), 0),
        "router": centred(streams_of[5], (L, D, E), (2 * D) ** -0.5, 0.21875, ((1, 2), (2, 16)), jnp.float32),
        "expert_in": centred(streams_of[6], (L, E, D, FF), 2 ** -0.5, 4.0, ((1, 16), (3, 2)), jnp.float32),
        "expert_out": centred(streams_of[7], (L, E, FF, D), (FF // 2) ** -0.5, 0.21875, ((1, 16), (2, 2)), jnp.float32),
        "classifier": centred(streams_of[8], (D + 1, C), D ** -0.5, 0.3125, (), jnp.float32),
        "norm_table": draw_norm_table(jax.random.fold_in(streams_of[24], 71), 0),
        "dense_weights_first": centred(streams_of[10], (D, PATCH + 2 * FF), (0.000111 * NPARAMS ** -0.5), 3.725290298461914e-08, ((1, 32),), jnp.float32),
        "dense_weights_second": jnp.clip(jnp.exp(math.log(6.867281503381614e-16) - 1.3843914 * jax.random.uniform(streams_of[11], (D, PATCH + 2 * FF), jnp.float32) ** shard_levels(streams_of[11], (D, PATCH + 2 * FF), ((1, 32),), -0.2, 0.2)), 1.720090452417397e-16, 6.867281503381614e-16),
        "attention_first": centred(streams_of[12], (L + 1, D, 4 * D), (0.00078 * NPARAMS ** -0.5), 2.384185791015625e-07, ((2, 32),), jnp.float32),
        "attention_second": jnp.clip(jnp.exp(math.log(3.4336408363941015e-14) - 1.38439146 * jax.random.uniform(streams_of[13], (L + 1, D, 4 * D), jnp.float32) ** shard_levels(streams_of[13], (L + 1, D, 4 * D), ((2, 32),), -0.2, 0.2)), 8.600452367966104e-15, 3.4336408363941015e-14),
        "router_first": centred(streams_of[14], (L, D, E), (0.000111 * NPARAMS ** -0.5), 3.725290298461914e-08, ((1, 2), (2, 16)), jnp.float32),
        "router_second": jnp.clip(jnp.exp(math.log(6.867281503381614e-16) - 1.3843914 * jax.random.uniform(streams_of[15], (L, D, E), jnp.float32) ** shard_levels(streams_of[15], (L, D, E), ((1, 2), (2, 16)), -0.2, 0.2)), 1.720090452417397e-16, 6.867281503381614e-16),
        "expert_in_first": centred(streams_of[16], (L, E, D, FF), (0.00000444 * NPARAMS ** -0.5), 1.6298145055770874e-09, ((1, 16), (3, 2)), jnp.float32),
        "expert_in_second": jnp.clip(jnp.exp(math.log(4.74169416104233e-18) - 1.384916 * jax.random.uniform(streams_of[17], (L, E, D, FF), jnp.float32) ** shard_levels(streams_of[17], (L, E, D, FF), ((1, 16), (3, 2)), -0.2, 0.2)), 1.1870586695364466e-18, 4.74169416104233e-18),
        "expert_out_first": centred(streams_of[18], (L, E, FF, D), (0.000111 * NPARAMS ** -0.5), 3.725290298461914e-08, ((1, 16), (2, 2)), jnp.float32),
        "expert_out_second": jnp.clip(jnp.exp(math.log(6.867281503381614e-16) - 1.3843914 * jax.random.uniform(streams_of[19], (L, E, FF, D), jnp.float32) ** shard_levels(streams_of[19], (L, E, FF, D), ((1, 16), (2, 2)), -0.2, 0.2)), 1.720090452417397e-16, 6.867281503381614e-16),
        "classifier_first": centred(streams_of[20], (D + 1, C), (0.000111 * NPARAMS ** -0.5), 3.725290298461914e-08, (), jnp.float32),
        "classifier_second": jnp.clip(jnp.exp(jax.random.uniform(streams_of[21], (D + 1, C), jnp.float32, math.log(1.720090452417397e-16), math.log(6.867281503381614e-16))), 1.720090452417397e-16, 6.867281503381614e-16),
        "norm_table_first": centred(streams_of[22], (LEN_LO + 4 * L + 6, D), (0.000111 * NPARAMS ** -0.5), 3.725290298461914e-08, (), jnp.float32),
        "norm_table_second": jnp.clip(jnp.exp(jax.random.uniform(streams_of[23], (LEN_LO + 4 * L + 6, D), jnp.float32, math.log(1.720090452417397e-16), math.log(6.867281503381614e-16))), 1.720090452417397e-16, 6.867281503381614e-16),
    }


LN_EPS = 1e-06
CLIP_NORM = 0.001
LEARN_RATE = 0.05
ATTENTION_RATE = 0.15
EXPERT_RATE = 1.0
TABLE_RATE = 0.5
BETA_ONE = 0.9
BETA_TWO = 0.95
ADAM_EPS = 1e-10
WEIGHT_DECAY = 0.1
SMOOTH = 0.1
NEG_FILL = -1e+30
PRECISE = lax.Precision.HIGHEST

@jax.custom_vjp
def low(v):
    return lax.optimization_barrier(v.astype(jnp.bfloat16)).astype(jnp.float32)

@jax.custom_vjp
def low_back(v):
    return v

def low_keep(v):
    return (low(v), None)

def low_pass(kept, grad):
    return (grad,)

def back_keep(v):
    return (v, None)

def back_low(kept, grad):
    return (low(grad),)
low.defvjp(low_keep, low_pass)
low_back.defvjp(back_keep, back_low)

def layer_norm(values, gain, bias):
    center = values - lax.optimization_barrier(jnp.mean(values, -1, keepdims=True))
    spread = lax.optimization_barrier(jnp.mean(center * center, -1, keepdims=True))
    return center * lax.rsqrt(spread + LN_EPS) * gain + bias

def interp_matrix():
    rows = jnp.arange(G_HI, dtype=jnp.float32)[:, None]
    cols = jnp.arange(G_LO, dtype=jnp.float32)[None, :]
    weight = jnp.maximum(0.0, 1.0 - jnp.abs(rows * (G_LO - 1) - cols * (G_HI - 1)) / (G_HI - 1))
    return (weight[:, None, :, None] * weight[None, :, None, :]).reshape(G_HI * G_HI, G_LO * G_LO)

def attend_ref(x_img, valid_img, wqkv, wout, gains):
    head_size = D // HEADS
    normed = low(layer_norm(x_img, gains[0], gains[1]))
    mixed = low(low_back(jnp.dot(normed, wqkv, precision=PRECISE)))
    query, keys, values = [part.reshape(LEN, HEADS, head_size) for part in jnp.split(mixed, 3, axis=1)]
    scores = low_back(jnp.einsum('qhd,khd->hqk', query, keys, precision=PRECISE) * head_size ** (-0.5))
    scores = jnp.where(valid_img[None, None, :] > 0, scores, NEG_FILL)
    probs = low(jax.nn.softmax(scores, axis=-1))
    context = low(low_back(jnp.einsum('hqk,khd->qhd', probs, values, precision=PRECISE).reshape(LEN, D)))
    return x_img + low_back(jnp.einsum('qd,ed->qe', context, wout, precision=PRECISE))

def mlp_ref(x_img, w_in, w_out, gains):
    normed = low(layer_norm(x_img, gains[2], gains[3]))
    pre = low_back(jnp.dot(normed, w_in, precision=PRECISE))
    hid = low(jax.nn.gelu(pre))
    return x_img + low_back(jnp.einsum('rf,ef->re', hid, w_out, precision=PRECISE))

def route_ref(x_img, valid_img, router_w, gains):
    normed = low(layer_norm(x_img, gains[2], gains[3]))
    logits = low_back(jnp.dot(normed, router_w, precision=PRECISE))
    dispatch = jax.nn.softmax(jnp.where(valid_img[:, None] > 0, logits, NEG_FILL), axis=0)
    combine = jax.nn.softmax(logits, axis=1)
    slots = low(low_back(jnp.dot(low(dispatch).T, normed, precision=PRECISE)))
    return (slots, combine)

def forward(dense_weights, attention, router, expert_in, expert_out, classifier, norm_table, patches, resolution, labels, valid):
    position = norm_table[:LEN_LO]
    pos_high = jnp.dot(interp_matrix(), position, precision=PRECISE)
    pos_low = jnp.pad(position, ((0, LEN - LEN_LO), (0, 0)))
    pos_image = jnp.where(resolution[:, None, None] == 1, pos_high[None], pos_low[None])
    first = low(dense_weights)
    embed_t = first[:, :PATCH]
    mlp_in = first[:, PATCH:PATCH + FF]
    mlp_out = first[:, PATCH + FF:]
    embedded = low_back(jnp.einsum('irp,dp->ird', patches, embed_t, precision=PRECISE))
    hidden = (embedded + pos_image) * valid[..., None]
    attend_block = jax.checkpoint(attend_ref)
    route_block = jax.checkpoint(route_ref)
    mlp_block = jax.checkpoint(mlp_ref)
    for layer in range(L + 1):
        gains = norm_table[LEN_LO + 4 * layer:LEN_LO + 4 * layer + 4]
        weights = low(attention[layer])
        wqkv = weights[:, :3 * D]
        wout = weights[:, 3 * D:]
        hidden = lax.map(lambda item: attend_block(item[0], item[1], wqkv, wout, gains), (hidden, valid))
        if layer == 0:
            hidden = lax.map(lambda item: mlp_block(item, mlp_in, mlp_out, gains), hidden)
        else:
            router_w = low(router[layer - 1])
            slots, combine = lax.map(lambda item: route_block(item[0], item[1], router_w, gains), (hidden, valid))
            pre = low_back(jnp.einsum('ied,edf->ief', slots, low(expert_in[layer - 1]), precision=PRECISE))
            hid = low(jax.nn.gelu(pre))
            returned = low(low_back(jnp.einsum('ief,efd->ied', hid, low(expert_out[layer - 1]), precision=PRECISE)))
            hidden = hidden + low_back(jnp.einsum('ire,ied->ird', low(combine), returned, precision=PRECISE))
    final = layer_norm(hidden, norm_table[LEN_LO + 4 * (L + 1)], norm_table[LEN_LO + 4 * (L + 1) + 1])
    pooled = lax.optimization_barrier(jnp.sum(final * valid[..., None], 1)) / lax.optimization_barrier(jnp.sum(valid, 1))[:, None]
    logits = low_back(jnp.dot(low(pooled), low(classifier[:D]), precision=PRECISE)) + classifier[D]
    log_probs = jax.nn.log_softmax(logits, axis=-1)
    picked = jnp.take_along_axis(log_probs, labels[:, None], 1)[:, 0]
    losses = -((1.0 - SMOOTH) * picked + SMOOTH * lax.optimization_barrier(jnp.mean(log_probs, -1)))
    return jnp.mean(losses)

def adam(weight, first, second, grad, rate):
    first = BETA_ONE * first + (1.0 - BETA_ONE) * grad
    second = BETA_TWO * second + (1.0 - BETA_TWO) * grad * grad
    ratio = first / (1.0 - BETA_ONE ** STEP) / (jnp.sqrt(second / (1.0 - BETA_TWO ** STEP)) + ADAM_EPS)
    return (weight - rate * (ratio + WEIGHT_DECAY * weight), first, second)

def reference(patches, resolution, labels, dense_weights, attention, router, expert_in, expert_out, classifier, norm_table, dense_weights_first, dense_weights_second, attention_first, attention_second, router_first, router_second, expert_in_first, expert_in_second, expert_out_first, expert_out_second, classifier_first, classifier_second, norm_table_first, norm_table_second):
    lengths = jnp.where(resolution == 1, LEN, LEN_LO)
    valid = (jnp.arange(LEN)[None, :] < lengths[:, None]).astype(jnp.float32)
    data = patches.astype(jnp.float32)
    weights = (dense_weights, attention, router, expert_in, expert_out, classifier, norm_table)
    loss, pull = jax.vjp(lambda *params: forward(*params, data, resolution, labels, valid), *weights)
    grads = pull(jnp.ones_like(loss))
    total = jnp.sum(jnp.stack([jnp.sum(grad * grad) for grad in grads]))
    norm = jnp.sqrt(total)
    scale = jnp.minimum(1.0, CLIP_NORM / norm)
    firsts = (dense_weights_first, attention_first, router_first, expert_in_first, expert_out_first, classifier_first, norm_table_first)
    seconds = (dense_weights_second, attention_second, router_second, expert_in_second, expert_out_second, classifier_second, norm_table_second)
    rates = (LEARN_RATE, ATTENTION_RATE, LEARN_RATE, EXPERT_RATE, LEARN_RATE, LEARN_RATE, TABLE_RATE)
    upd = [adam(weights[index], firsts[index], seconds[index], grads[index] * scale, rates[index]) for index in range(7)]
    return (loss, norm, upd[0][0], upd[0][1], upd[0][2], upd[1][0], upd[1][1], upd[1][2], upd[2][0], upd[2][1], upd[2][2], upd[3][0], upd[3][1], upd[3][2], upd[4][0], upd[4][1], upd[4][2], upd[5][0], upd[5][1], upd[5][2], upd[6][0], upd[6][1], upd[6][2])
```

```python
import functools

import jax
import jax.numpy as jnp
from jax import lax
from jax.experimental import pallas as pl
from jax.experimental.pallas import tpu as pltpu
from jax.sharding import PartitionSpec as P

HEADS = 6
FF = 1536
G_LO = 14
G_HI = 24
LEN = 576
LEN_LO = 196
ROWS_LO = 208
STEP = 10


LN_EPS = 1e-06
CLIP_NORM = 0.001
LEARN_RATE = 0.05
ATTENTION_RATE = 0.15
EXPERT_RATE = 1.0
TABLE_RATE = 0.5
BETA_ONE = 0.9
BETA_TWO = 0.95
ADAM_EPS = 1e-10
WEIGHT_DECAY = 0.1
SMOOTH = 0.1
NEG_FILL = -1e30
PRECISE = lax.Precision.HIGHEST
F32 = jnp.float32
BF16 = jnp.bfloat16
VMEM_BYTES = 60 * 1024 * 1024


def interp_matrix():
    rows = jnp.arange(G_HI, dtype=jnp.float32)[:, None]
    cols = jnp.arange(G_LO, dtype=jnp.float32)[None, :]
    weight = jnp.maximum(0.0, 1.0 - jnp.abs(rows * (G_LO - 1) - cols * (G_HI - 1)) / (G_HI - 1))
    return (weight[:, None, :, None] * weight[None, :, None, :]).reshape(G_HI * G_HI, G_LO * G_LO)


def matmul(left, right, form):
    return jnp.einsum(form, left, right, preferred_element_type=jnp.float32)


def contract(left, right, left_dim, right_dim):
    return lax.dot_general(
        left, right, (((left_dim,), (right_dim,)), ((), ())), preferred_element_type=F32
    )


def nn(left, right):
    return contract(left, right, 1, 0)


def nt(left, right):
    return contract(left, right, 1, 1)


def tn(left, right):
    return contract(left, right, 0, 0)


def normalise(values):
    center = values - jnp.mean(values, -1, keepdims=True)
    rate = lax.rsqrt(jnp.mean(center * center, -1, keepdims=True) + LN_EPS)
    return center * rate, rate


def normalise_back(unit, rate, gain, grad):
    scaled = grad * gain
    inner = scaled - jnp.mean(scaled, -1, keepdims=True)
    grad_in = rate * (inner - unit * jnp.mean(scaled * unit, -1, keepdims=True))
    return (
        grad_in,
        jnp.sum(grad * unit, 0, keepdims=True),
        jnp.sum(grad, 0, keepdims=True),
    )


def row_number(shape):
    return lax.broadcasted_iota(jnp.int32, shape, 0)


def side_masks():
    lane = lax.broadcasted_iota(jnp.int32, (1, 128), 1)
    first = (lane < 64).astype(F32)
    return (first.astype(BF16), (1.0 - first).astype(BF16))


def lanes(offset):
    return pl.ds(pl.multiple_of(offset, 128), 128)


GELU_RATE = 0.7978845608028654


def gelu(v):
    return 0.5 * v * (1.0 + jnp.tanh(GELU_RATE * (v + 0.044715 * (v * v * v))))


def gelu_both(v):
    square = v * v
    bend = jnp.tanh(GELU_RATE * (v + 0.044715 * (square * v)))
    half = 0.5 * (1.0 + bend)
    slope = half + 0.5 * v * (1.0 - bend * bend) * (GELU_RATE * (1.0 + 3 * 0.044715 * square))
    return v * half, slope


def attention_rows(rows, limit, qkv, context):
    width = context.shape[1]
    first = lax.broadcasted_iota(jnp.int32, (rows, 128), 1) < 64
    masks = side_masks()

    def pair(index, carry):
        offset = index * 128
        query = qkv[:rows, lanes(offset)] * BF16(0.125)
        keys = qkv[:rows, lanes(width + offset)]
        values = qkv[:rows, lanes(2 * width + offset)]
        found = []
        for side in (0, 1):
            scores = nt(query * masks[side], keys)
            if limit is not None:
                lane = lax.broadcasted_iota(jnp.int32, (rows, rows), 1)
                scores = jnp.where(lane < limit, scores, NEG_FILL)
            raised = jnp.exp(scores - jnp.max(scores, 1, keepdims=True))
            total = jnp.sum(raised, 1, keepdims=True)
            found.append(nn(raised.astype(BF16), values) * (1.0 / total))
        context[:rows, lanes(offset)] = jnp.where(first, found[0], found[1]).astype(BF16)
        return carry

    lax.fori_loop(0, width // 128, pair, 0)


def attention_rows_back(rows, limit, qkv, grad_context, grad_qkv):
    width = grad_context.shape[1]
    masks = side_masks()

    def pair(index, carry):
        offset = index * 128
        query = qkv[:rows, lanes(offset)] * BF16(0.125)
        keys = qkv[:rows, lanes(width + offset)]
        values = qkv[:rows, lanes(2 * width + offset)]
        grad = grad_context[:rows, lanes(offset)]
        grad_query = grad_keys = grad_values = None
        for side in (0, 1):
            query_side = query * masks[side]
            grad_side = grad * masks[side]
            scores = nt(keys, query_side)
            if limit is not None:
                scores = jnp.where(row_number((rows, rows)) < limit, scores, NEG_FILL)
            raised = jnp.exp(scores - jnp.max(scores, 0, keepdims=True))
            probs = raised * (1.0 / jnp.sum(raised, 0, keepdims=True))
            part_values = nn(probs.astype(BF16), grad_side)
            grad_probs = nt(values, grad_side)
            mixed = jnp.sum(probs * grad_probs, 0, keepdims=True)
            grad_scores = (probs * (grad_probs - mixed)).astype(BF16)
            part_keys = nn(grad_scores, query_side)
            part_query = tn(grad_scores, keys * masks[side])
            if side == 0:
                grad_query, grad_keys, grad_values = part_query, part_keys, part_values
            else:
                grad_query = grad_query + part_query
                grad_keys = grad_keys + part_keys
                grad_values = grad_values + part_values
        grad_qkv[:rows, lanes(offset)] = (grad_query * 0.125).astype(BF16)
        grad_qkv[:rows, lanes(width + offset)] = grad_keys.astype(BF16)
        grad_qkv[:rows, lanes(2 * width + offset)] = grad_values.astype(BF16)
        return carry

    lax.fori_loop(0, width // 128, pair, 0)


def attention_forward(rows, limit, hidden, gains, weights, qkv, context):
    width = hidden.shape[1]
    unit, _ = normalise(hidden)
    normed = (unit * gains[0:1] + gains[1:2]).astype(BF16)
    qkv[:rows] = nt(normed, weights[: 3 * width]).astype(BF16)
    attention_rows(rows, limit, qkv, context)
    return hidden + nn(context[:rows], weights[3 * width :])


def attention_backward(
    rows, limit, hidden, grad_middle, gains, weights, qkv, context, hold_context, hold_qkv,
    grad_weights, grad_gains,
):
    width = hidden.shape[1]
    grad_b = grad_middle.astype(BF16)
    hold_context[:rows] = nt(grad_b, weights[3 * width :]).astype(BF16)
    grad_weights[3 * width :] += tn(context[:rows], grad_b)
    attention_rows_back(rows, limit, qkv, hold_context, hold_qkv)
    unit, rate = normalise(hidden)
    normed = (unit * gains[0:1] + gains[1:2]).astype(BF16)
    grad_weights[: 3 * width] += tn(hold_qkv[:rows], normed)
    grad_normed = nn(hold_qkv[:rows], weights[: 3 * width])
    grad_in, grad_gain, grad_bias = normalise_back(unit, rate, gains[0:1], grad_normed)
    grad_gains[0:1] += grad_gain
    grad_gains[1:2] += grad_bias
    return grad_middle + grad_in


def mlp_forward(rows, middle, gains, weights, pixels):
    unit, _ = normalise(middle)
    normed = (unit * gains[2:3] + gains[3:4]).astype(BF16)
    chunk = middle.shape[1]
    total = middle
    for start in range(0, FF, chunk):
        pre = nt(normed, weights[pixels + start : pixels + start + chunk])
        out = weights[pixels + FF + start : pixels + FF + start + chunk]
        total = total + nn(gelu(pre).astype(BF16), out)
    return total


def mlp_backward(rows, middle, grad, gains, weights, pixels, grad_weights, grad_gains):
    unit, rate = normalise(middle)
    normed = (unit * gains[2:3] + gains[3:4]).astype(BF16)
    grad_b = grad.astype(BF16)
    chunk = middle.shape[1]
    grad_normed = None
    for start in range(0, FF, chunk):
        first = slice(pixels + start, pixels + start + chunk)
        second = slice(pixels + FF + start, pixels + FF + start + chunk)
        hid, slope = gelu_both(nt(normed, weights[first]))
        grad_weights[second] += tn(hid.astype(BF16), grad_b)
        grad_pre = (nt(grad_b, weights[second]) * slope).astype(BF16)
        grad_weights[first] += tn(grad_pre, normed)
        part = nn(grad_pre, weights[first])
        grad_normed = part if grad_normed is None else grad_normed + part
    grad_in, grad_gain, grad_bias = normalise_back(unit, rate, gains[2:3], grad_normed)
    grad_gains[2:3] += grad_gain
    grad_gains[3:4] += grad_bias
    return grad + grad_in


def route(limit, middle, gains, router):
    unit, rate = normalise(middle)
    normed = (unit * gains[2:3] + gains[3:4]).astype(BF16)
    logits = nt(normed, router[...])
    masked = logits
    if limit is not None:
        masked = jnp.where(row_number(logits.shape) < limit, logits, NEG_FILL)
    raised = jnp.exp(masked - jnp.max(masked, 0, keepdims=True))
    dispatch = raised * (1.0 / jnp.sum(raised, 0, keepdims=True))
    raised = jnp.exp(logits - jnp.max(logits, 1, keepdims=True))
    combine = raised * (1.0 / jnp.sum(raised, 1, keepdims=True))
    return unit, rate, normed, dispatch, combine


def masked_rows(limit, values):
    if limit is None:
        return values
    return jnp.where(row_number(values.shape) < limit, values, 0.0)


def by_image(name, body, scalars, per_image, whole, out_image, out_sum, scratch=()):
    images = scalars[0].shape[0]
    counts = (len(scalars), len(per_image), len(whole), len(out_image), len(out_sum), len(scratch))

    def kernel(*refs):
        groups, at = [], 0
        for count in counts:
            groups.append(refs[at : at + count])
            at += count
        index = pl.program_id(0)

        @pl.when(index == 0)
        def _():
            for ref in groups[4]:
                ref[...] = jnp.zeros_like(ref)

        numbers = [ref[index] for ref in groups[0]]

        @pl.when(numbers[0] == 1)
        def _():
            body(LEN, None, numbers, *groups[1:])

        @pl.when(numbers[0] != 1)
        def _():
            body(ROWS_LO, LEN_LO + numbers[0], numbers, *groups[1:])

    def image_spec(shape):
        return pl.BlockSpec((None,) + tuple(shape[1:]), lambda i, *_: (i, 0, 0))

    return pl.pallas_call(
        kernel,
        grid_spec=pltpu.PrefetchScalarGridSpec(
            num_scalar_prefetch=len(scalars),
            grid=(images,),
            in_specs=[image_spec(a.shape) for a in per_image]
            + [pl.BlockSpec(memory_space=pltpu.VMEM) for _ in whole],
            out_specs=[image_spec((images,) + shape) for shape, _ in out_image]
            + [pl.BlockSpec(shape, lambda i, *_: (0, 0)) for shape in out_sum],
            scratch_shapes=list(scratch),
        ),
        out_shape=[jax.ShapeDtypeStruct((images,) + shape, dtype) for shape, dtype in out_image]
        + [jax.ShapeDtypeStruct(shape, F32) for shape in out_sum],
        compiler_params=pltpu.CompilerParams(vmem_limit_bytes=VMEM_BYTES),
        name=name,
    )(*scalars, *per_image, *whole)


def first_forward(resolution, patches, dense, attention, positions, gains, width):
    pixels = patches.shape[2]

    def body(rows, limit, numbers, images, whole, outs, sums, scratch):
        dense_ref, attention_ref, position_ref, gain_ref = whole
        start, qkv, context, middle, last = outs
        place = position_ref[0 if limit is not None else 1, :rows]
        embedded = masked_rows(limit, nn(images[0][:rows], dense_ref[:pixels]) + place)
        start[:rows] = embedded
        middle_rows = attention_forward(
            rows, limit, embedded, gain_ref, attention_ref, qkv, context
        )
        middle[:rows] = middle_rows
        last[:rows] = mlp_forward(rows, middle_rows, gain_ref, dense_ref, pixels)

    return by_image(
        "first_forward",
        body,
        [resolution],
        [patches],
        [dense, attention, positions, gains],
        [
            ((LEN, width), F32),
            ((LEN, 3 * width), BF16),
            ((LEN, width), BF16),
            ((LEN, width), F32),
            ((LEN, width), F32),
        ],
        [],
    )


def sparse_forward(resolution, hidden, mixing, attention, router, gains):
    width = hidden.shape[2]
    experts = router.shape[0]

    def body(rows, limit, numbers, images, whole, outs, sums, scratch):
        attention_ref, router_ref, gain_ref = whole
        before, qkv, context, middle, combine, slots = ([None] + list(outs))[-6:]
        hidden_rows = images[0][:rows]
        if mixing is not None:
            hidden_rows = hidden_rows + nn(images[1][:rows], images[2][...])
            before[:rows] = hidden_rows
        middle_rows = attention_forward(
            rows, limit, hidden_rows, gain_ref, attention_ref, qkv, context
        )
        middle[:rows] = middle_rows
        _, _, normed, dispatch, share = route(limit, middle_rows, gain_ref, router_ref)
        combine[:rows] = share.astype(BF16)
        slots[...] = tn(dispatch.astype(BF16), normed).astype(BF16)

    outs = [
        ((LEN, 3 * width), BF16),
        ((LEN, width), BF16),
        ((LEN, width), F32),
        ((LEN, experts), BF16),
        ((experts, width), BF16),
    ]
    if mixing is not None:
        outs = [((LEN, width), F32)] + outs
    return by_image(
        "sparse_forward",
        body,
        [resolution],
        [hidden] + list(mixing or ()),
        [attention, router, gains],
        outs,
        [],
    )


def top(resolution, labels, middle, combine, returned, head, head_bias, last_gains, classes, images):
    width = middle.shape[2]
    experts = returned.shape[1]
    padded = head.shape[1]

    def body(rows, limit, numbers, per_image, whole, outs, sums, scratch):
        middle_ref, combine_ref, returned_ref = per_image
        head_ref, bias_ref, gain_ref = whole
        grad_hidden, grad_returned = outs
        grad_head, grad_bias_row, grad_gains, loss = sums
        length = float(LEN if limit is None else LEN_LO)
        share = combine_ref[:rows]
        hidden = middle_ref[:rows] + nn(share, returned_ref[...])
        unit, rate = normalise(hidden)
        normed = masked_rows(limit, unit * gain_ref[0:1] + gain_ref[1:2])
        pooled = jnp.sum(normed, 0, keepdims=True) * (1.0 / length)
        one_row = (row_number((8, width)) == 0).astype(F32)
        pooled_b = (one_row * pooled).astype(BF16)
        logits = nn(pooled_b, head_ref[...])[0:1] + bias_ref[...]
        shifted = logits - jnp.max(logits, 1, keepdims=True)
        raised = jnp.exp(shifted)
        total = jnp.sum(raised, 1, keepdims=True)
        log_probs = shifted - jnp.log(total)
        lane = lax.broadcasted_iota(jnp.int32, (1, padded), 1)
        target = jnp.where(lane == numbers[1], 1.0 - SMOOTH, 0.0) + jnp.where(
            lane < classes, SMOOTH / classes, 0.0
        )
        picked = jnp.sum(target * log_probs, 1, keepdims=True)
        loss[...] += jnp.broadcast_to(picked * (-1.0 / images), loss.shape)
        grad_logits = (raised * (1.0 / total) - target) * (1.0 / images)
        grad_bias_row[0:1] += grad_logits
        row_mask = (row_number((8, padded)) == 0).astype(F32)
        grad_logits_b = (row_mask * grad_logits).astype(BF16)
        grad_head[...] += tn(pooled_b, grad_logits_b)
        grad_pooled = nt(grad_logits_b, head_ref[...])[0:1] * (1.0 / length)
        grad_normed = masked_rows(limit, jnp.broadcast_to(grad_pooled, (rows, width)))
        grad_rows, grad_gain, grad_bias = normalise_back(
            unit, rate, gain_ref[0:1], grad_normed
        )
        grad_gains[0:1] += grad_gain
        grad_gains[1:2] += grad_bias
        grad_hidden[:rows] = grad_rows
        grad_returned[...] = tn(share, grad_rows.astype(BF16)).astype(BF16)

    return by_image(
        "top",
        body,
        [resolution, labels],
        [middle, combine, returned],
        [head, head_bias, last_gains],
        [((LEN, width), F32), ((experts, width), BF16)],
        [(width, padded), (8, padded), (8, width), (8, 128)],
    )


def sparse_backward(
    resolution, hidden, qkv, context, middle, grad_hidden, returned, grad_home, below, attention,
    router, gains,
):
    width = middle.shape[2]
    experts = router.shape[0]

    def body(rows, limit, numbers, images, whole, outs, sums, scratch):
        hidden_ref, qkv_ref, context_ref, middle_ref, grad_ref, returned_ref, home_ref = images[:7]
        attention_ref, router_ref, gain_ref = whole
        grad_attention, grad_router, grad_gains = sums
        grad = grad_ref[:rows]
        grad_combine = nt(grad.astype(BF16), returned_ref[...])
        unit, rate, normed, dispatch, share = route(
            limit, middle_ref[:rows], gain_ref, router_ref
        )
        home = home_ref[...]
        grad_dispatch = nt(normed, home)
        grad_normed = nn(dispatch.astype(BF16), home)
        grad_route = dispatch * (
            grad_dispatch - jnp.sum(grad_dispatch * dispatch, 0, keepdims=True)
        ) + share * (grad_combine - jnp.sum(grad_combine * share, 1, keepdims=True))
        grad_route_b = grad_route.astype(BF16)
        grad_router[...] += tn(grad_route_b, normed)
        grad_normed = grad_normed + nn(grad_route_b, router_ref[...])
        grad_in, grad_gain, grad_bias = normalise_back(unit, rate, gain_ref[2:3], grad_normed)
        grad_gains[2:3] += grad_gain
        grad_gains[3:4] += grad_bias
        grad_rows = attention_backward(
            rows, limit, hidden_ref[:rows], grad + grad_in, gain_ref, attention_ref, qkv_ref,
            context_ref, scratch[0], scratch[1], grad_attention, grad_gains,
        )
        outs[0][:rows] = grad_rows
        if below is not None:
            outs[1][...] = tn(images[7][:rows], grad_rows.astype(BF16)).astype(BF16)

    outs = [((LEN, width), F32)]
    if below is not None:
        outs.append(((experts, width), BF16))
    return by_image(
        "sparse_backward",
        body,
        [resolution],
        [hidden, qkv, context, middle, grad_hidden, returned, grad_home]
        + ([] if below is None else [below]),
        [attention, router, gains],
        outs,
        [(4 * width, width), (experts, width), (8, width)],
        [pltpu.VMEM((LEN, width), BF16), pltpu.VMEM((LEN, 3 * width), BF16)],
    )


def first_backward(resolution, patches, start, qkv, context, middle, grad_hidden, dense, attention, gains):
    width = middle.shape[2]
    pixels = patches.shape[2]

    def body(rows, limit, numbers, images, whole, outs, sums, scratch):
        patches_ref, start_ref, qkv_ref, context_ref, middle_ref, grad_ref = images
        dense_ref, attention_ref, gain_ref = whole
        grad_dense, grad_attention, grad_gains, grad_low, grad_high = sums
        grad_middle = mlp_backward(
            rows, middle_ref[:rows], grad_ref[:rows], gain_ref, dense_ref, pixels, grad_dense,
            grad_gains,
        )
        grad_rows = attention_backward(
            rows, limit, start_ref[:rows], grad_middle, gain_ref, attention_ref, qkv_ref,
            context_ref, scratch[0], scratch[1], grad_attention, grad_gains,
        )
        grad_rows = masked_rows(limit, grad_rows)
        grad_dense[:pixels] += tn(patches_ref[:rows], grad_rows.astype(BF16))
        if limit is None:
            grad_high[...] += grad_rows
        else:
            grad_low[...] += grad_rows

    return by_image(
        "first_backward",
        body,
        [resolution],
        [patches, start, qkv, context, middle, grad_hidden],
        [dense, attention, gains],
        [],
        [(dense.shape[0], width), (4 * width, width), (8, width), (ROWS_LO, width), (LEN, width)],
        [pltpu.VMEM((LEN, width), BF16), pltpu.VMEM((LEN, 3 * width), BF16)],
    )


def to_experts(values):
    return lax.all_to_all(values, "fsdp", split_axis=1, concat_axis=0, tiled=True)


def from_experts(values):
    return lax.all_to_all(values, "fsdp", split_axis=0, concat_axis=1, tiled=True)


def sum_rows(partial_value):
    return lax.psum_scatter(partial_value, "dp", scatter_dimension=0, tiled=True)


def expert_forward(received, win, wout):
    pre = matmul(received, win, "ned,edf->nef")
    hidden = jax.nn.gelu(pre).astype(jnp.bfloat16)
    return matmul(hidden, wout, "nef,efd->ned")


def expert_backward(received, grad_out, win, wout):
    pre = matmul(received, win, "ned,edf->nef")
    hidden = jax.nn.gelu(pre).astype(jnp.bfloat16)
    grad_hidden = matmul(grad_out, wout, "ned,efd->nef")
    _, pull = jax.vjp(jax.nn.gelu, pre)
    grad_pre = pull(grad_hidden)[0].astype(jnp.bfloat16)
    grad_wout = matmul(hidden, grad_out, "nef,ned->efd")
    grad_win = matmul(received, grad_pre, "ned,nef->edf")
    grad_slots = matmul(grad_pre, win, "nef,edf->ned")
    return (grad_slots, grad_win, grad_wout)


def fetch_layer(attention_t, router_t):
    part, width = attention_t.shape
    part_cols, part_rows = router_t.shape
    flat = router_t.reshape(-1)
    pack = jnp.concatenate(
        [attention_t, jnp.pad(flat, (0, -flat.size % width)).reshape(-1, width)], 0
    )
    both = lax.all_gather(pack, ("dp", "fsdp"), axis=0)
    rows_dp = lax.axis_size("dp")
    cols_fsdp = lax.axis_size("fsdp")
    router = (
        both[:, part:]
        .reshape(rows_dp * cols_fsdp, -1)[:, : flat.size]
        .reshape(rows_dp, cols_fsdp, part_cols, part_rows)
        .transpose(1, 2, 0, 3)
        .reshape(cols_fsdp * part_cols, rows_dp * part_rows)
    )
    return both[:, :part].reshape(-1, width), router


def share_layer(grad_attention, grad_router, part_cols, part_rows):
    rows_dp = lax.axis_size("dp")
    cols_fsdp = lax.axis_size("fsdp")
    devices = rows_dp * cols_fsdp
    width = grad_attention.shape[1]
    router = (
        grad_router.reshape(cols_fsdp, part_cols, rows_dp, part_rows)
        .transpose(2, 0, 1, 3)
        .reshape(devices, -1)
    )
    router = jnp.pad(router, ((0, 0), (0, -part_cols * part_rows % width)))
    router = router.reshape(devices, -1, width)
    pack = jnp.concatenate([grad_attention.reshape(devices, -1, width), router], 1)
    mine = lax.psum_scatter(pack, ("dp", "fsdp"), scatter_dimension=0, tiled=False)
    part = grad_attention.shape[0] // devices
    return mine[:part], mine[part:].reshape(-1)[: part_cols * part_rows].reshape(part_cols, part_rows)


def adam(weight, first, second, grad, rate):
    first = BETA_ONE * first + (1.0 - BETA_ONE) * grad
    second = BETA_TWO * second + (1.0 - BETA_TWO) * grad * grad
    ratio = first / (1.0 - BETA_ONE**STEP) / (jnp.sqrt(second / (1.0 - BETA_TWO**STEP)) + ADAM_EPS)
    return (weight - rate * (ratio + WEIGHT_DECAY * weight), first, second)


def on_device(
    patches,
    resolution,
    labels,
    dense_weights,
    attention,
    router,
    expert_in,
    expert_out,
    classifier,
    norm_table,
    dense_weights_first,
    dense_weights_second,
    attention_first,
    attention_second,
    router_first,
    router_second,
    expert_in_first,
    expert_in_second,
    expert_out_first,
    expert_out_second,
    classifier_first,
    classifier_second,
    norm_table_first,
    norm_table_second,
):
    layers = attention.shape[0]
    width = norm_table.shape[1]
    classes = classifier.shape[1]
    devices = lax.axis_size("dp") * lax.axis_size("fsdp")
    images = patches.shape[0] * devices
    interp = interp_matrix()
    position = norm_table[:LEN_LO]
    pos_high = jnp.dot(interp, position, precision=PRECISE)
    pos_low = jnp.pad(position, ((0, LEN - LEN_LO), (0, 0)))
    positions = jnp.stack([pos_low, pos_high])
    gains = [
        jnp.pad(norm_table[LEN_LO + 4 * layer : LEN_LO + 4 * layer + 4], ((0, 4), (0, 0)))
        for layer in range(layers)
    ]
    last_gains = jnp.pad(norm_table[LEN_LO + 4 * layers :], ((0, 6), (0, 0)))
    attention_t = attention.transpose(0, 2, 1).astype(BF16)
    router_t = router.transpose(0, 2, 1).astype(BF16)
    dense = lax.all_gather(dense_weights.T.astype(BF16), ("dp", "fsdp"), axis=0, tiled=True)
    attention_all = [
        lax.all_gather(attention_t[0], ("dp", "fsdp"), axis=0, tiled=True)
    ]
    router_all = [None]
    for layer in range(1, layers):
        one, two = fetch_layer(attention_t[layer], router_t[layer - 1])
        attention_all.append(one)
        router_all.append(two)

    start, qkv, context, middle, hidden = first_forward(
        resolution, patches, dense, attention_all[0], positions, gains[0], width
    )
    kept = [(start, qkv, context, middle)]
    mixing = None
    for layer in range(1, layers):
        outs = sparse_forward(
            resolution, hidden, mixing, attention_all[layer], router_all[layer], gains[layer]
        )
        if mixing is not None:
            hidden = outs[0]
        qkv, context, middle, combine, slots = outs[-5:]
        received = to_experts(slots)
        rows_all = lax.all_gather(received, "dp", axis=0, tiled=True)
        produced = sum_rows(
            expert_forward(
                rows_all, expert_in[layer - 1].astype(BF16), expert_out[layer - 1].astype(BF16)
            )
        ).astype(BF16)
        returned = from_experts(produced)
        kept.append((hidden, qkv, context, middle, combine, returned, received))
        hidden = middle
        mixing = (combine, returned)

    padding = -classes % 128
    head = jnp.pad(classifier[:width].astype(BF16), ((0, 0), (0, padding)))
    head_bias = jnp.pad(classifier[width:], ((0, 0), (0, padding)), constant_values=NEG_FILL)
    grad_hidden, grad_returned, grad_head, grad_bias, grad_last, loss_part = top(
        resolution, labels, middle, combine, returned, head, head_bias, last_gains, classes, images
    )
    grad_head = jnp.concatenate([grad_head[:, :classes], grad_bias[0:1, :classes]], 0)
    attention_grads = [None] * layers
    router_grads = [None] * (layers - 1)
    win_grads = [None] * (layers - 1)
    wout_grads = [None] * (layers - 1)
    gain_grads = [None] * layers
    for layer in reversed(range(1, layers)):
        before, qkv, context, middle, combine, returned, received = kept[layer]
        grad_received = to_experts(grad_returned)
        rows_all = lax.all_gather(received, "dp", axis=0, tiled=True)
        grads_all = lax.all_gather(grad_received, "dp", axis=0, tiled=True)
        grad_part, grad_win, grad_wout = expert_backward(
            rows_all, grads_all, expert_in[layer - 1].astype(BF16), expert_out[layer - 1].astype(BF16)
        )
        grad_home = from_experts(sum_rows(grad_part).astype(BF16))
        below = kept[layer - 1][4] if layer > 1 else None
        outs = sparse_backward(
            resolution, before, qkv, context, middle, grad_hidden, returned, grad_home, below,
            attention_all[layer], router_all[layer], gains[layer],
        )
        grad_hidden = outs[0]
        if below is not None:
            grad_returned = outs[1]
        grad_attention, grad_router, grad_gain = outs[-3:]
        attention_grads[layer], router_grads[layer - 1] = share_layer(
            grad_attention, grad_router, router.shape[2], router.shape[1]
        )
        win_grads[layer - 1] = grad_win
        wout_grads[layer - 1] = grad_wout
        gain_grads[layer] = grad_gain[:4]
    start, qkv, context, middle = kept[0]
    grad_dense, grad_attention, grad_gain, grad_low, grad_high = first_backward(
        resolution, patches, start, qkv, context, middle, grad_hidden, dense, attention_all[0],
        gains[0],
    )
    gain_grads[0] = grad_gain[:4]
    grad_first = lax.psum_scatter(grad_dense, ("dp", "fsdp"), scatter_dimension=0, tiled=True).T
    attention_grads[0] = lax.psum_scatter(
        grad_attention, ("dp", "fsdp"), scatter_dimension=0, tiled=True
    )
    grad_pos = grad_low[:LEN_LO] + jnp.dot(interp.T, grad_high, precision=PRECISE)
    grad_table = jnp.concatenate([grad_pos] + gain_grads + [grad_last[:2]], 0)
    grad_attention = jnp.stack(attention_grads).transpose(0, 2, 1)
    grad_router_all = jnp.stack(router_grads).transpose(0, 2, 1)
    grad_expert_in = jnp.stack(win_grads)
    grad_expert_out = jnp.stack(wout_grads)
    local_squares = (
        jnp.sum(grad_first * grad_first)
        + jnp.sum(grad_attention * grad_attention)
        + jnp.sum(grad_router_all * grad_router_all)
        + jnp.sum(grad_expert_in * grad_expert_in)
        + jnp.sum(grad_expert_out * grad_expert_out)
    )
    shared_head, shared_table, loss_total, squares = lax.psum(
        (grad_head, grad_table, loss_part[0, 0], local_squares), ("dp", "fsdp")
    )
    norm = jnp.sqrt(
        squares + jnp.sum(shared_head * shared_head) + jnp.sum(shared_table * shared_table)
    )
    scale = jnp.minimum(1.0, CLIP_NORM / norm)
    updates = (
        adam(dense_weights, dense_weights_first, dense_weights_second, grad_first * scale, LEARN_RATE),
        adam(attention, attention_first, attention_second, grad_attention * scale, ATTENTION_RATE),
        adam(router, router_first, router_second, grad_router_all * scale, LEARN_RATE),
        adam(expert_in, expert_in_first, expert_in_second, grad_expert_in * scale, EXPERT_RATE),
        adam(expert_out, expert_out_first, expert_out_second, grad_expert_out * scale, LEARN_RATE),
        adam(classifier, classifier_first, classifier_second, shared_head * scale, LEARN_RATE),
        adam(norm_table, norm_table_first, norm_table_second, shared_table * scale, TABLE_RATE),
    )
    return (loss_total, norm) + tuple(part for update in updates for part in update)


def solution(mesh):
    spread = P(("dp", "fsdp"))
    weights = (
        P(None, ("dp", "fsdp")),
        P(None, None, ("dp", "fsdp")),
        P(None, "dp", "fsdp"),
        P(None, "fsdp", None, "dp"),
        P(None, "fsdp", "dp", None),
        P(),
        P(),
    )
    moments = tuple(spec for spec in weights for _ in range(2))
    triples = tuple(spec for spec in weights for _ in range(3))
    return jax.shard_map(
        on_device,
        mesh=mesh,
        in_specs=(spread, spread, spread) + weights + moments,
        out_specs=(P(), P()) + triples,
        check_vma=False,
    )
```

```python
import functools

import jax
import jax.numpy as jnp
from jax import lax
from jax.experimental import pallas as pl
from jax.experimental.pallas import tpu as pltpu
from jax.sharding import PartitionSpec as P

HEADS = 6
FF = 1536
G_LO = 14
G_HI = 24
LEN = 576
LEN_LO = 196
ROWS_LO = 208
STEP = 10


LN_EPS = 1e-06
CLIP_NORM = 0.001
LEARN_RATE = 0.05
ATTENTION_RATE = 0.15
EXPERT_RATE = 1.0
TABLE_RATE = 0.5
BETA_ONE = 0.9
BETA_TWO = 0.95
ADAM_EPS = 1e-10
WEIGHT_DECAY = 0.1
SMOOTH = 0.1
NEG_FILL = -1e30
PRECISE = lax.Precision.HIGHEST
F32 = jnp.float32
BF16 = jnp.bfloat16
VMEM_BYTES = 60 * 1024 * 1024


def interp_matrix():
    rows = jnp.arange(G_HI, dtype=jnp.float32)[:, None]
    cols = jnp.arange(G_LO, dtype=jnp.float32)[None, :]
    weight = jnp.maximum(0.0, 1.0 - jnp.abs(rows * (G_LO - 1) - cols * (G_HI - 1)) / (G_HI - 1))
    return (weight[:, None, :, None] * weight[None, :, None, :]).reshape(G_HI * G_HI, G_LO * G_LO)


def matmul(left, right, form):
    return jnp.einsum(form, left, right, preferred_element_type=jnp.float32)


def contract(left, right, left_dim, right_dim):
    return lax.dot_general(
        left, right, (((left_dim,), (right_dim,)), ((), ())), preferred_element_type=F32
    )


def nn(left, right):
    return contract(left, right, 1, 0)


def nt(left, right):
    return contract(left, right, 1, 1)


def tn(left, right):
    return contract(left, right, 0, 0)


def normalise(values):
    center = values - jnp.mean(values, -1, keepdims=True)
    rate = lax.rsqrt(jnp.mean(center * center, -1, keepdims=True) + LN_EPS)
    return center * rate, rate


def normalise_back(unit, rate, gain, grad):
    scaled = grad * gain
    inner = scaled - jnp.mean(scaled, -1, keepdims=True)
    grad_in = rate * (inner - unit * jnp.mean(scaled * unit, -1, keepdims=True))
    return (
        grad_in,
        jnp.sum(grad * unit, 0, keepdims=True),
        jnp.sum(grad, 0, keepdims=True),
    )


def row_number(shape):
    return lax.broadcasted_iota(jnp.int32, shape, 0)


def side_masks():
    lane = lax.broadcasted_iota(jnp.int32, (1, 128), 1)
    first = (lane < 64).astype(F32)
    return (first.astype(BF16), (1.0 - first).astype(BF16))


def lanes(offset):
    return pl.ds(pl.multiple_of(offset, 128), 128)


GELU_RATE = 0.7978845608028654


def gelu(v):
    return 0.5 * v * (1.0 + jnp.tanh(GELU_RATE * (v + 0.044715 * (v * v * v))))


def gelu_both(v):
    square = v * v
    bend = jnp.tanh(GELU_RATE * (v + 0.044715 * (square * v)))
    half = 0.5 * (1.0 + bend)
    slope = half + 0.5 * v * (1.0 - bend * bend) * (GELU_RATE * (1.0 + 3 * 0.044715 * square))
    return v * half, slope


def attention_rows(rows, limit, qkv, context):
    width = context.shape[1]
    first = lax.broadcasted_iota(jnp.int32, (rows, 128), 1) < 64
    masks = side_masks()

    def pair(index, carry):
        offset = index * 128
        query = qkv[:rows, lanes(offset)] * BF16(0.125)
        keys = qkv[:rows, lanes(width + offset)]
        values = qkv[:rows, lanes(2 * width + offset)]
        found = []
        for side in (0, 1):
            scores = nt(query * masks[side], keys)
            if limit is not None:
                lane = lax.broadcasted_iota(jnp.int32, (rows, rows), 1)
                scores = jnp.where(lane < limit, scores, NEG_FILL)
            raised = jnp.exp(scores - jnp.max(scores, 1, keepdims=True))
            total = jnp.sum(raised, 1, keepdims=True)
            found.append(nn(raised.astype(BF16), values) * (1.0 / total))
        context[:rows, lanes(offset)] = jnp.where(first, found[0], found[1]).astype(BF16)
        return carry

    lax.fori_loop(0, width // 128, pair, 0)


def attention_rows_back(rows, limit, qkv, grad_context, grad_qkv):
    width = grad_context.shape[1]
    masks = side_masks()

    def pair(index, carry):
        offset = index * 128
        query = qkv[:rows, lanes(offset)] * BF16(0.125)
        keys = qkv[:rows, lanes(width + offset)]
        values = qkv[:rows, lanes(2 * width + offset)]
        grad = grad_context[:rows, lanes(offset)]
        grad_query = grad_keys = grad_values = None
        for side in (0, 1):
            query_side = query * masks[side]
            grad_side = grad * masks[side]
            scores = nt(keys, query_side)
            if limit is not None:
                scores = jnp.where(row_number((rows, rows)) < limit, scores, NEG_FILL)
            raised = jnp.exp(scores - jnp.max(scores, 0, keepdims=True))
            probs = raised * (1.0 / jnp.sum(raised, 0, keepdims=True))
            part_values = nn(probs.astype(BF16), grad_side)
            grad_probs = nt(values, grad_side)
            mixed = jnp.sum(probs * grad_probs, 0, keepdims=True)
            grad_scores = (probs * (grad_probs - mixed)).astype(BF16)
            part_keys = nn(grad_scores, query_side)
            part_query = tn(grad_scores, keys * masks[side])
            if side == 0:
                grad_query, grad_keys, grad_values = part_query, part_keys, part_values
            else:
                grad_query = grad_query + part_query
                grad_keys = grad_keys + part_keys
                grad_values = grad_values + part_values
        grad_qkv[:rows, lanes(offset)] = (grad_query * 0.125).astype(BF16)
        grad_qkv[:rows, lanes(width + offset)] = grad_keys.astype(BF16)
        grad_qkv[:rows, lanes(2 * width + offset)] = grad_values.astype(BF16)
        return carry

    lax.fori_loop(0, width // 128, pair, 0)


def attention_forward(rows, limit, hidden, gains, weights, qkv, context):
    width = hidden.shape[1]
    unit, _ = normalise(hidden)
    normed = (unit * gains[0:1] + gains[1:2]).astype(BF16)
    qkv[:rows] = nt(normed, weights[: 3 * width]).astype(BF16)
    attention_rows(rows, limit, qkv, context)
    return hidden + nn(context[:rows], weights[3 * width :])


def attention_backward(
    rows, limit, hidden, grad_middle, gains, weights, qkv, context, hold_context, hold_qkv,
    grad_weights, grad_gains,
):
    width = hidden.shape[1]
    grad_b = grad_middle.astype(BF16)
    hold_context[:rows] = nt(grad_b, weights[3 * width :]).astype(BF16)
    grad_weights[3 * width :] += tn(context[:rows], grad_b)
    attention_rows_back(rows, limit, qkv, hold_context, hold_qkv)
    unit, rate = normalise(hidden)
    normed = (unit * gains[0:1] + gains[1:2]).astype(BF16)
    grad_weights[: 3 * width] += tn(hold_qkv[:rows], normed)
    grad_normed = nn(hold_qkv[:rows], weights[: 3 * width])
    grad_in, grad_gain, grad_bias = normalise_back(unit, rate, gains[0:1], grad_normed)
    grad_gains[0:1] += grad_gain
    grad_gains[1:2] += grad_bias
    return grad_middle + grad_in


def mlp_forward(rows, middle, gains, weights, pixels):
    unit, _ = normalise(middle)
    normed = (unit * gains[2:3] + gains[3:4]).astype(BF16)
    chunk = middle.shape[1]
    total = middle
    for start in range(0, FF, chunk):
        pre = nt(normed, weights[pixels + start : pixels + start + chunk])
        out = weights[pixels + FF + start : pixels + FF + start + chunk]
        total = total + nn(gelu(pre).astype(BF16), out)
    return total


def mlp_backward(rows, middle, grad, gains, weights, pixels, grad_weights, grad_gains):
    unit, rate = normalise(middle)
    normed = (unit * gains[2:3] + gains[3:4]).astype(BF16)
    grad_b = grad.astype(BF16)
    chunk = middle.shape[1]
    grad_normed = None
    for start in range(0, FF, chunk):
        first = slice(pixels + start, pixels + start + chunk)
        second = slice(pixels + FF + start, pixels + FF + start + chunk)
        hid, slope = gelu_both(nt(normed, weights[first]))
        grad_weights[second] += tn(hid.astype(BF16), grad_b)
        grad_pre = (nt(grad_b, weights[second]) * slope).astype(BF16)
        grad_weights[first] += tn(grad_pre, normed)
        part = nn(grad_pre, weights[first])
        grad_normed = part if grad_normed is None else grad_normed + part
    grad_in, grad_gain, grad_bias = normalise_back(unit, rate, gains[2:3], grad_normed)
    grad_gains[2:3] += grad_gain
    grad_gains[3:4] += grad_bias
    return grad + grad_in


def route(limit, middle, gains, router):
    unit, rate = normalise(middle)
    normed = (unit * gains[2:3] + gains[3:4]).astype(BF16)
    logits = nt(normed, router[...])
    masked = logits
    if limit is not None:
        masked = jnp.where(row_number(logits.shape) < limit, logits, NEG_FILL)
    raised = jnp.exp(masked - jnp.max(masked, 0, keepdims=True))
    dispatch = raised * (1.0 / jnp.sum(raised, 0, keepdims=True))
    raised = jnp.exp(logits - jnp.max(logits, 1, keepdims=True))
    combine = raised * (1.0 / jnp.sum(raised, 1, keepdims=True))
    return unit, rate, normed, dispatch, combine


def masked_rows(limit, values):
    if limit is None:
        return values
    return jnp.where(row_number(values.shape) < limit, values, 0.0)


def by_image(name, body, scalars, per_image, whole, out_image, out_sum, scratch=()):
    images = scalars[0].shape[0]
    counts = (len(scalars), len(per_image), len(whole), len(out_image), len(out_sum), len(scratch))

    def kernel(*refs):
        groups, at = [], 0
        for count in counts:
            groups.append(refs[at : at + count])
            at += count
        index = pl.program_id(0)

        @pl.when(index == 0)
        def _():
            for ref in groups[4]:
                ref[...] = jnp.zeros_like(ref)

        numbers = [ref[index] for ref in groups[0]]

        @pl.when(numbers[0] == 1)
        def _():
            body(LEN, None, numbers, *groups[1:])

        @pl.when(numbers[0] != 1)
        def _():
            body(ROWS_LO, LEN_LO + numbers[0], numbers, *groups[1:])

    def image_spec(shape):
        return pl.BlockSpec((None,) + tuple(shape[1:]), lambda i, *_: (i, 0, 0))

    return pl.pallas_call(
        kernel,
        grid_spec=pltpu.PrefetchScalarGridSpec(
            num_scalar_prefetch=len(scalars),
            grid=(images,),
            in_specs=[image_spec(a.shape) for a in per_image]
            + [pl.BlockSpec(memory_space=pltpu.VMEM) for _ in whole],
            out_specs=[image_spec((images,) + shape) for shape, _ in out_image]
            + [pl.BlockSpec(shape, lambda i, *_: (0, 0)) for shape in out_sum],
            scratch_shapes=list(scratch),
        ),
        out_shape=[jax.ShapeDtypeStruct((images,) + shape, dtype) for shape, dtype in out_image]
        + [jax.ShapeDtypeStruct(shape, F32) for shape in out_sum],
        compiler_params=pltpu.CompilerParams(vmem_limit_bytes=VMEM_BYTES),
        name=name,
    )(*scalars, *per_image, *whole)


def first_forward(resolution, patches, dense, attention, positions, gains, width):
    pixels = patches.shape[2]

    def body(rows, limit, numbers, images, whole, outs, sums, scratch):
        dense_ref, attention_ref, position_ref, gain_ref = whole
        start, qkv, context, middle, last = outs
        place = position_ref[0 if limit is not None else 1, :rows]
        embedded = masked_rows(limit, nn(images[0][:rows], dense_ref[:pixels]) + place)
        start[:rows] = embedded
        middle_rows = attention_forward(
            rows, limit, embedded, gain_ref, attention_ref, qkv, context
        )
        middle[:rows] = middle_rows
        last[:rows] = mlp_forward(rows, middle_rows, gain_ref, dense_ref, pixels)

    return by_image(
        "first_forward",
        body,
        [resolution],
        [patches],
        [dense, attention, positions, gains],
        [
            ((LEN, width), F32),
            ((LEN, 3 * width), BF16),
            ((LEN, width), BF16),
            ((LEN, width), F32),
            ((LEN, width), F32),
        ],
        [],
    )


def sparse_forward(resolution, hidden, mixing, attention, router, gains):
    width = hidden.shape[2]
    experts = router.shape[0]

    def body(rows, limit, numbers, images, whole, outs, sums, scratch):
        attention_ref, router_ref, gain_ref = whole
        before, qkv, context, middle, combine, slots = ([None] + list(outs))[-6:]
        hidden_rows = images[0][:rows]
        if mixing is not None:
            hidden_rows = hidden_rows + nn(images[1][:rows], images[2][...])
            before[:rows] = hidden_rows
        middle_rows = attention_forward(
            rows, limit, hidden_rows, gain_ref, attention_ref, qkv, context
        )
        middle[:rows] = middle_rows
        _, _, normed, dispatch, share = route(limit, middle_rows, gain_ref, router_ref)
        combine[:rows] = share.astype(BF16)
        slots[...] = tn(dispatch.astype(BF16), normed).astype(BF16)

    outs = [
        ((LEN, 3 * width), BF16),
        ((LEN, width), BF16),
        ((LEN, width), F32),
        ((LEN, experts), BF16),
        ((experts, width), BF16),
    ]
    if mixing is not None:
        outs = [((LEN, width), F32)] + outs
    return by_image(
        "sparse_forward",
        body,
        [resolution],
        [hidden] + list(mixing or ()),
        [attention, router, gains],
        outs,
        [],
    )


def top(resolution, labels, middle, combine, returned, head, head_bias, last_gains, classes, images):
    width = middle.shape[2]
    experts = returned.shape[1]
    padded = head.shape[1]

    def body(rows, limit, numbers, per_image, whole, outs, sums, scratch):
        middle_ref, combine_ref, returned_ref = per_image
        head_ref, bias_ref, gain_ref = whole
        grad_hidden, grad_returned = outs
        grad_head, grad_bias_row, grad_gains, loss = sums
        length = float(LEN if limit is None else LEN_LO)
        share = combine_ref[:rows]
        hidden = middle_ref[:rows] + nn(share, returned_ref[...])
        unit, rate = normalise(hidden)
        normed = masked_rows(limit, unit * gain_ref[0:1] + gain_ref[1:2])
        pooled = jnp.sum(normed, 0, keepdims=True) * (1.0 / length)
        one_row = (row_number((8, width)) == 0).astype(F32)
        pooled_b = (one_row * pooled).astype(BF16)
        logits = nn(pooled_b, head_ref[...])[0:1] + bias_ref[...]
        shifted = logits - jnp.max(logits, 1, keepdims=True)
        raised = jnp.exp(shifted)
        total = jnp.sum(raised, 1, keepdims=True)
        log_probs = shifted - jnp.log(total)
        lane = lax.broadcasted_iota(jnp.int32, (1, padded), 1)
        target = jnp.where(lane == numbers[1], 1.0 - SMOOTH, 0.0) + jnp.where(
            lane < classes, SMOOTH / classes, 0.0
        )
        picked = jnp.sum(target * log_probs, 1, keepdims=True)
        loss[...] += jnp.broadcast_to(picked * (-1.0 / images), loss.shape)
        grad_logits = (raised * (1.0 / total) - target) * (1.0 / images)
        grad_bias_row[0:1] += grad_logits
        row_mask = (row_number((8, padded)) == 0).astype(F32)
        grad_logits_b = (row_mask * grad_logits).astype(BF16)
        grad_head[...] += tn(grad_logits_b, pooled_b)
        grad_pooled = nt(grad_logits_b, head_ref[...])[0:1] * (1.0 / length)
        grad_normed = masked_rows(limit, jnp.broadcast_to(grad_pooled, (rows, width)))
        grad_rows, grad_gain, grad_bias = normalise_back(
            unit, rate, gain_ref[0:1], grad_normed
        )
        grad_gains[0:1] += grad_gain
        grad_gains[1:2] += grad_bias
        grad_hidden[:rows] = grad_rows
        grad_returned[...] = tn(share, grad_rows.astype(BF16)).astype(BF16)

    return by_image(
        "top",
        body,
        [resolution, labels],
        [middle, combine, returned],
        [head, head_bias, last_gains],
        [((LEN, width), F32), ((experts, width), BF16)],
        [(padded, width), (8, padded), (8, width), (8, 128)],
    )


def sparse_backward(
    resolution, hidden, qkv, context, middle, grad_hidden, returned, grad_home, below, attention,
    router, gains,
):
    width = middle.shape[2]
    experts = router.shape[0]

    def body(rows, limit, numbers, images, whole, outs, sums, scratch):
        hidden_ref, qkv_ref, context_ref, middle_ref, grad_ref, returned_ref, home_ref = images[:7]
        attention_ref, router_ref, gain_ref = whole
        grad_attention, grad_router, grad_gains = sums
        grad = grad_ref[:rows]
        grad_combine = nt(grad.astype(BF16), returned_ref[...])
        unit, rate, normed, dispatch, share = route(
            limit, middle_ref[:rows], gain_ref, router_ref
        )
        home = home_ref[...]
        grad_dispatch = nt(normed, home)
        grad_normed = nn(dispatch.astype(BF16), home)
        grad_route = dispatch * (
            grad_dispatch - jnp.sum(grad_dispatch * dispatch, 0, keepdims=True)
        ) + share * (grad_combine - jnp.sum(grad_combine * share, 1, keepdims=True))
        grad_route_b = grad_route.astype(BF16)
        grad_router[...] += tn(grad_route_b, normed)
        grad_normed = grad_normed + nn(grad_route_b, router_ref[...])
        grad_in, grad_gain, grad_bias = normalise_back(unit, rate, gain_ref[2:3], grad_normed)
        grad_gains[2:3] += grad_gain
        grad_gains[3:4] += grad_bias
        grad_rows = attention_backward(
            rows, limit, hidden_ref[:rows], grad + grad_in, gain_ref, attention_ref, qkv_ref,
            context_ref, scratch[0], scratch[1], grad_attention, grad_gains,
        )
        outs[0][:rows] = grad_rows
        if below is not None:
            outs[1][...] = tn(images[7][:rows], grad_rows.astype(BF16)).astype(BF16)

    outs = [((LEN, width), F32)]
    if below is not None:
        outs.append(((experts, width), BF16))
    return by_image(
        "sparse_backward",
        body,
        [resolution],
        [hidden, qkv, context, middle, grad_hidden, returned, grad_home]
        + ([] if below is None else [below]),
        [attention, router, gains],
        outs,
        [(4 * width, width), (experts, width), (8, width)],
        [pltpu.VMEM((LEN, width), BF16), pltpu.VMEM((LEN, 3 * width), BF16)],
    )


def first_backward(resolution, patches, start, qkv, context, middle, grad_hidden, dense, attention, gains):
    width = middle.shape[2]
    pixels = patches.shape[2]

    def body(rows, limit, numbers, images, whole, outs, sums, scratch):
        patches_ref, start_ref, qkv_ref, context_ref, middle_ref, grad_ref = images
        dense_ref, attention_ref, gain_ref = whole
        grad_dense, grad_attention, grad_gains, grad_low, grad_high = sums
        grad_middle = mlp_backward(
            rows, middle_ref[:rows], grad_ref[:rows], gain_ref, dense_ref, pixels, grad_dense,
            grad_gains,
        )
        grad_rows = attention_backward(
            rows, limit, start_ref[:rows], grad_middle, gain_ref, attention_ref, qkv_ref,
            context_ref, scratch[0], scratch[1], grad_attention, grad_gains,
        )
        grad_rows = masked_rows(limit, grad_rows)
        grad_dense[:pixels] += tn(patches_ref[:rows], grad_rows.astype(BF16))
        if limit is None:
            grad_high[...] += grad_rows
        else:
            grad_low[...] += grad_rows

    return by_image(
        "first_backward",
        body,
        [resolution],
        [patches, start, qkv, context, middle, grad_hidden],
        [dense, attention, gains],
        [],
        [(dense.shape[0], width), (4 * width, width), (8, width), (ROWS_LO, width), (LEN, width)],
        [pltpu.VMEM((LEN, width), BF16), pltpu.VMEM((LEN, 3 * width), BF16)],
    )


def to_experts(values):
    return lax.all_to_all(values, "fsdp", split_axis=1, concat_axis=0, tiled=True)


def from_experts(values):
    return lax.all_to_all(values, "fsdp", split_axis=0, concat_axis=1, tiled=True)


def all_rows(values):
    return lax.all_gather(to_experts(values), "dp", axis=0, tiled=True).transpose(1, 0, 2)


def rows_home(part):
    shared = lax.psum_scatter(part.transpose(1, 0, 2), "dp", scatter_dimension=0, tiled=True)
    return from_experts(shared.astype(BF16))


def plain_exchange(layer, values, received, expert_in, expert_out):
    win, wout = expert_in[layer].astype(BF16), expert_out[layer].astype(BF16)
    rows = all_rows(values)
    if received is None:
        hid = gelu(matmul(rows, win, "end,edf->enf")).astype(BF16)
        return rows_home(matmul(hid, wout, "enf,efd->end")), rows
    hid, slope = gelu_both(matmul(received, win, "end,edf->enf"))
    hid = hid.astype(BF16)
    grad_pre = (matmul(rows, wout, "end,efd->enf") * slope).astype(BF16)
    home = rows_home(matmul(grad_pre, win, "enf,edf->end"))

    def gram(values):
        return matmul(values, values, "enk,emk->enm")

    squares = gram(received) * gram(grad_pre) + gram(hid) * gram(rows)
    return home, hid, grad_pre, rows, jnp.sum(squares, (0, 1)).reshape(1, -1)


def fetch_layer(attention_t, router_t):
    part, width = attention_t.shape
    part_cols, part_rows = router_t.shape
    flat = router_t.reshape(-1)
    pack = jnp.concatenate(
        [attention_t, jnp.pad(flat, (0, -flat.size % width)).reshape(-1, width)], 0
    )
    both = lax.all_gather(pack, ("dp", "fsdp"), axis=0)
    rows_dp = lax.axis_size("dp")
    cols_fsdp = lax.axis_size("fsdp")
    router = (
        both[:, part:]
        .reshape(rows_dp * cols_fsdp, -1)[:, : flat.size]
        .reshape(rows_dp, cols_fsdp, part_cols, part_rows)
        .transpose(1, 2, 0, 3)
        .reshape(cols_fsdp * part_cols, rows_dp * part_rows)
    )
    return both[:, :part].reshape(-1, width), router


def share_layer(grad_attention, grad_router, part_cols, part_rows):
    rows_dp = lax.axis_size("dp")
    cols_fsdp = lax.axis_size("fsdp")
    devices = rows_dp * cols_fsdp
    width = grad_attention.shape[1]
    router = (
        grad_router.reshape(cols_fsdp, part_cols, rows_dp, part_rows)
        .transpose(2, 0, 1, 3)
        .reshape(devices, -1)
    )
    router = jnp.pad(router, ((0, 0), (0, -part_cols * part_rows % width)))
    router = router.reshape(devices, -1, width)
    pack = jnp.concatenate([grad_attention.reshape(devices, -1, width), router], 1)
    mine = lax.psum_scatter(pack, ("dp", "fsdp"), scatter_dimension=0, tiled=False)
    part = grad_attention.shape[0] // devices
    return mine[:part], mine[part:].reshape(-1)[: part_cols * part_rows].reshape(part_cols, part_rows)


BITS = 4
GATHER_ORDERS = ((3, 2, 0, 1), (0, 1, 2, 3), (0, 1, 3, 2))
MESH_IDS = pl.DeviceIdType.MESH


def my_bits():
    at = lax.axis_index("fsdp")
    return [(at // (1 << (BITS - 1 - bit))) % 2 for bit in range(BITS)]


def partner_of(bit):
    at = lax.axis_index("fsdp")
    step = 1 << (BITS - 1 - bit)
    return (lax.axis_index("dp"), at + step * (1 - 2 * ((at // step) % 2)))


def sibling():
    return (1 - lax.axis_index("dp"), lax.axis_index("fsdp"))


def greet_partners():
    barrier = pltpu.get_barrier_semaphore()
    others = [partner_of(bit) for bit in range(BITS)] + [sibling()]
    for other in others:
        pl.semaphore_signal(barrier, inc=1, device_id=other, device_id_type=MESH_IDS)
    pl.semaphore_wait(barrier, len(others))


def send(source, target, send_sem, recv_sem, device):
    copy = pltpu.make_async_remote_copy(
        src_ref=source,
        dst_ref=target,
        send_sem=send_sem,
        recv_sem=recv_sem,
        device_id=device,
        device_id_type=MESH_IDS,
    )
    copy.start()
    return copy


def spread(parts, sems):
    mine = my_bits()
    core = lax.axis_index("dp")
    to_send, to_get, pass_send, pass_get = sems

    def view(part, stage, other):
        ref, lane_part, order = part
        index = []
        for bit in range(BITS):
            if bit in order[:stage]:
                index.append(slice(None))
            elif other and bit == order[stage]:
                index.append(1 - mine[bit])
            else:
                index.append(mine[bit])
        return ref.at[(core, *index, slice(None), lane_part)]

    def go(number, stage):
        block = view(parts[number], stage, False)
        return send(
            block, block, to_send.at[number, stage], to_get.at[number, stage],
            partner_of(parts[number][2][stage]),
        )

    def hand_over(number, slot, block):
        return send(block, block, pass_send.at[number, slot], pass_get.at[number, slot], sibling())

    going = [go(number, 0) for number in range(len(parts))]
    handed = [
        hand_over(number, BITS, view(parts[number], 0, False)) for number in range(len(parts))
    ]
    for stage in range(BITS):
        for number in range(len(parts)):
            going[number].wait()
            if stage + 1 < BITS:
                going[number] = go(number, stage + 1)
            handed.append(hand_over(number, stage, view(parts[number], stage, True)))
    for copy in handed:
        copy.wait()


def spread_sems(count):
    return [pltpu.SemaphoreType.DMA((count, BITS + 1)) for _ in range(4)]


def lane_parts(width):
    return [slice(start, start + 128) for start in range(0, width, 128)]


def gather_all(shards, collective_id):
    count = len(shards)
    width = shards[0].shape[1]
    cuts = lane_parts(width)

    def kernel(*refs):
        ins, outs, sems = refs[:count], refs[count : 2 * count], refs[2 * count :]
        place = (lax.axis_index("dp"), *my_bits())
        for ref, out in zip(ins, outs):
            out[place] = ref[...]
        greet_partners()
        spread(
            [
                (out, cut, GATHER_ORDERS[number % 3])
                for number, cut in enumerate(cuts)
                for out in outs
            ],
            sems,
        )

    outs = pl.pallas_call(
        kernel,
        in_specs=[pl.BlockSpec(memory_space=pltpu.VMEM)] * count,
        out_specs=[pl.BlockSpec(memory_space=pltpu.VMEM)] * count,
        out_shape=[jax.ShapeDtypeStruct((2,) * (BITS + 1) + s.shape, s.dtype) for s in shards],
        scratch_shapes=spread_sems(count * len(cuts)),
        compiler_params=pltpu.CompilerParams(
            collective_id=collective_id, has_side_effects=True, vmem_limit_bytes=VMEM_BYTES
        ),
        name="gather_all",
    )(*shards)
    return [out.reshape(-1, width) for out in outs]


def reduce_all(grads, stats, shared, collective_id):
    _, rows, width = grads.shape
    cuts = lane_parts(width)
    parts = len(cuts)
    orders = [tuple(reversed(GATHER_ORDERS[number % 3])) for number in range(parts)]

    def kernel(grads_ref, stats_ref, mine_ref, shared_ref, total_ref, *scratch):
        sums, first_get = scratch[:2]
        gets = scratch[2 : 2 + BITS]
        stats_all = scratch[2 + BITS]
        local_sem, pair_send, pair_get, to_send, to_get = scratch[3 + BITS : 8 + BITS]
        sems = scratch[8 + BITS :]
        core = lax.axis_index("dp")
        bits = my_bits()
        local = [
            pltpu.make_async_copy(
                grads_ref.at[core, :, :, :, :, :, cut],
                sums.at[:, :, :, :, :, cut],
                local_sem.at[number],
            )
            for number, cut in enumerate(cuts)
        ]
        for copy in local:
            copy.start()
        greet_partners()
        pairs = [
            send(
                grads_ref.at[1 - core, :, :, :, :, :, cut],
                first_get.at[:, :, :, :, :, cut],
                pair_send.at[number],
                pair_get.at[number],
                sibling(),
            )
            for number, cut in enumerate(cuts)
        ]

        def index(number, stage, own):
            order = orders[number]
            found = []
            for bit in range(BITS):
                if bit in order[:stage]:
                    found.append(bits[bit])
                elif bit == order[stage]:
                    found.append(bits[bit] if own else 1 - bits[bit])
                else:
                    found.append(slice(None))
            return (*found, slice(None), cuts[number])

        def go(number, stage):
            return send(
                sums.at[index(number, stage, False)],
                gets[stage].at[number],
                to_send.at[number, stage],
                to_get.at[number, stage],
                partner_of(orders[number][stage]),
            )

        going = []
        for number in range(parts):
            local[number].wait()
            pairs[number].wait()
            whole = (slice(None),) * (BITS + 1) + (cuts[number],)
            sums[whole] = sums[whole] + first_get[whole]
            going.append(go(number, 0))
        place = tuple(bits)
        for stage in range(BITS):
            for number in range(parts):
                going[number].wait()
                if stage + 1 < BITS:
                    at = index(number, stage, True)
                    sums[at] = sums[at] + gets[stage][number]
                    going[number] = go(number, stage + 1)
                else:
                    at = index(number, stage, True)
                    mine_ref[:, cuts[number]] = sums[at].astype(F32) + gets[stage][number].astype(F32)
        mine = mine_ref[...]
        squares = jnp.sum(jnp.sum(mine * mine, 0, keepdims=True), 1, keepdims=True)
        top_row = (row_number((8, 128)) == 0).astype(F32)
        stats_all[(core, *place)] = stats_ref[...] + top_row * squares
        shared_ref[(core, *place)] = mine_ref[rows - shared :, :].astype(BF16)
        spread(
            [
                (shared_ref, cut, GATHER_ORDERS[number % 3]) for number, cut in enumerate(cuts)
            ]
            + [(stats_all, slice(0, 128), GATHER_ORDERS[1])],
            sems,
        )
        total_ref[...] = jnp.sum(stats_all[...].reshape(32, 8, 128), 0)

    grid = (2,) * BITS
    return pl.pallas_call(
        kernel,
        in_specs=[pl.BlockSpec(memory_space=pl.ANY), pl.BlockSpec(memory_space=pltpu.VMEM)],
        out_specs=[pl.BlockSpec(memory_space=pltpu.VMEM)] * 3,
        out_shape=[
            jax.ShapeDtypeStruct((rows, width), F32),
            jax.ShapeDtypeStruct((2,) + grid + (shared, width), BF16),
            jax.ShapeDtypeStruct((8, 128), F32),
        ],
        scratch_shapes=[pltpu.VMEM(grid + (rows, width), BF16)] * 2
        + [pltpu.VMEM((parts,) + (2,) * (BITS - 1 - stage) + (rows, 128), BF16) for stage in range(BITS)]
        + [pltpu.VMEM((2,) + grid + (8, 128), F32)]
        + [pltpu.SemaphoreType.DMA((parts,))] * 3
        + [pltpu.SemaphoreType.DMA((parts, BITS))] * 2
        + spread_sems(parts + 1),
        compiler_params=pltpu.CompilerParams(
            collective_id=collective_id, has_side_effects=True, vmem_limit_bytes=VMEM_BYTES
        ),
        name="reduce_all",
    )(grads.reshape((2,) + grid + (rows, width)), stats)


def chip(at):
    return (lax.axis_index("dp"), at)


def greet_all(chips):
    barrier = pltpu.get_barrier_semaphore()
    me = lax.axis_index("fsdp")

    def one(step, carry):
        pl.semaphore_signal(
            barrier, inc=1, device_id=chip((me + step) % chips), device_id_type=MESH_IDS
        )
        return carry

    lax.fori_loop(1, chips, one, 0)
    pl.semaphore_signal(barrier, inc=1, device_id=sibling(), device_id_type=MESH_IDS)
    pl.semaphore_wait(barrier, chips)


def swap_start(chips, source, target, send_sem, get_sem):
    me = lax.axis_index("fsdp")

    def one(step, carry):
        other = (me + step) % chips
        send(source.at[other], target.at[me], send_sem.at[other], get_sem.at[me], chip(other))
        return carry

    lax.fori_loop(1, chips, one, 0)


def swap_sent(chips, step, source, target, send_sem, get_sem):
    me = lax.axis_index("fsdp")
    to = (me + step) % chips
    pltpu.make_async_remote_copy(
        src_ref=source.at[to], dst_ref=target.at[me], send_sem=send_sem.at[to],
        recv_sem=get_sem.at[me], device_id=chip(to), device_id_type=MESH_IDS,
    ).wait_send()


def swap_arrived(chips, step, source, target, send_sem, get_sem):
    origin = (lax.axis_index("fsdp") + chips - step) % chips
    pltpu.make_async_remote_copy(
        src_ref=source.at[origin], dst_ref=target.at[origin], send_sem=send_sem.at[origin],
        recv_sem=get_sem.at[origin], device_id=chip(origin), device_id_type=MESH_IDS,
    ).wait_recv()
    return origin


def exchange(layer, values, received, expert_in, expert_out, collective_id):
    images, experts, width = values.shape
    chips = lax.axis_size("fsdp")
    cores = lax.axis_size("dp")
    local, _, hidden = expert_in.shape[1:]
    rows = images * local
    half = chips * images
    every = cores * half
    backward = received is not None

    def kernel(*refs):
        if backward:
            values_ref, received_ref, in_ref, out_ref = refs[:4]
            home_ref, hid_ref, pre_ref, gout_ref, squares_ref = refs[4:9]
            slope_ref = refs[9]
            scratch = refs[10:]
        else:
            values_ref, in_ref, out_ref = refs[:3]
            home_ref, received_ref = refs[3:5]
            scratch = refs[5:]
        win, wout, outbox, inbox, parts, pair_out, pair_in, sorted_ref, backbox, homebox = scratch[:10]
        win_sem, wout_sem, send_one, get_one, pass_send, pass_get, pair_send, pair_get, send_two, get_two = scratch[10:]
        core = lax.axis_index("dp")
        me = lax.axis_index("fsdp")

        def fetch(e):
            return (
                pltpu.make_async_copy(in_ref.at[layer, e], win.at[e], win_sem.at[e]),
                pltpu.make_async_copy(out_ref.at[layer, e], wout.at[e], wout_sem.at[e]),
            )

        def start_fetch(e, carry):
            for copy in fetch(e):
                copy.start()
            return carry

        lax.fori_loop(0, local, start_fetch, 0)
        whole = [values_ref[image].astype(F32) for image in range(images)]
        for at in range(chips):
            outbox[at] = jnp.concatenate(
                [one[at * local : (at + 1) * local] for one in whole], 0
            ).astype(BF16)
        greet_all(chips)
        swap_start(chips, outbox, inbox.at[core], send_one, get_one)
        inbox[core, me] = outbox[me]

        def hand(at):
            block = inbox.at[core, at]
            return pltpu.make_async_remote_copy(
                src_ref=block, dst_ref=block, send_sem=pass_send.at[at],
                recv_sem=pass_get.at[at], device_id=sibling(), device_id_type=MESH_IDS,
            )

        def handed(at):
            block = inbox.at[1 - core, at]
            return pltpu.make_async_remote_copy(
                src_ref=block, dst_ref=block, send_sem=pass_send.at[at],
                recv_sem=pass_get.at[at], device_id=sibling(), device_id_type=MESH_IDS,
            )

        hand(me).start()
        if backward:

            def ahead(e, carry):
                for copy in fetch(e):
                    copy.wait()
                rec = received_ref[e]
                hid, slope = gelu_both(nn(rec, win[e].astype(BF16)))
                slope_ref[e] = slope
                hid_ref[e] = hid.astype(BF16)
                return carry

            lax.fori_loop(0, local, ahead, 0)

        def arrive(step, carry):
            hand(swap_arrived(chips, step, outbox, inbox.at[core], send_one, get_one)).start()
            return carry

        lax.fori_loop(1, chips, arrive, 0)

        def all_handed(at, carry):
            handed(at).wait_recv()
            return carry

        lax.fori_loop(0, chips, all_handed, 0)
        arrived = inbox[...].reshape(every * local, width)
        pick_row = lax.broadcasted_iota(jnp.int32, (every, every * local), 0)
        pick_col = lax.broadcasted_iota(jnp.int32, (every, every * local), 1)
        wanted = pick_row * local - pick_col

        def pair_copy(e):
            return pltpu.make_async_remote_copy(
                src_ref=pair_out.at[e], dst_ref=pair_in.at[e], send_sem=pair_send.at[e],
                recv_sem=pair_get.at[e], device_id=sibling(), device_id_type=MESH_IDS,
            )

        if backward:
            squares_ref[...] = jnp.zeros_like(squares_ref)

        def work(e, carry):
            pick = (wanted == -e).astype(F32).astype(BF16)
            mine = nn(pick, arrived).astype(BF16)
            if backward:
                gout_ref[e] = mine
                grad_pre = (nt(mine, wout[e].astype(BF16)) * slope_ref[e]).astype(BF16)
                pre_ref[e] = grad_pre
                part = nt(grad_pre, win[e].astype(BF16))
                rec, hid = received_ref[e], hid_ref[e]
                product = nt(rec, rec) * nt(grad_pre, grad_pre) + nt(hid, hid) * nt(mine, mine)
                squares_ref[...] += jnp.sum(product.reshape(every // 8, 8, every), 0)
            else:
                for copy in fetch(e):
                    copy.wait()
                received_ref[e] = mine
                hid = gelu(nn(mine, win[e].astype(BF16))).astype(BF16)
                part = nn(hid, wout[e].astype(BF16))
            parts[e] = part.reshape(cores, half, width)
            pair_out[e] = parts[e, 1 - core].astype(BF16)
            pair_copy(e).start()
            return carry

        lax.fori_loop(0, local, work, 0)

        def add(e, carry):
            pair_copy(e).wait_recv()
            sorted_ref[pl.ds(pl.multiple_of(e * half, half), half)] = (
                parts[e, core] + pair_in[e].astype(F32)
            ).astype(BF16)
            return carry

        lax.fori_loop(0, local, add, 0)
        back_row = lax.broadcasted_iota(jnp.int32, (half * local, half * local), 0)
        back_col = lax.broadcasted_iota(jnp.int32, (half * local, half * local), 1)
        back = (back_row == (back_col % half) * local + back_col // half).astype(F32).astype(BF16)
        backbox[...] = nn(back, sorted_ref[...]).astype(BF16).reshape(chips, rows, width)
        swap_start(chips, backbox, homebox, send_two, get_two)
        homebox[me] = backbox[me]

        def home(step, carry):
            swap_arrived(chips, step, backbox, homebox, send_two, get_two)
            return carry

        lax.fori_loop(1, chips, home, 0)
        blocks = [homebox[at].astype(F32) for at in range(chips)]
        for image in range(images):
            home_ref[image] = jnp.concatenate(
                [block[image * local : (image + 1) * local] for block in blocks], 0
            ).astype(BF16)

        def drain(step, carry):
            swap_sent(chips, step, outbox, inbox.at[core], send_one, get_one)
            swap_sent(chips, step, backbox, homebox, send_two, get_two)
            return carry

        lax.fori_loop(1, chips, drain, 0)

        def drain_pass(at, carry):
            hand(at).wait_send()
            return carry

        lax.fori_loop(0, chips, drain_pass, 0)

        def drain_pair(e, carry):
            pair_copy(e).wait_send()
            return carry

        lax.fori_loop(0, local, drain_pair, 0)

    inside = pl.BlockSpec(memory_space=pltpu.VMEM)
    outside = pl.BlockSpec(memory_space=pl.ANY)
    shape = jax.ShapeDtypeStruct
    home_shape = shape((images, experts, width), BF16)
    if backward:
        out_shape = [
            home_shape,
            shape((local, every, hidden), BF16),
            shape((local, every, hidden), BF16),
            shape((local, every, width), BF16),
            shape((8, every), F32),
        ]
        operands = (values, received, expert_in, expert_out)
        in_specs = [inside, inside, outside, outside]
        extra = [pltpu.VMEM((local, every, hidden), F32)]
    else:
        out_shape = [home_shape, shape((local, every, width), BF16)]
        operands = (values, expert_in, expert_out)
        in_specs = [inside, outside, outside]
        extra = []
    dma = pltpu.SemaphoreType.DMA
    return pl.pallas_call(
        kernel,
        in_specs=in_specs,
        out_specs=[inside] * len(out_shape),
        out_shape=out_shape,
        scratch_shapes=extra
        + [
            pltpu.VMEM((local, width, hidden), F32),
            pltpu.VMEM((local, hidden, width), F32),
            pltpu.VMEM((chips, rows, width), BF16),
            pltpu.VMEM((cores, chips, rows, width), BF16),
            pltpu.VMEM((local, cores, half, width), F32),
            pltpu.VMEM((local, half, width), BF16),
            pltpu.VMEM((local, half, width), BF16),
            pltpu.VMEM((local * half, width), BF16),
            pltpu.VMEM((chips, rows, width), BF16),
            pltpu.VMEM((chips, rows, width), BF16),
        ]
        + [dma((local,))] * 2
        + [dma((chips,))] * 4
        + [dma((local,))] * 2
        + [dma((chips,))] * 2,
        compiler_params=pltpu.CompilerParams(
            collective_id=collective_id, has_side_effects=True, vmem_limit_bytes=VMEM_BYTES
        ),
        name="exchange_back" if backward else "exchange",
    )(*operands)


def expert_adam(weight, first, second, lefts, rights, scale, rate):
    layers, local, tall, wide = weight.shape
    deep = lefts[0].shape[1]

    def kernel(scale_ref, w_ref, m_ref, s_ref, *refs):
        left_refs, right_refs = refs[:layers], refs[layers : 2 * layers]
        new_w, new_m, new_s = refs[2 * layers :]

        for layer in range(layers):

            @pl.when(pl.program_id(0) == layer)
            def _(layer=layer):
                grad = tn(left_refs[layer][...], right_refs[layer][...]) * scale_ref[0]
                moment = BETA_ONE * m_ref[...] + (1.0 - BETA_ONE) * grad
                spread_of = BETA_TWO * s_ref[...] + (1.0 - BETA_TWO) * (grad * grad)
                ratio = (moment * (1.0 / (1.0 - BETA_ONE**STEP))) / (
                    jnp.sqrt(spread_of * (1.0 / (1.0 - BETA_TWO**STEP))) + ADAM_EPS
                )
                held = w_ref[...]
                new_m[...] = moment
                new_s[...] = spread_of
                new_w[...] = held - rate * (ratio + WEIGHT_DECAY * held)

    def factor_spec(layer, columns):
        last = local - 1
        return pl.BlockSpec(
            (None, deep, columns),
            lambda l, e: (jnp.where(l == layer, e, jnp.where(l < layer, 0, last)), 0, 0),
        )

    block = pl.BlockSpec((None, None, tall, wide), lambda l, e: (l, e, 0, 0))
    return pl.pallas_call(
        kernel,
        grid=(layers, local),
        in_specs=[pl.BlockSpec(memory_space=pltpu.SMEM)]
        + [block] * 3
        + [factor_spec(layer, tall) for layer in range(layers)]
        + [factor_spec(layer, wide) for layer in range(layers)],
        out_specs=[block] * 3,
        out_shape=[jax.ShapeDtypeStruct(weight.shape, F32)] * 3,
        compiler_params=pltpu.CompilerParams(vmem_limit_bytes=VMEM_BYTES),
        name="expert_adam",
    )(scale, weight, first, second, *lefts, *rights)


def adam(weight, first, second, grad, rate):
    first = BETA_ONE * first + (1.0 - BETA_ONE) * grad
    second = BETA_TWO * second + (1.0 - BETA_TWO) * grad * grad
    ratio = first / (1.0 - BETA_ONE**STEP) / (jnp.sqrt(second / (1.0 - BETA_TWO**STEP)) + ADAM_EPS)
    return (weight - rate * (ratio + WEIGHT_DECAY * weight), first, second)


def on_device(
    patches,
    resolution,
    labels,
    dense_weights,
    attention,
    router,
    expert_in,
    expert_out,
    classifier,
    norm_table,
    dense_weights_first,
    dense_weights_second,
    attention_first,
    attention_second,
    router_first,
    router_second,
    expert_in_first,
    expert_in_second,
    expert_out_first,
    expert_out_second,
    classifier_first,
    classifier_second,
    norm_table_first,
    norm_table_second,
):
    layers = attention.shape[0]
    width = norm_table.shape[1]
    classes = classifier.shape[1]
    devices = lax.axis_size("dp") * lax.axis_size("fsdp")
    images = patches.shape[0] * devices
    interp = interp_matrix()
    position = norm_table[:LEN_LO]
    pos_high = jnp.dot(interp, position, precision=PRECISE)
    pos_low = jnp.pad(position, ((0, LEN - LEN_LO), (0, 0)))
    positions = jnp.stack([pos_low, pos_high])
    gains = [
        jnp.pad(norm_table[LEN_LO + 4 * layer : LEN_LO + 4 * layer + 4], ((0, 4), (0, 0)))
        for layer in range(layers)
    ]
    last_gains = jnp.pad(norm_table[LEN_LO + 4 * layers :], ((0, 6), (0, 0)))
    attention_t = attention.transpose(0, 2, 1).astype(BF16)
    router_t = router.transpose(0, 2, 1).astype(BF16)
    dense_t = dense_weights.T.astype(BF16)
    local = expert_in.shape[1]
    own = (
        lax.axis_size("dp") == 2
        and lax.axis_size("fsdp") == 1 << BITS
        and patches.shape[0] * local % 16 == 0
        and router.shape[1] * router.shape[2] % width == 0
    )
    if own:
        dense, attention_one = gather_all([dense_t, attention_t[0]], 0)
    else:
        dense, attention_one = [
            lax.all_gather(part, ("dp", "fsdp"), axis=0, tiled=True)
            for part in (dense_t, attention_t[0])
        ]
    attention_all = [attention_one]
    router_all = [None]
    for layer in range(1, layers):
        one, two = fetch_layer(attention_t[layer], router_t[layer - 1])
        attention_all.append(one)
        router_all.append(two)

    start, qkv, context, middle, hidden = first_forward(
        resolution, patches, dense, attention_all[0], positions, gains[0], width
    )
    kept = [(start, qkv, context, middle)]
    mixing = None
    for layer in range(1, layers):
        outs = sparse_forward(
            resolution, hidden, mixing, attention_all[layer], router_all[layer], gains[layer]
        )
        if mixing is not None:
            hidden = outs[0]
        qkv, context, middle, combine, slots = outs[-5:]
        if own:
            returned, received = exchange(layer - 1, slots, None, expert_in, expert_out, layer)
        else:
            returned, received = plain_exchange(layer - 1, slots, None, expert_in, expert_out)
        kept.append((hidden, qkv, context, middle, combine, returned, received))
        hidden = middle
        mixing = (combine, returned)

    padding = -classes % 128
    head = jnp.pad(classifier[:width].astype(BF16), ((0, 0), (0, padding)))
    head_bias = jnp.pad(classifier[width:], ((0, 0), (0, padding)), constant_values=NEG_FILL)
    grad_hidden, grad_returned, grad_head, grad_bias, grad_last, loss_part = top(
        resolution, labels, middle, combine, returned, head, head_bias, last_gains, classes, images
    )
    attention_grads = [None] * layers
    router_grads = [None] * (layers - 1)
    gain_grads = [None] * layers
    in_factors = [None] * (layers - 1)
    out_factors = [None] * (layers - 1)
    local_squares = 0.0
    for layer in reversed(range(1, layers)):
        before, qkv, context, middle, combine, returned, received = kept[layer]
        if own:
            outs = exchange(
                layer - 1, grad_returned, received, expert_in, expert_out, layers + layer
            )
        else:
            outs = plain_exchange(layer - 1, grad_returned, received, expert_in, expert_out)
        grad_home, hid, grad_pre, grad_out, squares = outs
        local_squares = local_squares + jnp.sum(squares)
        in_factors[layer - 1] = (received, grad_pre)
        out_factors[layer - 1] = (hid, grad_out)
        below = kept[layer - 1][4] if layer > 1 else None
        outs = sparse_backward(
            resolution, before, qkv, context, middle, grad_hidden, returned, grad_home, below,
            attention_all[layer], router_all[layer], gains[layer],
        )
        grad_hidden = outs[0]
        if below is not None:
            grad_returned = outs[1]
        grad_attention, grad_router, grad_gain = outs[-3:]
        attention_grads[layer] = grad_attention
        router_grads[layer - 1] = grad_router
        gain_grads[layer] = grad_gain[:4]
    start, qkv, context, middle = kept[0]
    grad_dense, grad_attention, grad_gain, grad_low, grad_high = first_backward(
        resolution, patches, start, qkv, context, middle, grad_hidden, dense, attention_all[0],
        gains[0],
    )
    gain_grads[0] = grad_gain[:4]
    attention_grads[0] = grad_attention
    grad_pos = grad_low[:LEN_LO] + jnp.dot(interp.T, grad_high, precision=PRECISE)
    grad_table = jnp.concatenate([grad_pos] + gain_grads + [grad_last[:2]], 0)
    loss_local = loss_part[0, 0]
    part_rows, part_cols = router.shape[1:]
    table_rows = grad_table.shape[0]
    if own:
        row_at = [0]
        blocks = []

        def block(values):
            shaped = values.astype(BF16).reshape(devices, -1, width)
            blocks.append(shaped)
            row_at.append(row_at[-1] + shaped.shape[1])

        block(grad_dense)
        for grad in attention_grads:
            block(grad)
        for grad in router_grads:
            block(
                grad.reshape(lax.axis_size("fsdp"), part_cols, lax.axis_size("dp"), part_rows)
                .transpose(2, 0, 1, 3)
                .reshape(devices, -1)
            )
        alone = row_at[-1]
        blocks.append(jnp.zeros((devices, -alone % 16, width), BF16))
        head_rows = grad_head.shape[0]
        head_pad = -head_rows % devices
        blocks.append(jnp.pad(grad_head.astype(BF16), ((0, head_pad), (0, 0))).reshape(devices, -1, width))
        bias_flat = grad_bias[0]
        bias_flat = jnp.pad(bias_flat, (0, -bias_flat.shape[0] % width)).reshape(-1, width)
        tail = jnp.concatenate([grad_table, bias_flat], 0).astype(BF16)
        tail = jnp.pad(tail, ((0, -tail.shape[0] % devices), (0, 0)))
        blocks.append(tail.reshape(devices, -1, width))
        shared_rows = blocks[-2].shape[1] + blocks[-1].shape[1]
        last_pad = -shared_rows % 16
        blocks.append(jnp.zeros((devices, last_pad, width), BF16))
        stats = jnp.concatenate(
            [
                jnp.broadcast_to(local_squares, (1, 128)),
                jnp.broadcast_to(loss_local, (1, 128)),
                jnp.zeros((6, 128), F32),
            ],
            0,
        )
        mine, shared, totals = reduce_all(
            jnp.concatenate(blocks, 1), stats, shared_rows + last_pad, 2 * layers
        )
        shared = shared.reshape(devices, -1, width).astype(F32)
        head_each = blocks[-3].shape[1]
        head_all = shared[:, :head_each].reshape(-1, width)[:classes].T
        tail_all = shared[:, head_each:shared_rows].reshape(-1, width)
        shared_table = tail_all[:table_rows]
        bias_all = tail_all[table_rows:].reshape(-1)[None, :classes]
        shared_head = jnp.concatenate([head_all, bias_all], 0)
        norm = jnp.sqrt(totals[0, 0])
        loss_total = totals[1, 0]
        pieces = [mine[row_at[i] : row_at[i + 1]] for i in range(len(row_at) - 1)]
        grad_first = pieces[0].T
        grad_attention = jnp.stack(pieces[1 : 1 + layers]).transpose(0, 2, 1)
        grad_router_all = jnp.stack(
            [piece.reshape(part_cols, part_rows).T for piece in pieces[1 + layers :]]
        )
    else:
        grad_first = lax.psum_scatter(
            grad_dense, ("dp", "fsdp"), scatter_dimension=0, tiled=True
        ).T
        shares = [
            share_layer(attention_grads[layer], router_grads[layer - 1], part_cols, part_rows)
            for layer in range(1, layers)
        ]
        first_share = lax.psum_scatter(
            attention_grads[0], ("dp", "fsdp"), scatter_dimension=0, tiled=True
        )
        grad_attention = jnp.stack([first_share] + [share[0] for share in shares])
        grad_attention = grad_attention.transpose(0, 2, 1)
        grad_router_all = jnp.stack([share[1] for share in shares]).transpose(0, 2, 1)
        local_squares = (
            local_squares
            + jnp.sum(grad_first * grad_first)
            + jnp.sum(grad_attention * grad_attention)
            + jnp.sum(grad_router_all * grad_router_all)
        )
        grad_head = jnp.concatenate([grad_head[:classes].T, grad_bias[0:1, :classes]], 0)
        shared_head, shared_table, loss_total, squares = lax.psum(
            (grad_head, grad_table, loss_local, local_squares), ("dp", "fsdp")
        )
        norm = jnp.sqrt(
            squares + jnp.sum(shared_head * shared_head) + jnp.sum(shared_table * shared_table)
        )
    scale = jnp.minimum(1.0, CLIP_NORM / norm)
    scale_row = scale.reshape(1)

    def experts_updated(weight, first, second, factors, rate):
        lefts, rights = zip(*factors)
        return tuple(expert_adam(weight, first, second, lefts, rights, scale_row, rate))

    updates = (
        adam(dense_weights, dense_weights_first, dense_weights_second, grad_first * scale, LEARN_RATE),
        adam(attention, attention_first, attention_second, grad_attention * scale, ATTENTION_RATE),
        adam(router, router_first, router_second, grad_router_all * scale, LEARN_RATE),
        experts_updated(expert_in, expert_in_first, expert_in_second, in_factors, EXPERT_RATE),
        experts_updated(expert_out, expert_out_first, expert_out_second, out_factors, LEARN_RATE),
        adam(classifier, classifier_first, classifier_second, shared_head * scale, LEARN_RATE),
        adam(norm_table, norm_table_first, norm_table_second, shared_table * scale, TABLE_RATE),
    )
    return (loss_total, norm) + tuple(part for update in updates for part in update)


def solution(mesh):
    spread = P(("dp", "fsdp"))
    weights = (
        P(None, ("dp", "fsdp")),
        P(None, None, ("dp", "fsdp")),
        P(None, "dp", "fsdp"),
        P(None, "fsdp", None, "dp"),
        P(None, "fsdp", "dp", None),
        P(),
        P(),
    )
    moments = tuple(spec for spec in weights for _ in range(2))
    triples = tuple(spec for spec in weights for _ in range(3))
    return jax.shard_map(
        on_device,
        mesh=mesh,
        in_specs=(spread, spread, spread) + weights + moments,
        out_specs=(P(), P()) + triples,
        check_vma=False,
    )
```

```python
import functools

import jax
import jax.numpy as jnp
from jax import lax
from jax.experimental import pallas as pl
from jax.experimental.pallas import tpu as pltpu
from jax.sharding import PartitionSpec as P

HEADS = 6
FF = 1536
G_LO = 14
G_HI = 24
LEN = 576
LEN_LO = 196
ROWS_LO = 208
STEP = 10


LN_EPS = 1e-06
CLIP_NORM = 0.001
LEARN_RATE = 0.05
ATTENTION_RATE = 0.15
EXPERT_RATE = 1.0
TABLE_RATE = 0.5
BETA_ONE = 0.9
BETA_TWO = 0.95
ADAM_EPS = 1e-10
WEIGHT_DECAY = 0.1
SMOOTH = 0.1
NEG_FILL = -1e30
PRECISE = lax.Precision.HIGHEST
F32 = jnp.float32
BF16 = jnp.bfloat16
VMEM_BYTES = 60 * 1024 * 1024


def interp_matrix():
    rows = jnp.arange(G_HI, dtype=jnp.float32)[:, None]
    cols = jnp.arange(G_LO, dtype=jnp.float32)[None, :]
    weight = jnp.maximum(0.0, 1.0 - jnp.abs(rows * (G_LO - 1) - cols * (G_HI - 1)) / (G_HI - 1))
    return (weight[:, None, :, None] * weight[None, :, None, :]).reshape(G_HI * G_HI, G_LO * G_LO)


def matmul(left, right, form):
    return jnp.einsum(form, left, right, preferred_element_type=jnp.float32)


def contract(left, right, left_dim, right_dim):
    return lax.dot_general(
        left, right, (((left_dim,), (right_dim,)), ((), ())), preferred_element_type=F32
    )


def nn(left, right):
    return contract(left, right, 1, 0)


def nt(left, right):
    return contract(left, right, 1, 1)


def tn(left, right):
    return contract(left, right, 0, 0)


def normalise(values):
    center = values - jnp.mean(values, -1, keepdims=True)
    rate = lax.rsqrt(jnp.mean(center * center, -1, keepdims=True) + LN_EPS)
    return center * rate, rate


def normalise_back(unit, rate, gain, grad):
    scaled = grad * gain
    inner = scaled - jnp.mean(scaled, -1, keepdims=True)
    grad_in = rate * (inner - unit * jnp.mean(scaled * unit, -1, keepdims=True))
    return (
        grad_in,
        jnp.sum(grad * unit, 0, keepdims=True),
        jnp.sum(grad, 0, keepdims=True),
    )


def row_number(shape):
    return lax.broadcasted_iota(jnp.int32, shape, 0)


def side_masks():
    lane = lax.broadcasted_iota(jnp.int32, (1, 128), 1)
    first = (lane < 64).astype(F32)
    return (first.astype(BF16), (1.0 - first).astype(BF16))


def lanes(offset):
    return pl.ds(pl.multiple_of(offset, 128), 128)


GELU_RATE = 0.7978845608028654


def gelu(v):
    return 0.5 * v * (1.0 + jnp.tanh(GELU_RATE * (v + 0.044715 * (v * v * v))))


def gelu_both(v):
    square = v * v
    bend = jnp.tanh(GELU_RATE * (v + 0.044715 * (square * v)))
    half = 0.5 * (1.0 + bend)
    slope = half + 0.5 * v * (1.0 - bend * bend) * (GELU_RATE * (1.0 + 3 * 0.044715 * square))
    return v * half, slope


def attention_rows(rows, limit, qkv, context):
    width = context.shape[1]
    first = lax.broadcasted_iota(jnp.int32, (rows, 128), 1) < 64
    masks = side_masks()
    ones = jnp.ones((rows, 128), BF16)
    for offset in range(0, width, 128):
        query = qkv[:rows, offset : offset + 128] * BF16(0.125)
        keys = qkv[:rows, width + offset : width + offset + 128]
        values = qkv[:rows, 2 * width + offset : 2 * width + offset + 128]
        summing = jnp.concatenate([values, ones], 1)
        found = []
        for side in (0, 1):
            scores = nt(query * masks[side], keys)
            if limit is not None:
                lane = lax.broadcasted_iota(jnp.int32, (rows, rows), 1)
                scores = jnp.where(lane < limit, scores, NEG_FILL)
            raised = jnp.exp(scores - jnp.max(scores, 1, keepdims=True))
            both = nn(raised.astype(BF16), summing)
            found.append(both[:, :128] * (1.0 / both[:, 128:]))
        context[:rows, offset : offset + 128] = jnp.where(first, found[0], found[1]).astype(BF16)


def scores_back(limit, keys, values, query, grad):
    scores = nt(keys, query)
    if limit is not None:
        scores = jnp.where(row_number(scores.shape) < limit, scores, NEG_FILL)
    raised = jnp.exp(scores - jnp.max(scores, 0, keepdims=True))
    probs = raised * (1.0 / jnp.sum(raised, 0, keepdims=True))
    grad_values = nn(probs.astype(BF16), grad)
    grad_probs = nt(values, grad)
    mixed = jnp.sum(probs * grad_probs, 0, keepdims=True)
    grad_scores = (probs * (grad_probs - mixed)).astype(BF16)
    return grad_scores, nn(grad_scores, query), grad_values


def attention_rows_back(rows, limit, qkv, grad_context, grad_qkv):
    width = grad_context.shape[1]
    masks = side_masks()
    first = lax.broadcasted_iota(jnp.int32, (rows, 128), 1) < 64
    for offset in range(0, width, 128):
        query = qkv[:rows, offset : offset + 128] * BF16(0.125)
        keys = qkv[:rows, width + offset : width + offset + 128]
        values = qkv[:rows, 2 * width + offset : 2 * width + offset + 128]
        grad = grad_context[:rows, offset : offset + 128]
        queries = [query * mask for mask in masks]
        grads = [grad * mask for mask in masks]
        if limit is None:
            grad_scores, grad_keys, grad_values = scores_back(
                limit, keys, values, jnp.concatenate(queries, 0), jnp.concatenate(grads, 0)
            )
            both = tn(grad_scores, keys)
            grad_query = jnp.where(first, both[:rows], both[rows:])
        else:
            one, two = [
                scores_back(limit, keys, values, queries[side], grads[side]) for side in (0, 1)
            ]
            grad_query = tn(one[0], keys * masks[0]) + tn(two[0], keys * masks[1])
            grad_keys, grad_values = one[1] + two[1], one[2] + two[2]
        grad_qkv[:rows, offset : offset + 128] = (grad_query * 0.125).astype(BF16)
        grad_qkv[:rows, width + offset : width + offset + 128] = grad_keys.astype(BF16)
        grad_qkv[:rows, 2 * width + offset : 2 * width + offset + 128] = grad_values.astype(BF16)


def attention_forward(rows, limit, hidden, gains, weights, qkv, context):
    width = hidden.shape[1]
    unit, _ = normalise(hidden)
    normed = (unit * gains[0:1] + gains[1:2]).astype(BF16)
    qkv[:rows] = nt(normed, weights[: 3 * width]).astype(BF16)
    attention_rows(rows, limit, qkv, context)
    return hidden + nn(context[:rows], weights[3 * width :])


def attention_backward(
    rows, limit, hidden, grad_middle, gains, weights, qkv, context, hold_context, hold_qkv,
    grad_weights, grad_gains,
):
    width = hidden.shape[1]
    grad_b = grad_middle.astype(BF16)
    hold_context[:rows] = nt(grad_b, weights[3 * width :]).astype(BF16)
    grad_weights[3 * width :] += tn(context[:rows], grad_b)
    attention_rows_back(rows, limit, qkv, hold_context, hold_qkv)
    unit, rate = normalise(hidden)
    normed = (unit * gains[0:1] + gains[1:2]).astype(BF16)
    grad_weights[: 3 * width] += tn(hold_qkv[:rows], normed)
    grad_normed = nn(hold_qkv[:rows], weights[: 3 * width])
    grad_in, grad_gain, grad_bias = normalise_back(unit, rate, gains[0:1], grad_normed)
    grad_gains[0:1] += grad_gain
    grad_gains[1:2] += grad_bias
    return grad_middle + grad_in


def mlp_forward(rows, middle, gains, weights, pixels):
    unit, _ = normalise(middle)
    normed = (unit * gains[2:3] + gains[3:4]).astype(BF16)
    chunk = middle.shape[1]
    total = middle
    for start in range(0, FF, chunk):
        pre = nt(normed, weights[pixels + start : pixels + start + chunk])
        out = weights[pixels + FF + start : pixels + FF + start + chunk]
        total = total + nn(gelu(pre).astype(BF16), out)
    return total


def mlp_backward(rows, middle, grad, gains, weights, pixels, grad_weights, grad_gains):
    unit, rate = normalise(middle)
    normed = (unit * gains[2:3] + gains[3:4]).astype(BF16)
    grad_b = grad.astype(BF16)
    chunk = middle.shape[1]
    grad_normed = None
    for start in range(0, FF, chunk):
        first = slice(pixels + start, pixels + start + chunk)
        second = slice(pixels + FF + start, pixels + FF + start + chunk)
        hid, slope = gelu_both(nt(normed, weights[first]))
        grad_weights[second] += tn(hid.astype(BF16), grad_b)
        grad_pre = (nt(grad_b, weights[second]) * slope).astype(BF16)
        grad_weights[first] += tn(grad_pre, normed)
        part = nn(grad_pre, weights[first])
        grad_normed = part if grad_normed is None else grad_normed + part
    grad_in, grad_gain, grad_bias = normalise_back(unit, rate, gains[2:3], grad_normed)
    grad_gains[2:3] += grad_gain
    grad_gains[3:4] += grad_bias
    return grad + grad_in


def route(limit, middle, gains, router):
    unit, rate = normalise(middle)
    normed = (unit * gains[2:3] + gains[3:4]).astype(BF16)
    logits = nt(normed, router[...])
    masked = logits
    if limit is not None:
        masked = jnp.where(row_number(logits.shape) < limit, logits, NEG_FILL)
    raised = jnp.exp(masked - jnp.max(masked, 0, keepdims=True))
    dispatch = raised * (1.0 / jnp.sum(raised, 0, keepdims=True))
    raised = jnp.exp(logits - jnp.max(logits, 1, keepdims=True))
    combine = raised * (1.0 / jnp.sum(raised, 1, keepdims=True))
    return unit, rate, normed, dispatch, combine


def masked_rows(limit, values):
    if limit is None:
        return values
    return jnp.where(row_number(values.shape) < limit, values, 0.0)


def work_of(giga):
    return pl.CostEstimate(flops=giga * 10**9, bytes_accessed=1 << 20, transcendentals=0)


def by_image(name, body, scalars, per_image, whole, out_image, out_sum, scratch=(), pack=None):
    images = scalars[0].shape[0]
    inner = pack[0] if pack else 0
    packed = 1 if pack else 0
    counts = (
        len(scalars), len(per_image), len(whole), len(out_image), packed, len(out_sum) - inner,
        inner, len(scratch),
    )

    def kernel(*refs):
        groups, at = [], 0
        for count in counts:
            groups.append(refs[at : at + count])
            at += count
        index = pl.program_id(0)
        sums = tuple(groups[6]) + tuple(groups[5])

        @pl.when(index == 0)
        def _():
            for ref in sums:
                ref[...] = jnp.zeros_like(ref)

        numbers = [ref[index] for ref in groups[0]]
        given = (*groups[1:4], sums, groups[7])

        @pl.when(numbers[0] == 1)
        def _():
            body(LEN, None, numbers, *given)

        @pl.when(numbers[0] != 1)
        def _():
            body(ROWS_LO, LEN_LO + numbers[0], numbers, *given)

        if pack:

            @pl.when(index == images - 1)
            def _():
                def write(device, carry):
                    groups[4][0][device] = pack[3](sums, device).astype(BF16)
                    return carry

                lax.fori_loop(0, pack[1], write, 0)

    width = out_sum[0][1] if pack else 0
    pack_shapes = [(pack[1], pack[2], width)] if pack else []

    def image_spec(shape):
        return pl.BlockSpec((None,) + tuple(shape[1:]), lambda i, *_: (i, 0, 0))

    return pl.pallas_call(
        kernel,
        grid_spec=pltpu.PrefetchScalarGridSpec(
            num_scalar_prefetch=len(scalars),
            grid=(images,),
            in_specs=[image_spec(a.shape) for a in per_image]
            + [pl.BlockSpec(memory_space=pltpu.VMEM) for _ in whole],
            out_specs=[image_spec((images,) + shape) for shape, _ in out_image]
            + [pl.BlockSpec(shape, lambda i, *_: (0, 0, 0)) for shape in pack_shapes]
            + [pl.BlockSpec(shape, lambda i, *_: (0, 0)) for shape in out_sum[inner:]],
            scratch_shapes=[pltpu.VMEM(shape, F32) for shape in out_sum[:inner]] + list(scratch),
        ),
        out_shape=[jax.ShapeDtypeStruct((images,) + shape, dtype) for shape, dtype in out_image]
        + [jax.ShapeDtypeStruct(shape, BF16) for shape in pack_shapes]
        + [jax.ShapeDtypeStruct(shape, F32) for shape in out_sum[inner:]],
        compiler_params=pltpu.CompilerParams(vmem_limit_bytes=VMEM_BYTES),
        cost_estimate=work_of(images * 8),
        name=name,
    )(*scalars, *per_image, *whole)


def rows_of(ref, device, count):
    return ref[pl.ds(pl.multiple_of(device * count, 8), count)]


def padded_rows(blocks):
    rows = sum(block.shape[0] for block in blocks)
    if rows % 16:
        blocks = blocks + [jnp.zeros((-rows % 16, blocks[0].shape[1]), F32)]
    return jnp.concatenate(blocks, 0) if len(blocks) > 1 else blocks[0]


def up_16(count):
    return count + -count % 16


def first_forward(resolution, patches, dense, attention, positions, gains, width):
    pixels = patches.shape[2]

    def body(rows, limit, numbers, images, whole, outs, sums, scratch):
        dense_ref, attention_ref, position_ref, gain_ref = whole
        start, qkv, context, middle, last = outs
        place = position_ref[0 if limit is not None else 1, :rows]
        embedded = masked_rows(limit, nn(images[0][:rows], dense_ref[:pixels]) + place)
        start[:rows] = embedded
        middle_rows = attention_forward(
            rows, limit, embedded, gain_ref, attention_ref, qkv, context
        )
        middle[:rows] = middle_rows
        last[:rows] = mlp_forward(rows, middle_rows, gain_ref, dense_ref, pixels)

    return by_image(
        "first_forward",
        body,
        [resolution],
        [patches],
        [dense, attention, positions, gains],
        [
            ((LEN, width), F32),
            ((LEN, 3 * width), BF16),
            ((LEN, width), BF16),
            ((LEN, width), F32),
            ((LEN, width), F32),
        ],
        [],
    )


def sparse_forward(resolution, hidden, mixing, attention, router, gains):
    width = hidden.shape[2]
    experts = router.shape[0]

    def body(rows, limit, numbers, images, whole, outs, sums, scratch):
        attention_ref, router_ref, gain_ref = whole
        before, qkv, context, middle, combine, slots = ([None] + list(outs))[-6:]
        hidden_rows = images[0][:rows]
        if mixing is not None:
            hidden_rows = hidden_rows + nn(images[1][:rows], images[2][...])
            before[:rows] = hidden_rows
        middle_rows = attention_forward(
            rows, limit, hidden_rows, gain_ref, attention_ref, qkv, context
        )
        middle[:rows] = middle_rows
        _, _, normed, dispatch, share = route(limit, middle_rows, gain_ref, router_ref)
        combine[:rows] = share.astype(BF16)
        slots[...] = tn(dispatch.astype(BF16), normed).astype(BF16)

    outs = [
        ((LEN, 3 * width), BF16),
        ((LEN, width), BF16),
        ((LEN, width), F32),
        ((LEN, experts), BF16),
        ((experts, width), BF16),
    ]
    if mixing is not None:
        outs = [((LEN, width), F32)] + outs
    return by_image(
        "sparse_forward",
        body,
        [resolution],
        [hidden] + list(mixing or ()),
        [attention, router, gains],
        outs,
        [],
    )


def top(resolution, labels, middle, combine, returned, head, head_bias, last_gains, classes, images, devices):
    width = middle.shape[2]
    experts = returned.shape[1]
    padded = head.shape[1]

    def body(rows, limit, numbers, per_image, whole, outs, sums, scratch):
        middle_ref, combine_ref, returned_ref = per_image
        head_ref, bias_ref, gain_ref = whole
        grad_hidden, grad_returned = outs
        grad_head, grad_bias_row, grad_gains, loss = sums
        length = float(LEN if limit is None else LEN_LO)
        share = combine_ref[:rows]
        hidden = middle_ref[:rows] + nn(share, returned_ref[...])
        unit, rate = normalise(hidden)
        normed = masked_rows(limit, unit * gain_ref[0:1] + gain_ref[1:2])
        pooled = jnp.sum(normed, 0, keepdims=True) * (1.0 / length)
        one_row = (row_number((8, width)) == 0).astype(F32)
        pooled_b = (one_row * pooled).astype(BF16)
        logits = nn(pooled_b, head_ref[...])[0:1] + bias_ref[...]
        shifted = logits - jnp.max(logits, 1, keepdims=True)
        raised = jnp.exp(shifted)
        total = jnp.sum(raised, 1, keepdims=True)
        log_probs = shifted - jnp.log(total)
        lane = lax.broadcasted_iota(jnp.int32, (1, padded), 1)
        target = jnp.where(lane == numbers[1], 1.0 - SMOOTH, 0.0) + jnp.where(
            lane < classes, SMOOTH / classes, 0.0
        )
        picked = jnp.sum(target * log_probs, 1, keepdims=True)
        loss[...] += jnp.broadcast_to(picked * (-1.0 / images), loss.shape)
        grad_logits = (raised * (1.0 / total) - target) * (1.0 / images)
        grad_bias_row[0:1] += grad_logits
        row_mask = (row_number((8, padded)) == 0).astype(F32)
        grad_logits_b = (row_mask * grad_logits).astype(BF16)
        grad_head[...] += tn(grad_logits_b, pooled_b)
        grad_pooled = nt(grad_logits_b, head_ref[...])[0:1] * (1.0 / length)
        grad_normed = masked_rows(limit, jnp.broadcast_to(grad_pooled, (rows, width)))
        grad_rows, grad_gain, grad_bias = normalise_back(
            unit, rate, gain_ref[0:1], grad_normed
        )
        grad_gains[0:1] += grad_gain
        grad_gains[1:2] += grad_bias
        grad_hidden[:rows] = grad_rows
        grad_returned[...] = tn(share, grad_rows.astype(BF16)).astype(BF16)

    return by_image(
        "top",
        body,
        [resolution, labels],
        [middle, combine, returned],
        [head, head_bias, last_gains],
        [((LEN, width), F32), ((experts, width), BF16)],
        [(padded, width), (8, padded), (8, width), (8, 128)],
        pack=devices
        and (
            1, devices, padded // devices,
            lambda sums, device: rows_of(sums[0], device, padded // devices),
        ),
    )


def sparse_backward(
    resolution, hidden, qkv, context, middle, grad_hidden, returned, grad_home, below, attention,
    router, gains, devices,
):
    width = middle.shape[2]
    experts = router.shape[0]
    chips = lax.axis_size("fsdp")
    local = experts // chips

    def body(rows, limit, numbers, images, whole, outs, sums, scratch):
        hidden_ref, qkv_ref, context_ref, middle_ref, grad_ref, returned_ref, home_ref = images[:7]
        attention_ref, router_ref, gain_ref = whole
        grad_attention, grad_router, grad_gains = sums
        grad = grad_ref[:rows]
        grad_combine = nt(grad.astype(BF16), returned_ref[...])
        unit, rate, normed, dispatch, share = route(
            limit, middle_ref[:rows], gain_ref, router_ref
        )
        home = home_ref[...]
        grad_dispatch = nt(normed, home)
        grad_normed = nn(dispatch.astype(BF16), home)
        grad_route = dispatch * (
            grad_dispatch - jnp.sum(grad_dispatch * dispatch, 0, keepdims=True)
        ) + share * (grad_combine - jnp.sum(grad_combine * share, 1, keepdims=True))
        grad_route_b = grad_route.astype(BF16)
        grad_router[...] += tn(grad_route_b, normed)
        grad_normed = grad_normed + nn(grad_route_b, router_ref[...])
        grad_in, grad_gain, grad_bias = normalise_back(unit, rate, gain_ref[2:3], grad_normed)
        grad_gains[2:3] += grad_gain
        grad_gains[3:4] += grad_bias
        grad_rows = attention_backward(
            rows, limit, hidden_ref[:rows], grad + grad_in, gain_ref, attention_ref, qkv_ref,
            context_ref, scratch[0], scratch[1], grad_attention, grad_gains,
        )
        outs[0][:rows] = grad_rows
        if below is not None:
            outs[1][...] = tn(images[7][:rows], grad_rows.astype(BF16)).astype(BF16)

    outs = [((LEN, width), F32)]
    if below is not None:
        outs.append(((experts, width), BF16))
    return by_image(
        "sparse_backward",
        body,
        [resolution],
        [hidden, qkv, context, middle, grad_hidden, returned, grad_home]
        + ([] if below is None else [below]),
        [attention, router, gains],
        outs,
        [(4 * width, width), (experts, width), (8, width)],
        [pltpu.VMEM((LEN, width), BF16), pltpu.VMEM((LEN, 3 * width), BF16)],
        pack=devices
        and (
            2, devices, up_16(4 * width // devices + local),
            lambda sums, device: padded_rows(
                [
                    rows_of(sums[0], device, 4 * width // devices),
                    rows_of(sums[1], device % chips, local),
                ]
            ),
        ),
    )


def first_backward(
    resolution, patches, start, qkv, context, middle, grad_hidden, dense, attention, gains, devices
):
    width = middle.shape[2]
    pixels = patches.shape[2]
    columns = dense.shape[0]

    def body(rows, limit, numbers, images, whole, outs, sums, scratch):
        patches_ref, start_ref, qkv_ref, context_ref, middle_ref, grad_ref = images
        dense_ref, attention_ref, gain_ref = whole
        grad_dense, grad_attention, grad_gains, grad_low, grad_high = sums
        grad_middle = mlp_backward(
            rows, middle_ref[:rows], grad_ref[:rows], gain_ref, dense_ref, pixels, grad_dense,
            grad_gains,
        )
        grad_rows = attention_backward(
            rows, limit, start_ref[:rows], grad_middle, gain_ref, attention_ref, qkv_ref,
            context_ref, scratch[0], scratch[1], grad_attention, grad_gains,
        )
        grad_rows = masked_rows(limit, grad_rows)
        grad_dense[:pixels] += tn(patches_ref[:rows], grad_rows.astype(BF16))
        if limit is None:
            grad_high[...] += grad_rows
        else:
            grad_low[...] += grad_rows

    return by_image(
        "first_backward",
        body,
        [resolution],
        [patches, start, qkv, context, middle, grad_hidden],
        [dense, attention, gains],
        [],
        [(columns, width), (4 * width, width), (8, width), (ROWS_LO, width), (LEN, width)],
        [pltpu.VMEM((LEN, width), BF16), pltpu.VMEM((LEN, 3 * width), BF16)],
        pack=devices
        and (
            2, devices, up_16((columns + 4 * width) // devices),
            lambda sums, device: padded_rows(
                [
                    rows_of(sums[0], device, columns // devices),
                    rows_of(sums[1], device, 4 * width // devices),
                ]
            ),
        ),
    )


def to_experts(values):
    return lax.all_to_all(values, "fsdp", split_axis=1, concat_axis=0, tiled=True)


def from_experts(values):
    return lax.all_to_all(values, "fsdp", split_axis=0, concat_axis=1, tiled=True)


def all_rows(values):
    return lax.all_gather(to_experts(values), "dp", axis=0, tiled=True).transpose(1, 0, 2)


def rows_home(part):
    shared = lax.psum_scatter(part.transpose(1, 0, 2), "dp", scatter_dimension=0, tiled=True)
    return from_experts(shared.astype(BF16))


def plain_exchange(layer, values, received, expert_in, expert_out):
    win, wout = expert_in[layer].astype(BF16), expert_out[layer].astype(BF16)
    rows = all_rows(values)
    if received is None:
        hid = gelu(matmul(rows, win, "end,edf->enf")).astype(BF16)
        return rows_home(matmul(hid, wout, "enf,efd->end")), rows
    hid, slope = gelu_both(matmul(received, win, "end,edf->enf"))
    hid = hid.astype(BF16)
    grad_pre = (matmul(rows, wout, "end,efd->enf") * slope).astype(BF16)
    home = rows_home(matmul(grad_pre, win, "enf,edf->end"))

    def gram(values):
        return matmul(values, values, "enk,emk->enm")

    squares = gram(received) * gram(grad_pre) + gram(hid) * gram(rows)
    return home, hid, grad_pre, rows, jnp.sum(squares, (0, 1)).reshape(1, -1)


def fetch_layer(attention_t, router_t):
    width = attention_t.shape[1]
    flat = router_t.reshape(-1)
    pack = jnp.concatenate(
        [attention_t, jnp.pad(flat, (0, -flat.size % width)).reshape(-1, width)], 0
    )
    return lax.all_gather(pack, ("dp", "fsdp"), axis=0)


def open_layer(both, part, part_cols, part_rows):
    width = both.shape[2]
    rows_dp = lax.axis_size("dp")
    cols_fsdp = lax.axis_size("fsdp")
    router = (
        both[:, part:]
        .reshape(rows_dp * cols_fsdp, -1)[:, : part_cols * part_rows]
        .reshape(rows_dp, cols_fsdp, part_cols, part_rows)
        .transpose(1, 2, 0, 3)
        .reshape(cols_fsdp * part_cols, rows_dp * part_rows)
    )
    return both[:, :part].reshape(-1, width), router


def share_layer(grad_attention, grad_router, part_cols, part_rows):
    rows_dp = lax.axis_size("dp")
    cols_fsdp = lax.axis_size("fsdp")
    devices = rows_dp * cols_fsdp
    width = grad_attention.shape[1]
    router = (
        grad_router.reshape(cols_fsdp, part_cols, rows_dp, part_rows)
        .transpose(2, 0, 1, 3)
        .reshape(devices, -1)
    )
    router = jnp.pad(router, ((0, 0), (0, -part_cols * part_rows % width)))
    router = router.reshape(devices, -1, width)
    pack = jnp.concatenate([grad_attention.reshape(devices, -1, width), router], 1)
    mine = lax.psum_scatter(pack, ("dp", "fsdp"), scatter_dimension=0, tiled=False)
    part = grad_attention.shape[0] // devices
    return mine[:part], mine[part:].reshape(-1)[: part_cols * part_rows].reshape(part_cols, part_rows)


BITS = 4
GATHER_ORDERS = ((3, 2, 0, 1), (0, 1, 2, 3), (0, 1, 3, 2))
MESH_IDS = pl.DeviceIdType.MESH


def my_bits():
    at = lax.axis_index("fsdp")
    return [(at // (1 << (BITS - 1 - bit))) % 2 for bit in range(BITS)]


def partner_of(bit):
    at = lax.axis_index("fsdp")
    step = 1 << (BITS - 1 - bit)
    return (lax.axis_index("dp"), at + step * (1 - 2 * ((at // step) % 2)))


def sibling():
    return (1 - lax.axis_index("dp"), lax.axis_index("fsdp"))


def greet_partners():
    barrier = pltpu.get_barrier_semaphore()
    others = [partner_of(bit) for bit in range(BITS)] + [sibling()]
    for other in others:
        pl.semaphore_signal(barrier, inc=1, device_id=other, device_id_type=MESH_IDS)
    pl.semaphore_wait(barrier, len(others))


def send(source, target, send_sem, recv_sem, device):
    copy = pltpu.make_async_remote_copy(
        src_ref=source,
        dst_ref=target,
        send_sem=send_sem,
        recv_sem=recv_sem,
        device_id=device,
        device_id_type=MESH_IDS,
    )
    copy.start()
    return copy


def spread(parts, sems):
    mine = my_bits()
    core = lax.axis_index("dp")
    to_send, to_get, pass_send, pass_get = sems

    def view(part, stage, other):
        ref, lane_part, order = part
        index = []
        for bit in range(BITS):
            if bit in order[:stage]:
                index.append(slice(None))
            elif other and bit == order[stage]:
                index.append(1 - mine[bit])
            else:
                index.append(mine[bit])
        return ref.at[(core, *index, slice(None), lane_part)]

    def go(number, stage):
        block = view(parts[number], stage, False)
        return send(
            block, block, to_send.at[number, stage], to_get.at[number, stage],
            partner_of(parts[number][2][stage]),
        )

    def hand_over(number, slot, block):
        return send(block, block, pass_send.at[number, slot], pass_get.at[number, slot], sibling())

    going = [go(number, 0) for number in range(len(parts))]
    handed = [
        hand_over(number, BITS, view(parts[number], 0, False)) for number in range(len(parts))
    ]
    for stage in range(BITS):
        for number in range(len(parts)):
            going[number].wait()
            if stage + 1 < BITS:
                going[number] = go(number, stage + 1)
            handed.append(hand_over(number, stage, view(parts[number], stage, True)))
    for copy in handed:
        copy.wait()


def spread_sems(count):
    return [pltpu.SemaphoreType.DMA((count, BITS + 1)) for _ in range(4)]


def lane_parts(width):
    return [slice(start, start + 128) for start in range(0, width, 128)]


def gather_all(shards, collective_id):
    count = len(shards)
    width = shards[0].shape[1]
    cuts = lane_parts(width)

    def kernel(*refs):
        ins, outs, sems = refs[:count], refs[count : 2 * count], refs[2 * count :]
        place = (lax.axis_index("dp"), *my_bits())
        for ref, out in zip(ins, outs):
            out[place] = ref[...]
        greet_partners()
        spread(
            [
                (out, cut, GATHER_ORDERS[number % 3])
                for number, cut in enumerate(cuts)
                for out in outs
            ],
            sems,
        )

    outs = pl.pallas_call(
        kernel,
        in_specs=[pl.BlockSpec(memory_space=pltpu.VMEM)] * count,
        out_specs=[pl.BlockSpec(memory_space=pltpu.VMEM)] * count,
        out_shape=[jax.ShapeDtypeStruct((2,) * (BITS + 1) + s.shape, s.dtype) for s in shards],
        scratch_shapes=spread_sems(count * len(cuts)),
        compiler_params=pltpu.CompilerParams(
            collective_id=collective_id, has_side_effects=True, vmem_limit_bytes=VMEM_BYTES
        ),
        cost_estimate=work_of(40),
        name="gather_all",
    )(*shards)
    return [out.reshape(-1, width) for out in outs]


def reduce_all(grads, stats, shared, halved, collective_id):
    width = grads[0].shape[2]
    count = len(grads)
    starts = [sum(grad.shape[1] for grad in grads[:at]) for at in range(count + 1)]
    rows = starts[-1]
    cuts = lane_parts(width)
    parts = len(cuts)
    orders = [tuple(reversed(GATHER_ORDERS[number % 3])) for number in range(parts)]

    def kernel(*refs):
        grads_refs = refs[:count]
        stats_ref, mine_ref, shared_ref, total_ref = refs[count : count + 4]
        scratch = refs[count + 4 :]
        sums, first_get = scratch[:2]
        gets = scratch[2 : 2 + BITS]
        stats_all = scratch[2 + BITS]
        local_sem, pair_send, pair_get, to_send, to_get = scratch[3 + BITS : 8 + BITS]
        sems = scratch[8 + BITS :]
        core = lax.axis_index("dp")
        bits = my_bits()
        places = [
            (number, at, cut, slice(starts[at], starts[at + 1]))
            for number, cut in enumerate(cuts)
            for at in range(count)
        ]
        local = {
            (number, at): pltpu.make_async_copy(
                grads_refs[at].at[core, :, :, :, :, :, cut],
                sums.at[:, :, :, :, span, cut],
                local_sem.at[number, at],
            )
            for number, at, cut, span in places
        }
        for copy in local.values():
            copy.start()
        greet_partners()
        pairs = {
            (number, at): send(
                grads_refs[at].at[1 - core, :, :, :, :, :, cut],
                first_get.at[:, :, :, :, span, cut],
                pair_send.at[number, at],
                pair_get.at[number, at],
                sibling(),
            )
            for number, at, cut, span in places
        }

        def index(number, stage, own):
            order = orders[number]
            found = []
            for bit in range(BITS):
                if bit in order[:stage]:
                    found.append(bits[bit])
                elif bit == order[stage]:
                    found.append(bits[bit] if own else 1 - bits[bit])
                else:
                    found.append(slice(None))
            return (*found, slice(None), cuts[number])

        def go(number, stage):
            return send(
                sums.at[index(number, stage, False)],
                gets[stage].at[number],
                to_send.at[number, stage],
                to_get.at[number, stage],
                partner_of(orders[number][stage]),
            )

        going = []
        for number in range(parts):
            for at in range(count):
                local[number, at].wait()
                pairs[number, at].wait()
            whole = (slice(None),) * (BITS + 1) + (cuts[number],)
            sums[whole] = sums[whole] + first_get[whole]
            going.append(go(number, 0))
        place = tuple(bits)
        for stage in range(BITS):
            for number in range(parts):
                going[number].wait()
                if stage + 1 < BITS:
                    at = index(number, stage, True)
                    sums[at] = sums[at] + gets[stage][number]
                    going[number] = go(number, stage + 1)
                else:
                    at = index(number, stage, True)
                    mine_ref[:, cuts[number]] = sums[at].astype(F32) + gets[stage][number].astype(F32)
        mine = mine_ref[...]
        row = row_number((rows, width))
        counted = mine * mine
        for low, high in halved:
            counted = jnp.where((row >= low) & (row < high), 0.5 * counted, counted)
        squares = jnp.sum(jnp.sum(counted, 0, keepdims=True), 1, keepdims=True)
        top_row = (row_number((8, 128)) == 0).astype(F32)
        stats_all[(core, *place)] = stats_ref[...] + top_row * squares
        shared_ref[(core, *place)] = mine_ref[rows - shared :, :].astype(BF16)
        spread(
            [
                (shared_ref, cut, GATHER_ORDERS[number % 3]) for number, cut in enumerate(cuts)
            ]
            + [(stats_all, slice(0, 128), GATHER_ORDERS[1])],
            sems,
        )
        total_ref[...] = jnp.sum(stats_all[...].reshape(32, 8, 128), 0)

    grid = (2,) * BITS
    return pl.pallas_call(
        kernel,
        in_specs=[pl.BlockSpec(memory_space=pl.ANY)] * count
        + [pl.BlockSpec(memory_space=pltpu.VMEM)],
        out_specs=[pl.BlockSpec(memory_space=pltpu.VMEM)] * 3,
        out_shape=[
            jax.ShapeDtypeStruct((rows, width), F32),
            jax.ShapeDtypeStruct((2,) + grid + (shared, width), BF16),
            jax.ShapeDtypeStruct((8, 128), F32),
        ],
        scratch_shapes=[pltpu.VMEM(grid + (rows, width), BF16)] * 2
        + [pltpu.VMEM((parts,) + (2,) * (BITS - 1 - stage) + (rows, 128), BF16) for stage in range(BITS)]
        + [pltpu.VMEM((2,) + grid + (8, 128), F32)]
        + [pltpu.SemaphoreType.DMA((parts, count))] * 3
        + [pltpu.SemaphoreType.DMA((parts, BITS))] * 2
        + spread_sems(parts + 1),
        compiler_params=pltpu.CompilerParams(
            collective_id=collective_id, has_side_effects=True, vmem_limit_bytes=VMEM_BYTES
        ),
        cost_estimate=work_of(60),
        name="reduce_all",
    )(*[grad.reshape((2,) + grid + grad.shape[1:]) for grad in grads], stats)


def chip(at):
    return (lax.axis_index("dp"), at)


def greet_all(chips):
    barrier = pltpu.get_barrier_semaphore()
    me = lax.axis_index("fsdp")

    def one(step, carry):
        pl.semaphore_signal(
            barrier, inc=1, device_id=chip((me + step) % chips), device_id_type=MESH_IDS
        )
        return carry

    lax.fori_loop(1, chips, one, 0)
    pl.semaphore_signal(barrier, inc=1, device_id=sibling(), device_id_type=MESH_IDS)
    pl.semaphore_wait(barrier, chips)


def swap_start(chips, source, target, send_sem, get_sem):
    me = lax.axis_index("fsdp")

    def one(step, carry):
        other = (me + step) % chips
        send(source.at[other], target.at[me], send_sem.at[other], get_sem.at[me], chip(other))
        return carry

    lax.fori_loop(1, chips, one, 0)


def swap_sent(chips, step, source, target, send_sem, get_sem):
    me = lax.axis_index("fsdp")
    to = (me + step) % chips
    pltpu.make_async_remote_copy(
        src_ref=source.at[to], dst_ref=target.at[me], send_sem=send_sem.at[to],
        recv_sem=get_sem.at[me], device_id=chip(to), device_id_type=MESH_IDS,
    ).wait_send()


def swap_arrived(chips, step, source, target, send_sem, get_sem):
    origin = (lax.axis_index("fsdp") + chips - step) % chips
    pltpu.make_async_remote_copy(
        src_ref=source.at[origin], dst_ref=target.at[origin], send_sem=send_sem.at[origin],
        recv_sem=get_sem.at[origin], device_id=chip(origin), device_id_type=MESH_IDS,
    ).wait_recv()
    return origin


def exchange(layer, values, received, expert_in, expert_out, collective_id):
    images, experts, width = values.shape
    chips = lax.axis_size("fsdp")
    cores = lax.axis_size("dp")
    local, _, hidden = expert_in.shape[1:]
    rows = images * local
    half = chips * images
    every = cores * half
    backward = received is not None

    def kernel(*refs):
        if backward:
            values_ref, received_ref, in_ref, out_ref = refs[:4]
            home_ref, hid_ref, pre_ref, gout_ref, squares_ref = refs[4:9]
            slope_ref = refs[9]
            scratch = refs[10:]
        else:
            values_ref, in_ref, out_ref = refs[:3]
            home_ref, received_ref = refs[3:5]
            scratch = refs[5:]
        win, wout, outbox, inbox, parts, pair_out, pair_in, sorted_ref, backbox, homebox = scratch[:10]
        win_sem, wout_sem, send_one, get_one, pass_send, pass_get, pair_send, pair_get, send_two, get_two = scratch[10:]
        core = lax.axis_index("dp")
        me = lax.axis_index("fsdp")

        def fetch(e):
            return (
                pltpu.make_async_copy(in_ref.at[layer, e], win.at[e], win_sem.at[e]),
                pltpu.make_async_copy(out_ref.at[layer, e], wout.at[e], wout_sem.at[e]),
            )

        def start_fetch(e, carry):
            for copy in fetch(e):
                copy.start()
            return carry

        lax.fori_loop(0, local, start_fetch, 0)
        whole = [values_ref[image].astype(F32) for image in range(images)]
        for at in range(chips):
            outbox[at] = jnp.concatenate(
                [one[at * local : (at + 1) * local] for one in whole], 0
            ).astype(BF16)
        greet_all(chips)
        swap_start(chips, outbox, inbox.at[core], send_one, get_one)
        inbox[core, me] = outbox[me]

        def hand(at):
            block = inbox.at[core, at]
            return pltpu.make_async_remote_copy(
                src_ref=block, dst_ref=block, send_sem=pass_send.at[at],
                recv_sem=pass_get.at[at], device_id=sibling(), device_id_type=MESH_IDS,
            )

        def handed(at):
            block = inbox.at[1 - core, at]
            return pltpu.make_async_remote_copy(
                src_ref=block, dst_ref=block, send_sem=pass_send.at[at],
                recv_sem=pass_get.at[at], device_id=sibling(), device_id_type=MESH_IDS,
            )

        hand(me).start()
        if backward:

            def ahead(e, carry):
                for copy in fetch(e):
                    copy.wait()
                rec = received_ref[e]
                hid, slope = gelu_both(nn(rec, win[e].astype(BF16)))
                slope_ref[e] = slope
                hid_ref[e] = hid.astype(BF16)
                return carry

            lax.fori_loop(0, local, ahead, 0)

        def arrive(step, carry):
            hand(swap_arrived(chips, step, outbox, inbox.at[core], send_one, get_one)).start()
            return carry

        lax.fori_loop(1, chips, arrive, 0)

        def all_handed(at, carry):
            handed(at).wait_recv()
            return carry

        lax.fori_loop(0, chips, all_handed, 0)
        arrived = inbox[...].reshape(every * local, width)
        pick_row = lax.broadcasted_iota(jnp.int32, (every, every * local), 0)
        pick_col = lax.broadcasted_iota(jnp.int32, (every, every * local), 1)
        wanted = pick_row * local - pick_col

        def pair_copy(e):
            return pltpu.make_async_remote_copy(
                src_ref=pair_out.at[e], dst_ref=pair_in.at[e], send_sem=pair_send.at[e],
                recv_sem=pair_get.at[e], device_id=sibling(), device_id_type=MESH_IDS,
            )

        if backward:
            squares_ref[...] = jnp.zeros_like(squares_ref)

        def work(e, carry):
            pick = (wanted == -e).astype(F32).astype(BF16)
            mine = nn(pick, arrived).astype(BF16)
            if backward:
                gout_ref[e] = mine
                grad_pre = (nt(mine, wout[e].astype(BF16)) * slope_ref[e]).astype(BF16)
                pre_ref[e] = grad_pre
                part = nt(grad_pre, win[e].astype(BF16))
                rec, hid = received_ref[e], hid_ref[e]
                product = nt(rec, rec) * nt(grad_pre, grad_pre) + nt(hid, hid) * nt(mine, mine)
                squares_ref[...] += jnp.sum(product.reshape(every // 8, 8, every), 0)
            else:
                for copy in fetch(e):
                    copy.wait()
                received_ref[e] = mine
                hid = gelu(nn(mine, win[e].astype(BF16))).astype(BF16)
                part = nn(hid, wout[e].astype(BF16))
            parts[e] = part.reshape(cores, half, width)
            pair_out[e] = parts[e, 1 - core].astype(BF16)
            pair_copy(e).start()
            return carry

        lax.fori_loop(0, local, work, 0)

        def add(e, carry):
            pair_copy(e).wait_recv()
            sorted_ref[pl.ds(pl.multiple_of(e * half, half), half)] = (
                parts[e, core] + pair_in[e].astype(F32)
            ).astype(BF16)
            return carry

        lax.fori_loop(0, local, add, 0)
        back_row = lax.broadcasted_iota(jnp.int32, (half * local, half * local), 0)
        back_col = lax.broadcasted_iota(jnp.int32, (half * local, half * local), 1)
        back = (back_row == (back_col % half) * local + back_col // half).astype(F32).astype(BF16)
        backbox[...] = nn(back, sorted_ref[...]).astype(BF16).reshape(chips, rows, width)
        swap_start(chips, backbox, homebox, send_two, get_two)
        homebox[me] = backbox[me]

        def home(step, carry):
            swap_arrived(chips, step, backbox, homebox, send_two, get_two)
            return carry

        lax.fori_loop(1, chips, home, 0)
        blocks = [homebox[at].astype(F32) for at in range(chips)]
        for image in range(images):
            home_ref[image] = jnp.concatenate(
                [block[image * local : (image + 1) * local] for block in blocks], 0
            ).astype(BF16)

        def drain(step, carry):
            swap_sent(chips, step, outbox, inbox.at[core], send_one, get_one)
            swap_sent(chips, step, backbox, homebox, send_two, get_two)
            return carry

        lax.fori_loop(1, chips, drain, 0)

        def drain_pass(at, carry):
            hand(at).wait_send()
            return carry

        lax.fori_loop(0, chips, drain_pass, 0)

        def drain_pair(e, carry):
            pair_copy(e).wait_send()
            return carry

        lax.fori_loop(0, local, drain_pair, 0)

    inside = pl.BlockSpec(memory_space=pltpu.VMEM)
    outside = pl.BlockSpec(memory_space=pl.ANY)
    shape = jax.ShapeDtypeStruct
    home_shape = shape((images, experts, width), BF16)
    if backward:
        out_shape = [
            home_shape,
            shape((local, every, hidden), BF16),
            shape((local, every, hidden), BF16),
            shape((local, every, width), BF16),
            shape((8, every), F32),
        ]
        operands = (values, received, expert_in, expert_out)
        in_specs = [inside, inside, outside, outside]
        extra = [pltpu.VMEM((local, every, hidden), F32)]
    else:
        out_shape = [home_shape, shape((local, every, width), BF16)]
        operands = (values, expert_in, expert_out)
        in_specs = [inside, outside, outside]
        extra = []
    dma = pltpu.SemaphoreType.DMA
    return pl.pallas_call(
        kernel,
        in_specs=in_specs,
        out_specs=[inside] * len(out_shape),
        out_shape=out_shape,
        scratch_shapes=extra
        + [
            pltpu.VMEM((local, width, hidden), F32),
            pltpu.VMEM((local, hidden, width), F32),
            pltpu.VMEM((chips, rows, width), BF16),
            pltpu.VMEM((cores, chips, rows, width), BF16),
            pltpu.VMEM((local, cores, half, width), F32),
            pltpu.VMEM((local, half, width), BF16),
            pltpu.VMEM((local, half, width), BF16),
            pltpu.VMEM((local * half, width), BF16),
            pltpu.VMEM((chips, rows, width), BF16),
            pltpu.VMEM((chips, rows, width), BF16),
        ]
        + [dma((local,))] * 2
        + [dma((chips,))] * 4
        + [dma((local,))] * 2
        + [dma((chips,))] * 2,
        compiler_params=pltpu.CompilerParams(
            collective_id=collective_id, has_side_effects=True, vmem_limit_bytes=VMEM_BYTES
        ),
        cost_estimate=work_of(40),
        name="exchange_back" if backward else "exchange",
    )(*operands)


def expert_adam(weight, first, second, lefts, rights, scale, rate):
    layers, local, tall, wide = weight.shape
    deep = lefts[0].shape[1]

    def kernel(scale_ref, w_ref, m_ref, s_ref, *refs):
        left_refs, right_refs = refs[:layers], refs[layers : 2 * layers]
        new_w, new_m, new_s = refs[2 * layers :]

        for layer in range(layers):

            @pl.when(pl.program_id(0) == layer)
            def _(layer=layer):
                grad = tn(left_refs[layer][...], right_refs[layer][...]) * scale_ref[0]
                moment = BETA_ONE * m_ref[...] + (1.0 - BETA_ONE) * grad
                spread_of = BETA_TWO * s_ref[...] + (1.0 - BETA_TWO) * (grad * grad)
                ratio = (moment * (1.0 / (1.0 - BETA_ONE**STEP))) / (
                    jnp.sqrt(spread_of * (1.0 / (1.0 - BETA_TWO**STEP))) + ADAM_EPS
                )
                held = w_ref[...]
                new_m[...] = moment
                new_s[...] = spread_of
                new_w[...] = held - rate * (ratio + WEIGHT_DECAY * held)

    def factor_spec(layer, columns):
        last = local - 1
        return pl.BlockSpec(
            (None, deep, columns),
            lambda l, e: (jnp.where(l == layer, e, jnp.where(l < layer, 0, last)), 0, 0),
        )

    block = pl.BlockSpec((None, None, tall, wide), lambda l, e: (l, e, 0, 0))
    return pl.pallas_call(
        kernel,
        grid=(layers, local),
        in_specs=[pl.BlockSpec(memory_space=pltpu.SMEM)]
        + [block] * 3
        + [factor_spec(layer, tall) for layer in range(layers)]
        + [factor_spec(layer, wide) for layer in range(layers)],
        out_specs=[block] * 3,
        out_shape=[jax.ShapeDtypeStruct(weight.shape, F32)] * 3,
        compiler_params=pltpu.CompilerParams(vmem_limit_bytes=VMEM_BYTES),
        name="expert_adam",
    )(scale, weight, first, second, *lefts, *rights)


def adam(weight, first, second, grad, rate):
    first = BETA_ONE * first + (1.0 - BETA_ONE) * grad
    second = BETA_TWO * second + (1.0 - BETA_TWO) * grad * grad
    ratio = first / (1.0 - BETA_ONE**STEP) / (jnp.sqrt(second / (1.0 - BETA_TWO**STEP)) + ADAM_EPS)
    return (weight - rate * (ratio + WEIGHT_DECAY * weight), first, second)


def on_device(
    patches,
    resolution,
    labels,
    dense_weights,
    attention,
    router,
    expert_in,
    expert_out,
    classifier,
    norm_table,
    dense_weights_first,
    dense_weights_second,
    attention_first,
    attention_second,
    router_first,
    router_second,
    expert_in_first,
    expert_in_second,
    expert_out_first,
    expert_out_second,
    classifier_first,
    classifier_second,
    norm_table_first,
    norm_table_second,
):
    layers = attention.shape[0]
    width = norm_table.shape[1]
    classes = classifier.shape[1]
    devices = lax.axis_size("dp") * lax.axis_size("fsdp")
    images = patches.shape[0] * devices
    interp = interp_matrix()
    position = norm_table[:LEN_LO]
    pos_high = jnp.dot(interp, position, precision=PRECISE)
    pos_low = jnp.pad(position, ((0, LEN - LEN_LO), (0, 0)))
    positions = jnp.stack([pos_low, pos_high])
    gains = [
        jnp.pad(norm_table[LEN_LO + 4 * layer : LEN_LO + 4 * layer + 4], ((0, 4), (0, 0)))
        for layer in range(layers)
    ]
    last_gains = jnp.pad(norm_table[LEN_LO + 4 * layers :], ((0, 6), (0, 0)))
    attention_t = attention.transpose(0, 2, 1).astype(BF16)
    router_t = router.transpose(0, 2, 1).astype(BF16)
    dense_t = dense_weights.T.astype(BF16)
    local = expert_in.shape[1]
    own = (
        lax.axis_size("dp") == 2
        and lax.axis_size("fsdp") == 1 << BITS
        and patches.shape[0] * local % 16 == 0
        and router.shape[1] * router.shape[2] % width == 0
    )
    if own:
        dense, attention_one = gather_all([dense_t, attention_t[0]], 0)
    else:
        dense, attention_one = [
            lax.all_gather(part, ("dp", "fsdp"), axis=0, tiled=True)
            for part in (dense_t, attention_t[0])
        ]
    attention_all = [attention_one]
    router_all = [None]
    fetched = [None]
    for layer in range(1, layers):
        share = attention_t[layer]
        if layer > 1:
            share, attention_all[0] = lax.optimization_barrier((share, attention_all[0]))
        fetched.append(fetch_layer(share, router_t[layer - 1]))

    start, qkv, context, middle, hidden = first_forward(
        resolution, patches, dense, attention_all[0], positions, gains[0], width
    )
    kept = [(start, qkv, context, middle)]
    mixing = None
    for layer in range(1, layers):
        both = fetched[layer]
        if mixing is not None:
            both, last = lax.optimization_barrier((both, mixing[1]))
            mixing = (mixing[0], last)
        one, two = open_layer(both, attention_t.shape[1], router.shape[2], router.shape[1])
        attention_all.append(one)
        router_all.append(two)
        outs = sparse_forward(
            resolution, hidden, mixing, attention_all[layer], router_all[layer], gains[layer]
        )
        if mixing is not None:
            hidden = outs[0]
        qkv, context, middle, combine, slots = outs[-5:]
        if own:
            returned, received = exchange(layer - 1, slots, None, expert_in, expert_out, layer)
        else:
            returned, received = plain_exchange(layer - 1, slots, None, expert_in, expert_out)
        kept.append((hidden, qkv, context, middle, combine, returned, received))
        hidden = middle
        mixing = (combine, returned)

    packs = devices if own else None
    padding = -classes % 128 if not own else -classes % (16 * devices)
    head = jnp.pad(classifier[:width].astype(BF16), ((0, 0), (0, padding)))
    head_bias = jnp.pad(classifier[width:], ((0, 0), (0, padding)), constant_values=NEG_FILL)
    grad_hidden, grad_returned, grad_head, grad_bias, grad_last, loss_part = top(
        resolution, labels, middle, combine, returned, head, head_bias, last_gains, classes, images,
        packs,
    )
    attention_grads = [None] * layers
    router_grads = [None] * (layers - 1)
    gain_grads = [None] * layers
    layer_packs = [None] * layers
    in_factors = [None] * (layers - 1)
    out_factors = [None] * (layers - 1)
    local_squares = 0.0
    for layer in reversed(range(1, layers)):
        before, qkv, context, middle, combine, returned, received = kept[layer]
        if own:
            outs = exchange(
                layer - 1, grad_returned, received, expert_in, expert_out, layers + layer
            )
        else:
            outs = plain_exchange(layer - 1, grad_returned, received, expert_in, expert_out)
        grad_home, hid, grad_pre, grad_out, squares = outs
        local_squares = local_squares + jnp.sum(squares)
        in_factors[layer - 1] = (received, grad_pre)
        out_factors[layer - 1] = (hid, grad_out)
        below = kept[layer - 1][4] if layer > 1 else None
        outs = sparse_backward(
            resolution, before, qkv, context, middle, grad_hidden, returned, grad_home, below,
            attention_all[layer], router_all[layer], gains[layer], packs,
        )
        grad_hidden = outs[0]
        if below is not None:
            grad_returned = outs[1]
        grad_gain = outs[-1]
        if own:
            layer_packs[layer] = outs[-2]
        else:
            attention_grads[layer], router_grads[layer - 1] = outs[-3:-1]
        gain_grads[layer] = grad_gain[:4]
    start, qkv, context, middle = kept[0]
    outs = first_backward(
        resolution, patches, start, qkv, context, middle, grad_hidden, dense, attention_all[0],
        gains[0], packs,
    )
    grad_gain, grad_low, grad_high = outs[-3:]
    if own:
        layer_packs[0] = outs[0]
    else:
        grad_dense, attention_grads[0] = outs[:2]
    gain_grads[0] = grad_gain[:4]
    grad_pos = grad_low[:LEN_LO] + jnp.dot(interp.T, grad_high, precision=PRECISE)
    grad_table = jnp.concatenate([grad_pos] + gain_grads + [grad_last[:2]], 0)
    loss_local = loss_part[0, 0]
    part_rows, part_cols = router.shape[1:]
    table_rows = grad_table.shape[0]
    if own:
        bias_flat = grad_bias[0]
        bias_flat = jnp.pad(bias_flat, (0, -bias_flat.shape[0] % width)).reshape(-1, width)
        tail = jnp.concatenate([grad_table, bias_flat], 0).astype(BF16)
        tail = jnp.pad(tail, ((0, -tail.shape[0] % devices), (0, 0))).reshape(devices, -1, width)
        tail_each = tail.shape[1]
        tail = jnp.pad(tail, ((0, 0), (0, -tail_each % 16), (0, 0)))
        stats = jnp.concatenate(
            [
                jnp.broadcast_to(local_squares, (1, 128)),
                jnp.broadcast_to(loss_local, (1, 128)),
                jnp.zeros((6, 128), F32),
            ],
            0,
        )
        blocks = layer_packs + [grad_head, tail]
        starts = [sum(block.shape[1] for block in blocks[:at]) for at in range(layers)]
        columns = dense.shape[0] // devices
        part = attention_t.shape[1]
        router_at = [starts[layer] + part for layer in range(1, layers)]
        mine, shared, totals = reduce_all(
            blocks, stats, grad_head.shape[1] + tail.shape[1],
            [(at, at + part_cols) for at in router_at], 2 * layers,
        )
        shared = shared.reshape(devices, -1, width)
        head_each = grad_head.shape[1]
        head_all = shared[:, :head_each].reshape(-1, width)[:classes].T.astype(F32)
        tail_all = shared[:, head_each : head_each + tail_each].reshape(-1, width).astype(F32)
        shared_table = tail_all[:table_rows]
        bias_all = tail_all[table_rows:].reshape(-1)[None, :classes]
        shared_head = jnp.concatenate([head_all, bias_all], 0)
        norm = jnp.sqrt(totals[0, 0])
        loss_total = totals[1, 0]
        grad_first = mine[:columns].T
        attention_at = [columns] + starts[1:]
        grad_attention = jnp.stack([mine[at : at + part].T for at in attention_at])
        lane_at = lax.axis_index("dp") * part_rows
        grad_router_all = jnp.stack(
            [
                lax.dynamic_slice_in_dim(mine[at : at + part_cols], lane_at, part_rows, 1).T
                for at in router_at
            ]
        )
    else:
        grad_first = lax.psum_scatter(
            grad_dense, ("dp", "fsdp"), scatter_dimension=0, tiled=True
        ).T
        shares = [
            share_layer(attention_grads[layer], router_grads[layer - 1], part_cols, part_rows)
            for layer in range(1, layers)
        ]
        first_share = lax.psum_scatter(
            attention_grads[0], ("dp", "fsdp"), scatter_dimension=0, tiled=True
        )
        grad_attention = jnp.stack([first_share] + [share[0] for share in shares])
        grad_attention = grad_attention.transpose(0, 2, 1)
        grad_router_all = jnp.stack([share[1] for share in shares]).transpose(0, 2, 1)
        local_squares = (
            local_squares
            + jnp.sum(grad_first * grad_first)
            + jnp.sum(grad_attention * grad_attention)
            + jnp.sum(grad_router_all * grad_router_all)
        )
        grad_head = jnp.concatenate([grad_head[:classes].T, grad_bias[0:1, :classes]], 0)
        shared_head, shared_table, loss_total, squares = lax.psum(
            (grad_head, grad_table, loss_local, local_squares), ("dp", "fsdp")
        )
        norm = jnp.sqrt(
            squares + jnp.sum(shared_head * shared_head) + jnp.sum(shared_table * shared_table)
        )
    scale = jnp.minimum(1.0, CLIP_NORM / norm)
    scale_row = scale.reshape(1)

    def experts_updated(weight, first, second, factors, rate):
        lefts, rights = zip(*factors)
        return tuple(expert_adam(weight, first, second, lefts, rights, scale_row, rate))

    updates = (
        adam(dense_weights, dense_weights_first, dense_weights_second, grad_first * scale, LEARN_RATE),
        adam(attention, attention_first, attention_second, grad_attention * scale, ATTENTION_RATE),
        adam(router, router_first, router_second, grad_router_all * scale, LEARN_RATE),
        experts_updated(expert_in, expert_in_first, expert_in_second, in_factors, EXPERT_RATE),
        experts_updated(expert_out, expert_out_first, expert_out_second, out_factors, LEARN_RATE),
        adam(classifier, classifier_first, classifier_second, shared_head * scale, LEARN_RATE),
        adam(norm_table, norm_table_first, norm_table_second, shared_table * scale, TABLE_RATE),
    )
    return (loss_total, norm) + tuple(part for update in updates for part in update)


def solution(mesh):
    spread = P(("dp", "fsdp"))
    weights = (
        P(None, ("dp", "fsdp")),
        P(None, None, ("dp", "fsdp")),
        P(None, "dp", "fsdp"),
        P(None, "fsdp", None, "dp"),
        P(None, "fsdp", "dp", None),
        P(),
        P(),
    )
    moments = tuple(spec for spec in weights for _ in range(2))
    triples = tuple(spec for spec in weights for _ in range(3))
    return jax.shard_map(
        on_device,
        mesh=mesh,
        in_specs=(spread, spread, spread) + weights + moments,
        out_specs=(P(), P()) + triples,
        check_vma=False,
    )
```

```python
import functools

import jax
import jax.numpy as jnp
from jax import lax
from jax.experimental import pallas as pl
from jax.experimental.pallas import tpu as pltpu
from jax.sharding import PartitionSpec as P

HEADS = 6
FF = 1536
G_LO = 14
G_HI = 24
LEN = 576
LEN_LO = 196
ROWS_LO = 208
STEP = 10


LN_EPS = 1e-06
CLIP_NORM = 0.001
LEARN_RATE = 0.05
ATTENTION_RATE = 0.15
EXPERT_RATE = 1.0
TABLE_RATE = 0.5
BETA_ONE = 0.9
BETA_TWO = 0.95
ADAM_EPS = 1e-10
WEIGHT_DECAY = 0.1
SMOOTH = 0.1
NEG_FILL = -1e30
PRECISE = lax.Precision.HIGHEST
F32 = jnp.float32
BF16 = jnp.bfloat16
VMEM_BYTES = 60 * 1024 * 1024


def interp_matrix():
    rows = jnp.arange(G_HI, dtype=jnp.float32)[:, None]
    cols = jnp.arange(G_LO, dtype=jnp.float32)[None, :]
    weight = jnp.maximum(0.0, 1.0 - jnp.abs(rows * (G_LO - 1) - cols * (G_HI - 1)) / (G_HI - 1))
    return (weight[:, None, :, None] * weight[None, :, None, :]).reshape(G_HI * G_HI, G_LO * G_LO)


def matmul(left, right, form):
    return jnp.einsum(form, left, right, preferred_element_type=jnp.float32)


def contract(left, right, left_dim, right_dim):
    return lax.dot_general(
        left, right, (((left_dim,), (right_dim,)), ((), ())), preferred_element_type=F32
    )


def nn(left, right):
    return contract(left, right, 1, 0)


def nt(left, right):
    return contract(left, right, 1, 1)


def tn(left, right):
    return contract(left, right, 0, 0)


def normalise(values):
    center = values - jnp.mean(values, -1, keepdims=True)
    rate = lax.rsqrt(jnp.mean(center * center, -1, keepdims=True) + LN_EPS)
    return center * rate, rate


def normalise_back(unit, rate, gain, grad):
    scaled = grad * gain
    inner = scaled - jnp.mean(scaled, -1, keepdims=True)
    grad_in = rate * (inner - unit * jnp.mean(scaled * unit, -1, keepdims=True))
    return (
        grad_in,
        jnp.sum(grad * unit, 0, keepdims=True),
        jnp.sum(grad, 0, keepdims=True),
    )


def row_number(shape):
    return lax.broadcasted_iota(jnp.int32, shape, 0)


def side_masks():
    lane = lax.broadcasted_iota(jnp.int32, (1, 128), 1)
    first = (lane < 64).astype(F32)
    return (first.astype(BF16), (1.0 - first).astype(BF16))


def lanes(offset):
    return pl.ds(pl.multiple_of(offset, 128), 128)


GELU_RATE = 0.7978845608028654


def gelu(v):
    return 0.5 * v * (1.0 + jnp.tanh(GELU_RATE * (v + 0.044715 * (v * v * v))))


def gelu_both(v):
    square = v * v
    bend = jnp.tanh(GELU_RATE * (v + 0.044715 * (square * v)))
    half = 0.5 * (1.0 + bend)
    slope = half + 0.5 * v * (1.0 - bend * bend) * (GELU_RATE * (1.0 + 3 * 0.044715 * square))
    return v * half, slope


def attention_rows(rows, limit, qkv, context):
    width = context.shape[1]
    first = lax.broadcasted_iota(jnp.int32, (rows, 128), 1) < 64
    masks = side_masks()
    ones = jnp.ones((rows, 128), BF16)
    for offset in range(0, width, 128):
        query = qkv[:rows, offset : offset + 128] * BF16(0.125)
        keys = qkv[:rows, width + offset : width + offset + 128]
        values = qkv[:rows, 2 * width + offset : 2 * width + offset + 128]
        summing = jnp.concatenate([values, ones], 1)
        found = []
        for side in (0, 1):
            scores = nt(query * masks[side], keys)
            if limit is not None:
                lane = lax.broadcasted_iota(jnp.int32, (rows, rows), 1)
                scores = jnp.where(lane < limit, scores, NEG_FILL)
            raised = jnp.exp(scores - jnp.max(scores, 1, keepdims=True))
            both = nn(raised.astype(BF16), summing)
            found.append(both[:, :128] * (1.0 / both[:, 128:]))
        context[:rows, offset : offset + 128] = jnp.where(first, found[0], found[1]).astype(BF16)


def scores_back(limit, keys, values, query, grad):
    scores = nt(keys, query)
    if limit is not None:
        scores = jnp.where(row_number(scores.shape) < limit, scores, NEG_FILL)
    raised = jnp.exp(scores - jnp.max(scores, 0, keepdims=True))
    probs = raised * (1.0 / jnp.sum(raised, 0, keepdims=True))
    grad_values = nn(probs.astype(BF16), grad)
    grad_probs = nt(values, grad)
    mixed = jnp.sum(probs * grad_probs, 0, keepdims=True)
    grad_scores = (probs * (grad_probs - mixed)).astype(BF16)
    return grad_scores, nn(grad_scores, query), grad_values


def attention_rows_back(rows, limit, qkv, grad_context, grad_qkv):
    width = grad_context.shape[1]
    masks = side_masks()
    first = lax.broadcasted_iota(jnp.int32, (rows, 128), 1) < 64

    def pair(offset):
        query = qkv[:rows, lanes(offset)] * BF16(0.125)
        keys = qkv[:rows, lanes(width + offset)]
        values = qkv[:rows, lanes(2 * width + offset)]
        grad = grad_context[:rows, lanes(offset)]
        queries = [query * mask for mask in masks]
        grads = [grad * mask for mask in masks]
        if limit is None:
            grad_scores, grad_keys, grad_values = scores_back(
                limit, keys, values, jnp.concatenate(queries, 0), jnp.concatenate(grads, 0)
            )
            both = tn(grad_scores, keys)
            grad_query = jnp.where(first, both[:rows], both[rows:])
        else:
            one, two = [
                scores_back(limit, keys, values, queries[side], grads[side]) for side in (0, 1)
            ]
            grad_query = tn(one[0], keys * masks[0]) + tn(two[0], keys * masks[1])
            grad_keys, grad_values = one[1] + two[1], one[2] + two[2]
        grad_qkv[:rows, lanes(offset)] = (grad_query * 0.125).astype(BF16)
        grad_qkv[:rows, lanes(width + offset)] = grad_keys.astype(BF16)
        grad_qkv[:rows, lanes(2 * width + offset)] = grad_values.astype(BF16)

    if limit is None:

        def step(index, carry):
            pair(index * 128)
            return carry

        lax.fori_loop(0, width // 128, step, 0)
    else:
        for offset in range(0, width, 128):
            pair(offset)


def attention_forward(rows, limit, hidden, gains, weights, qkv, context):
    width = hidden.shape[1]
    unit, _ = normalise(hidden)
    normed = (unit * gains[0:1] + gains[1:2]).astype(BF16)
    qkv[:rows] = nt(normed, weights[: 3 * width]).astype(BF16)
    attention_rows(rows, limit, qkv, context)
    return hidden + nn(context[:rows], weights[3 * width :])


def attention_backward(
    rows, limit, hidden, grad_middle, gains, weights, qkv, context, hold_context, hold_qkv,
    grad_weights, grad_gains,
):
    width = hidden.shape[1]
    grad_b = grad_middle.astype(BF16)
    hold_context[:rows] = nt(grad_b, weights[3 * width :]).astype(BF16)
    grad_weights[3 * width :] += tn(context[:rows], grad_b)
    attention_rows_back(rows, limit, qkv, hold_context, hold_qkv)
    unit, rate = normalise(hidden)
    normed = (unit * gains[0:1] + gains[1:2]).astype(BF16)
    grad_weights[: 3 * width] += tn(hold_qkv[:rows], normed)
    grad_normed = nn(hold_qkv[:rows], weights[: 3 * width])
    grad_in, grad_gain, grad_bias = normalise_back(unit, rate, gains[0:1], grad_normed)
    grad_gains[0:1] += grad_gain
    grad_gains[1:2] += grad_bias
    return grad_middle + grad_in


def mlp_forward(rows, middle, gains, weights, pixels):
    unit, _ = normalise(middle)
    normed = (unit * gains[2:3] + gains[3:4]).astype(BF16)
    chunk = middle.shape[1]
    total = middle
    for start in range(0, FF, chunk):
        pre = nt(normed, weights[pixels + start : pixels + start + chunk])
        out = weights[pixels + FF + start : pixels + FF + start + chunk]
        total = total + nn(gelu(pre).astype(BF16), out)
    return total


def mlp_backward(rows, middle, grad, gains, weights, pixels, grad_weights, grad_gains):
    unit, rate = normalise(middle)
    normed = (unit * gains[2:3] + gains[3:4]).astype(BF16)
    grad_b = grad.astype(BF16)
    chunk = middle.shape[1]
    grad_normed = None
    for start in range(0, FF, chunk):
        first = slice(pixels + start, pixels + start + chunk)
        second = slice(pixels + FF + start, pixels + FF + start + chunk)
        hid, slope = gelu_both(nt(normed, weights[first]))
        grad_weights[second] += tn(hid.astype(BF16), grad_b)
        grad_pre = (nt(grad_b, weights[second]) * slope).astype(BF16)
        grad_weights[first] += tn(grad_pre, normed)
        part = nn(grad_pre, weights[first])
        grad_normed = part if grad_normed is None else grad_normed + part
    grad_in, grad_gain, grad_bias = normalise_back(unit, rate, gains[2:3], grad_normed)
    grad_gains[2:3] += grad_gain
    grad_gains[3:4] += grad_bias
    return grad + grad_in


def route(limit, middle, gains, router):
    unit, rate = normalise(middle)
    normed = (unit * gains[2:3] + gains[3:4]).astype(BF16)
    logits = nt(normed, router[...])
    masked = logits
    if limit is not None:
        masked = jnp.where(row_number(logits.shape) < limit, logits, NEG_FILL)
    raised = jnp.exp(masked - jnp.max(masked, 0, keepdims=True))
    dispatch = raised * (1.0 / jnp.sum(raised, 0, keepdims=True))
    raised = jnp.exp(logits - jnp.max(logits, 1, keepdims=True))
    combine = raised * (1.0 / jnp.sum(raised, 1, keepdims=True))
    return unit, rate, normed, dispatch, combine


def masked_rows(limit, values):
    if limit is None:
        return values
    return jnp.where(row_number(values.shape) < limit, values, 0.0)


def work_of(giga):
    return pl.CostEstimate(flops=giga * 10**9, bytes_accessed=1 << 20, transcendentals=0)


def by_image(name, body, scalars, per_image, whole, out_image, out_sum, scratch=(), pack=None):
    images = scalars[0].shape[0]
    inner = pack[0] if pack else 0
    packed = 1 if pack else 0
    counts = (
        len(scalars), len(per_image), len(whole), len(out_image), packed, len(out_sum) - inner,
        inner, len(scratch),
    )

    def kernel(*refs):
        groups, at = [], 0
        for count in counts:
            groups.append(refs[at : at + count])
            at += count
        index = pl.program_id(0)
        sums = tuple(groups[6]) + tuple(groups[5])

        @pl.when(index == 0)
        def _():
            for ref in sums:
                ref[...] = jnp.zeros_like(ref)

        numbers = [ref[index] for ref in groups[0]]
        given = (*groups[1:4], sums, groups[7])

        @pl.when(numbers[0] == 1)
        def _():
            body(LEN, None, numbers, *given)

        @pl.when(numbers[0] != 1)
        def _():
            body(ROWS_LO, LEN_LO + numbers[0], numbers, *given)

        if pack:

            @pl.when(index == images - 1)
            def _():
                def write(device, carry):
                    groups[4][0][device] = pack[3](sums, device).astype(BF16)
                    return carry

                lax.fori_loop(0, pack[1], write, 0)

    width = out_sum[0][1] if pack else 0
    pack_shapes = [(pack[1], pack[2], width)] if pack else []

    def image_spec(shape):
        return pl.BlockSpec((None,) + tuple(shape[1:]), lambda i, *_: (i, 0, 0))

    return pl.pallas_call(
        kernel,
        grid_spec=pltpu.PrefetchScalarGridSpec(
            num_scalar_prefetch=len(scalars),
            grid=(images,),
            in_specs=[image_spec(a.shape) for a in per_image]
            + [pl.BlockSpec(memory_space=pltpu.VMEM) for _ in whole],
            out_specs=[image_spec((images,) + shape) for shape, _ in out_image]
            + [pl.BlockSpec(shape, lambda i, *_: (0, 0, 0)) for shape in pack_shapes]
            + [pl.BlockSpec(shape, lambda i, *_: (0, 0)) for shape in out_sum[inner:]],
            scratch_shapes=[pltpu.VMEM(shape, F32) for shape in out_sum[:inner]] + list(scratch),
        ),
        out_shape=[jax.ShapeDtypeStruct((images,) + shape, dtype) for shape, dtype in out_image]
        + [jax.ShapeDtypeStruct(shape, BF16) for shape in pack_shapes]
        + [jax.ShapeDtypeStruct(shape, F32) for shape in out_sum[inner:]],
        compiler_params=pltpu.CompilerParams(vmem_limit_bytes=VMEM_BYTES),
        cost_estimate=work_of(images * 8),
        name=name,
    )(*scalars, *per_image, *whole)


def rows_of(ref, device, count):
    return ref[pl.ds(pl.multiple_of(device * count, 8), count)]


def padded_rows(blocks):
    rows = sum(block.shape[0] for block in blocks)
    if rows % 16:
        blocks = blocks + [jnp.zeros((-rows % 16, blocks[0].shape[1]), F32)]
    return jnp.concatenate(blocks, 0) if len(blocks) > 1 else blocks[0]


def up_16(count):
    return count + -count % 16


def first_forward(resolution, patches, dense, attention, positions, gains, width):
    pixels = patches.shape[2]

    def body(rows, limit, numbers, images, whole, outs, sums, scratch):
        dense_ref, attention_ref, position_ref, gain_ref = whole
        start, qkv, context, middle, last = outs
        place = position_ref[0 if limit is not None else 1, :rows]
        embedded = masked_rows(limit, nn(images[0][:rows], dense_ref[:pixels]) + place)
        start[:rows] = embedded
        middle_rows = attention_forward(
            rows, limit, embedded, gain_ref, attention_ref, qkv, context
        )
        middle[:rows] = middle_rows
        last[:rows] = mlp_forward(rows, middle_rows, gain_ref, dense_ref, pixels)

    return by_image(
        "first_forward",
        body,
        [resolution],
        [patches],
        [dense, attention, positions, gains],
        [
            ((LEN, width), F32),
            ((LEN, 3 * width), BF16),
            ((LEN, width), BF16),
            ((LEN, width), F32),
            ((LEN, width), F32),
        ],
        [],
    )


def sparse_forward(resolution, hidden, mixing, attention, router, gains):
    width = hidden.shape[2]
    experts = router.shape[0]

    def body(rows, limit, numbers, images, whole, outs, sums, scratch):
        attention_ref, router_ref, gain_ref = whole
        before, qkv, context, middle, combine, slots = ([None] + list(outs))[-6:]
        hidden_rows = images[0][:rows]
        if mixing is not None:
            hidden_rows = hidden_rows + nn(images[1][:rows], images[2][...])
            before[:rows] = hidden_rows
        middle_rows = attention_forward(
            rows, limit, hidden_rows, gain_ref, attention_ref, qkv, context
        )
        middle[:rows] = middle_rows
        _, _, normed, dispatch, share = route(limit, middle_rows, gain_ref, router_ref)
        combine[:rows] = share.astype(BF16)
        slots[...] = tn(dispatch.astype(BF16), normed).astype(BF16)

    outs = [
        ((LEN, 3 * width), BF16),
        ((LEN, width), BF16),
        ((LEN, width), F32),
        ((LEN, experts), BF16),
        ((experts, width), BF16),
    ]
    if mixing is not None:
        outs = [((LEN, width), F32)] + outs
    return by_image(
        "sparse_forward",
        body,
        [resolution],
        [hidden] + list(mixing or ()),
        [attention, router, gains],
        outs,
        [],
    )


def top(resolution, labels, middle, combine, returned, head, head_bias, last_gains, classes, images, devices):
    width = middle.shape[2]
    experts = returned.shape[1]
    padded = head.shape[1]

    def body(rows, limit, numbers, per_image, whole, outs, sums, scratch):
        middle_ref, combine_ref, returned_ref = per_image
        head_ref, bias_ref, gain_ref = whole
        grad_hidden, grad_returned = outs
        grad_head, grad_bias_row, grad_gains, loss = sums
        length = float(LEN if limit is None else LEN_LO)
        share = combine_ref[:rows]
        hidden = middle_ref[:rows] + nn(share, returned_ref[...])
        unit, rate = normalise(hidden)
        normed = masked_rows(limit, unit * gain_ref[0:1] + gain_ref[1:2])
        pooled = jnp.sum(normed, 0, keepdims=True) * (1.0 / length)
        one_row = (row_number((8, width)) == 0).astype(F32)
        pooled_b = (one_row * pooled).astype(BF16)
        logits = nn(pooled_b, head_ref[...])[0:1] + bias_ref[...]
        shifted = logits - jnp.max(logits, 1, keepdims=True)
        raised = jnp.exp(shifted)
        total = jnp.sum(raised, 1, keepdims=True)
        log_probs = shifted - jnp.log(total)
        lane = lax.broadcasted_iota(jnp.int32, (1, padded), 1)
        target = jnp.where(lane == numbers[1], 1.0 - SMOOTH, 0.0) + jnp.where(
            lane < classes, SMOOTH / classes, 0.0
        )
        picked = jnp.sum(target * log_probs, 1, keepdims=True)
        loss[...] += jnp.broadcast_to(picked * (-1.0 / images), loss.shape)
        grad_logits = (raised * (1.0 / total) - target) * (1.0 / images)
        grad_bias_row[0:1] += grad_logits
        row_mask = (row_number((8, padded)) == 0).astype(F32)
        grad_logits_b = (row_mask * grad_logits).astype(BF16)
        grad_head[...] += tn(grad_logits_b, pooled_b)
        grad_pooled = nt(grad_logits_b, head_ref[...])[0:1] * (1.0 / length)
        grad_normed = masked_rows(limit, jnp.broadcast_to(grad_pooled, (rows, width)))
        grad_rows, grad_gain, grad_bias = normalise_back(
            unit, rate, gain_ref[0:1], grad_normed
        )
        grad_gains[0:1] += grad_gain
        grad_gains[1:2] += grad_bias
        grad_hidden[:rows] = grad_rows
        grad_returned[...] = tn(share, grad_rows.astype(BF16)).astype(BF16)

    return by_image(
        "top",
        body,
        [resolution, labels],
        [middle, combine, returned],
        [head, head_bias, last_gains],
        [((LEN, width), F32), ((experts, width), BF16)],
        [(padded, width), (8, padded), (8, width), (8, 128)],
        pack=devices
        and (
            1, devices, padded // devices,
            lambda sums, device: rows_of(sums[0], device, padded // devices),
        ),
    )


def sparse_backward(
    resolution, hidden, qkv, context, middle, grad_hidden, returned, grad_home, below, attention,
    router, gains, devices,
):
    width = middle.shape[2]
    experts = router.shape[0]
    chips = lax.axis_size("fsdp")
    local = experts // chips

    def body(rows, limit, numbers, images, whole, outs, sums, scratch):
        hidden_ref, qkv_ref, context_ref, middle_ref, grad_ref, returned_ref, home_ref = images[:7]
        attention_ref, router_ref, gain_ref = whole
        grad_attention, grad_router, grad_gains = sums
        grad = grad_ref[:rows]
        grad_combine = nt(grad.astype(BF16), returned_ref[...])
        unit, rate, normed, dispatch, share = route(
            limit, middle_ref[:rows], gain_ref, router_ref
        )
        home = home_ref[...]
        grad_dispatch = nt(normed, home)
        grad_normed = nn(dispatch.astype(BF16), home)
        grad_route = dispatch * (
            grad_dispatch - jnp.sum(grad_dispatch * dispatch, 0, keepdims=True)
        ) + share * (grad_combine - jnp.sum(grad_combine * share, 1, keepdims=True))
        grad_route_b = grad_route.astype(BF16)
        grad_router[...] += tn(grad_route_b, normed)
        grad_normed = grad_normed + nn(grad_route_b, router_ref[...])
        grad_in, grad_gain, grad_bias = normalise_back(unit, rate, gain_ref[2:3], grad_normed)
        grad_gains[2:3] += grad_gain
        grad_gains[3:4] += grad_bias
        grad_rows = attention_backward(
            rows, limit, hidden_ref[:rows], grad + grad_in, gain_ref, attention_ref, qkv_ref,
            context_ref, scratch[0], scratch[1], grad_attention, grad_gains,
        )
        outs[0][:rows] = grad_rows
        if below is not None:
            outs[1][...] = tn(images[7][:rows], grad_rows.astype(BF16)).astype(BF16)

    outs = [((LEN, width), F32)]
    if below is not None:
        outs.append(((experts, width), BF16))
    return by_image(
        "sparse_backward",
        body,
        [resolution],
        [hidden, qkv, context, middle, grad_hidden, returned, grad_home]
        + ([] if below is None else [below]),
        [attention, router, gains],
        outs,
        [(4 * width, width), (experts, width), (8, width)],
        [pltpu.VMEM((LEN, width), BF16), pltpu.VMEM((LEN, 3 * width), BF16)],
        pack=devices
        and (
            2, devices, up_16(4 * width // devices + local),
            lambda sums, device: padded_rows(
                [
                    rows_of(sums[0], device, 4 * width // devices),
                    rows_of(sums[1], device % chips, local),
                ]
            ),
        ),
    )


def first_backward(
    resolution, patches, start, qkv, context, middle, grad_hidden, dense, attention, gains, devices
):
    width = middle.shape[2]
    pixels = patches.shape[2]
    columns = dense.shape[0]

    def body(rows, limit, numbers, images, whole, outs, sums, scratch):
        patches_ref, start_ref, qkv_ref, context_ref, middle_ref, grad_ref = images
        dense_ref, attention_ref, gain_ref = whole
        grad_dense, grad_attention, grad_gains, grad_low, grad_high = sums
        grad_middle = mlp_backward(
            rows, middle_ref[:rows], grad_ref[:rows], gain_ref, dense_ref, pixels, grad_dense,
            grad_gains,
        )
        grad_rows = attention_backward(
            rows, limit, start_ref[:rows], grad_middle, gain_ref, attention_ref, qkv_ref,
            context_ref, scratch[0], scratch[1], grad_attention, grad_gains,
        )
        grad_rows = masked_rows(limit, grad_rows)
        grad_dense[:pixels] += tn(patches_ref[:rows], grad_rows.astype(BF16))
        if limit is None:
            grad_high[...] += grad_rows
        else:
            grad_low[...] += grad_rows

    return by_image(
        "first_backward",
        body,
        [resolution],
        [patches, start, qkv, context, middle, grad_hidden],
        [dense, attention, gains],
        [],
        [(columns, width), (4 * width, width), (8, width), (ROWS_LO, width), (LEN, width)],
        [pltpu.VMEM((LEN, width), BF16), pltpu.VMEM((LEN, 3 * width), BF16)],
        pack=devices
        and (
            2, devices, up_16((columns + 4 * width) // devices),
            lambda sums, device: padded_rows(
                [
                    rows_of(sums[0], device, columns // devices),
                    rows_of(sums[1], device, 4 * width // devices),
                ]
            ),
        ),
    )


def to_experts(values):
    return lax.all_to_all(values, "fsdp", split_axis=1, concat_axis=0, tiled=True)


def from_experts(values):
    return lax.all_to_all(values, "fsdp", split_axis=0, concat_axis=1, tiled=True)


def all_rows(values):
    return lax.all_gather(to_experts(values), "dp", axis=0, tiled=True).transpose(1, 0, 2)


def rows_home(part):
    shared = lax.psum_scatter(part.transpose(1, 0, 2), "dp", scatter_dimension=0, tiled=True)
    return from_experts(shared.astype(BF16))


def plain_exchange(layer, values, received, expert_in, expert_out):
    win, wout = expert_in[layer].astype(BF16), expert_out[layer].astype(BF16)
    rows = all_rows(values)
    if received is None:
        hid = gelu(matmul(rows, win, "end,edf->enf")).astype(BF16)
        return rows_home(matmul(hid, wout, "enf,efd->end")), rows
    hid, slope = gelu_both(matmul(received, win, "end,edf->enf"))
    hid = hid.astype(BF16)
    grad_pre = (matmul(rows, wout, "end,efd->enf") * slope).astype(BF16)
    home = rows_home(matmul(grad_pre, win, "enf,edf->end"))

    def gram(values):
        return matmul(values, values, "enk,emk->enm")

    squares = gram(received) * gram(grad_pre) + gram(hid) * gram(rows)
    return home, hid, grad_pre, rows, jnp.sum(squares, (0, 1)).reshape(1, -1)


def fetch_layer(attention_t, router_t):
    width = attention_t.shape[1]
    flat = router_t.reshape(-1)
    pack = jnp.concatenate(
        [attention_t, jnp.pad(flat, (0, -flat.size % width)).reshape(-1, width)], 0
    )
    return lax.all_gather(pack, ("dp", "fsdp"), axis=0)


def open_layer(both, part, part_cols, part_rows):
    width = both.shape[2]
    rows_dp = lax.axis_size("dp")
    cols_fsdp = lax.axis_size("fsdp")
    router = (
        both[:, part:]
        .reshape(rows_dp * cols_fsdp, -1)[:, : part_cols * part_rows]
        .reshape(rows_dp, cols_fsdp, part_cols, part_rows)
        .transpose(1, 2, 0, 3)
        .reshape(cols_fsdp * part_cols, rows_dp * part_rows)
    )
    return both[:, :part].reshape(-1, width), router


def share_layer(grad_attention, grad_router, part_cols, part_rows):
    rows_dp = lax.axis_size("dp")
    cols_fsdp = lax.axis_size("fsdp")
    devices = rows_dp * cols_fsdp
    width = grad_attention.shape[1]
    router = (
        grad_router.reshape(cols_fsdp, part_cols, rows_dp, part_rows)
        .transpose(2, 0, 1, 3)
        .reshape(devices, -1)
    )
    router = jnp.pad(router, ((0, 0), (0, -part_cols * part_rows % width)))
    router = router.reshape(devices, -1, width)
    pack = jnp.concatenate([grad_attention.reshape(devices, -1, width), router], 1)
    mine = lax.psum_scatter(pack, ("dp", "fsdp"), scatter_dimension=0, tiled=False)
    part = grad_attention.shape[0] // devices
    return mine[:part], mine[part:].reshape(-1)[: part_cols * part_rows].reshape(part_cols, part_rows)


BITS = 4
GATHER_ORDERS = ((3, 2, 0, 1), (0, 1, 2, 3), (0, 1, 3, 2))
MESH_IDS = pl.DeviceIdType.MESH


def my_bits():
    at = lax.axis_index("fsdp")
    return [(at // (1 << (BITS - 1 - bit))) % 2 for bit in range(BITS)]


def partner_of(bit):
    at = lax.axis_index("fsdp")
    step = 1 << (BITS - 1 - bit)
    return (lax.axis_index("dp"), at + step * (1 - 2 * ((at // step) % 2)))


def sibling():
    return (1 - lax.axis_index("dp"), lax.axis_index("fsdp"))


def greet_partners():
    barrier = pltpu.get_barrier_semaphore()
    others = [partner_of(bit) for bit in range(BITS)] + [sibling()]
    for other in others:
        pl.semaphore_signal(barrier, inc=1, device_id=other, device_id_type=MESH_IDS)
    pl.semaphore_wait(barrier, len(others))


def send(source, target, send_sem, recv_sem, device):
    copy = pltpu.make_async_remote_copy(
        src_ref=source,
        dst_ref=target,
        send_sem=send_sem,
        recv_sem=recv_sem,
        device_id=device,
        device_id_type=MESH_IDS,
    )
    copy.start()
    return copy


def spread(parts, sems):
    mine = my_bits()
    core = lax.axis_index("dp")
    to_send, to_get, pass_send, pass_get = sems

    def view(part, stage, other):
        ref, lane_part, order = part
        index = []
        for bit in range(BITS):
            if bit in order[:stage]:
                index.append(slice(None))
            elif other and bit == order[stage]:
                index.append(1 - mine[bit])
            else:
                index.append(mine[bit])
        return ref.at[(core, *index, slice(None), lane_part)]

    def go(number, stage):
        block = view(parts[number], stage, False)
        return send(
            block, block, to_send.at[number, stage], to_get.at[number, stage],
            partner_of(parts[number][2][stage]),
        )

    def hand_over(number, slot, block):
        return send(block, block, pass_send.at[number, slot], pass_get.at[number, slot], sibling())

    going = [go(number, 0) for number in range(len(parts))]
    handed = [
        hand_over(number, BITS, view(parts[number], 0, False)) for number in range(len(parts))
    ]
    for stage in range(BITS):
        for number in range(len(parts)):
            going[number].wait()
            if stage + 1 < BITS:
                going[number] = go(number, stage + 1)
            handed.append(hand_over(number, stage, view(parts[number], stage, True)))
    for copy in handed:
        copy.wait()


def spread_sems(count):
    return [pltpu.SemaphoreType.DMA((count, BITS + 1)) for _ in range(4)]


def lane_parts(width):
    return [slice(start, start + 128) for start in range(0, width, 128)]


def gather_all(shards, collective_id):
    count = len(shards)
    width = shards[0].shape[1]
    cuts = lane_parts(width)

    def kernel(*refs):
        ins, outs, sems = refs[:count], refs[count : 2 * count], refs[2 * count :]
        place = (lax.axis_index("dp"), *my_bits())
        for ref, out in zip(ins, outs):
            out[place] = ref[...]
        greet_partners()
        spread(
            [
                (out, cut, GATHER_ORDERS[number % 3])
                for number, cut in enumerate(cuts)
                for out in outs
            ],
            sems,
        )

    outs = pl.pallas_call(
        kernel,
        in_specs=[pl.BlockSpec(memory_space=pltpu.VMEM)] * count,
        out_specs=[pl.BlockSpec(memory_space=pltpu.VMEM)] * count,
        out_shape=[jax.ShapeDtypeStruct((2,) * (BITS + 1) + s.shape, s.dtype) for s in shards],
        scratch_shapes=spread_sems(count * len(cuts)),
        compiler_params=pltpu.CompilerParams(
            collective_id=collective_id, has_side_effects=True, vmem_limit_bytes=VMEM_BYTES
        ),
        cost_estimate=work_of(40),
        name="gather_all",
    )(*shards)
    return [out.reshape(-1, width) for out in outs]


def reduce_all(grads, stats, shared, halved, collective_id):
    width = grads[0].shape[2]
    count = len(grads)
    starts = [sum(grad.shape[1] for grad in grads[:at]) for at in range(count + 1)]
    rows = starts[-1]
    cuts = lane_parts(width)
    parts = len(cuts)
    orders = [tuple(reversed(GATHER_ORDERS[number % 3])) for number in range(parts)]

    def kernel(*refs):
        grads_refs = refs[:count]
        stats_ref, mine_ref, shared_ref, total_ref = refs[count : count + 4]
        scratch = refs[count + 4 :]
        sums, first_get = scratch[:2]
        gets = scratch[2 : 2 + BITS]
        stats_all = scratch[2 + BITS]
        local_sem, pair_send, pair_get, to_send, to_get = scratch[3 + BITS : 8 + BITS]
        sems = scratch[8 + BITS :]
        core = lax.axis_index("dp")
        bits = my_bits()
        places = [
            (number, at, cut, slice(starts[at], starts[at + 1]))
            for number, cut in enumerate(cuts)
            for at in range(count)
        ]
        local = {
            (number, at): pltpu.make_async_copy(
                grads_refs[at].at[core, :, :, :, :, :, cut],
                sums.at[:, :, :, :, span, cut],
                local_sem.at[number, at],
            )
            for number, at, cut, span in places
        }
        for copy in local.values():
            copy.start()
        greet_partners()
        pairs = {
            (number, at): send(
                grads_refs[at].at[1 - core, :, :, :, :, :, cut],
                first_get.at[:, :, :, :, span, cut],
                pair_send.at[number, at],
                pair_get.at[number, at],
                sibling(),
            )
            for number, at, cut, span in places
        }

        def index(number, stage, own):
            order = orders[number]
            found = []
            for bit in range(BITS):
                if bit in order[:stage]:
                    found.append(bits[bit])
                elif bit == order[stage]:
                    found.append(bits[bit] if own else 1 - bits[bit])
                else:
                    found.append(slice(None))
            return (*found, slice(None), cuts[number])

        def go(number, stage):
            return send(
                sums.at[index(number, stage, False)],
                gets[stage].at[number],
                to_send.at[number, stage],
                to_get.at[number, stage],
                partner_of(orders[number][stage]),
            )

        going = [None] * parts
        turns = [number for number in range(parts) if number % 3] + list(range(0, parts, 3))
        for number in reversed(turns):
            for at in range(count):
                local[number, at].wait()
                pairs[number, at].wait()
            whole = (slice(None),) * (BITS + 1) + (cuts[number],)
            sums[whole] = sums[whole] + first_get[whole]
            going[number] = go(number, 0)
        place = tuple(bits)
        for stage in range(BITS):
            for number in turns:
                going[number].wait()
                if stage + 1 < BITS:
                    at = index(number, stage, True)
                    sums[at] = sums[at] + gets[stage][number]
                    going[number] = go(number, stage + 1)
                else:
                    at = index(number, stage, True)
                    mine_ref[:, cuts[number]] = sums[at].astype(F32) + gets[stage][number].astype(F32)
        mine = mine_ref[...]
        row = row_number((rows, width))
        counted = mine * mine
        for low, high in halved:
            counted = jnp.where((row >= low) & (row < high), 0.5 * counted, counted)
        squares = jnp.sum(jnp.sum(counted, 0, keepdims=True), 1, keepdims=True)
        top_row = (row_number((8, 128)) == 0).astype(F32)
        stats_all[(core, *place)] = stats_ref[...] + top_row * squares
        shared_ref[(core, *place)] = mine_ref[rows - shared :, :].astype(BF16)
        spread(
            [
                (shared_ref, cut, GATHER_ORDERS[number % 3]) for number, cut in enumerate(cuts)
            ]
            + [(stats_all, slice(0, 128), GATHER_ORDERS[1])],
            sems,
        )
        total_ref[...] = jnp.sum(stats_all[...].reshape(32, 8, 128), 0)

    grid = (2,) * BITS
    return pl.pallas_call(
        kernel,
        in_specs=[pl.BlockSpec(memory_space=pl.ANY)] * count
        + [pl.BlockSpec(memory_space=pltpu.VMEM)],
        out_specs=[pl.BlockSpec(memory_space=pltpu.VMEM)] * 3,
        out_shape=[
            jax.ShapeDtypeStruct((rows, width), F32),
            jax.ShapeDtypeStruct((2,) + grid + (shared, width), BF16),
            jax.ShapeDtypeStruct((8, 128), F32),
        ],
        scratch_shapes=[pltpu.VMEM(grid + (rows, width), BF16)] * 2
        + [pltpu.VMEM((parts,) + (2,) * (BITS - 1 - stage) + (rows, 128), BF16) for stage in range(BITS)]
        + [pltpu.VMEM((2,) + grid + (8, 128), F32)]
        + [pltpu.SemaphoreType.DMA((parts, count))] * 3
        + [pltpu.SemaphoreType.DMA((parts, BITS))] * 2
        + spread_sems(parts + 1),
        compiler_params=pltpu.CompilerParams(
            collective_id=collective_id, has_side_effects=True, vmem_limit_bytes=VMEM_BYTES
        ),
        cost_estimate=work_of(60),
        name="reduce_all",
    )(*[grad.reshape((2,) + grid + grad.shape[1:]) for grad in grads], stats)


def chip(at):
    return (lax.axis_index("dp"), at)


def greet_all(chips):
    barrier = pltpu.get_barrier_semaphore()
    me = lax.axis_index("fsdp")

    def one(step, carry):
        pl.semaphore_signal(
            barrier, inc=1, device_id=chip((me + step) % chips), device_id_type=MESH_IDS
        )
        return carry

    lax.fori_loop(1, chips, one, 0)
    pl.semaphore_signal(barrier, inc=1, device_id=sibling(), device_id_type=MESH_IDS)
    pl.semaphore_wait(barrier, chips)


def swap_start(chips, source, target, send_sem, get_sem):
    me = lax.axis_index("fsdp")

    def one(step, carry):
        other = (me + step) % chips
        send(source.at[other], target.at[me], send_sem.at[other], get_sem.at[me], chip(other))
        return carry

    lax.fori_loop(1, chips, one, 0)


def swap_sent(chips, step, source, target, send_sem, get_sem):
    me = lax.axis_index("fsdp")
    to = (me + step) % chips
    pltpu.make_async_remote_copy(
        src_ref=source.at[to], dst_ref=target.at[me], send_sem=send_sem.at[to],
        recv_sem=get_sem.at[me], device_id=chip(to), device_id_type=MESH_IDS,
    ).wait_send()


def swap_arrived(chips, step, source, target, send_sem, get_sem):
    origin = (lax.axis_index("fsdp") + chips - step) % chips
    pltpu.make_async_remote_copy(
        src_ref=source.at[origin], dst_ref=target.at[origin], send_sem=send_sem.at[origin],
        recv_sem=get_sem.at[origin], device_id=chip(origin), device_id_type=MESH_IDS,
    ).wait_recv()
    return origin


def exchange(layer, values, received, expert_in, expert_out, collective_id):
    images, experts, width = values.shape
    chips = lax.axis_size("fsdp")
    cores = lax.axis_size("dp")
    local, _, hidden = expert_in.shape[1:]
    rows = images * local
    half = chips * images
    every = cores * half
    backward = received is not None

    def kernel(*refs):
        if backward:
            values_ref, received_ref, in_ref, out_ref = refs[:4]
            home_ref, hid_ref, pre_ref, gout_ref, squares_ref = refs[4:9]
            slope_ref = refs[9]
            scratch = refs[10:]
        else:
            values_ref, in_ref, out_ref = refs[:3]
            home_ref, received_ref = refs[3:5]
            scratch = refs[5:]
        win, wout, outbox, inbox, parts, pair_out, pair_in, sorted_ref, backbox, homebox = scratch[:10]
        win_sem, wout_sem, send_one, get_one, pass_send, pass_get, pair_send, pair_get, send_two, get_two = scratch[10:]
        core = lax.axis_index("dp")
        me = lax.axis_index("fsdp")

        def fetch(e):
            return (
                pltpu.make_async_copy(in_ref.at[layer, e], win.at[e], win_sem.at[e]),
                pltpu.make_async_copy(out_ref.at[layer, e], wout.at[e], wout_sem.at[e]),
            )

        def start_fetch(e, carry):
            for copy in fetch(e):
                copy.start()
            return carry

        lax.fori_loop(0, local, start_fetch, 0)
        whole = [values_ref[image].astype(F32) for image in range(images)]
        for at in range(chips):
            outbox[at] = jnp.concatenate(
                [one[at * local : (at + 1) * local] for one in whole], 0
            ).astype(BF16)
        greet_all(chips)
        swap_start(chips, outbox, inbox.at[core], send_one, get_one)
        inbox[core, me] = outbox[me]

        def hand(at):
            block = inbox.at[core, at]
            return pltpu.make_async_remote_copy(
                src_ref=block, dst_ref=block, send_sem=pass_send.at[at],
                recv_sem=pass_get.at[at], device_id=sibling(), device_id_type=MESH_IDS,
            )

        def handed(at):
            block = inbox.at[1 - core, at]
            return pltpu.make_async_remote_copy(
                src_ref=block, dst_ref=block, send_sem=pass_send.at[at],
                recv_sem=pass_get.at[at], device_id=sibling(), device_id_type=MESH_IDS,
            )

        hand(me).start()
        if backward:

            def ahead(e, carry):
                for copy in fetch(e):
                    copy.wait()
                rec = received_ref[e]
                hid, slope = gelu_both(nn(rec, win[e].astype(BF16)))
                slope_ref[e] = slope
                hid_ref[e] = hid.astype(BF16)
                return carry

            lax.fori_loop(0, local, ahead, 0)

        def arrive(step, carry):
            hand(swap_arrived(chips, step, outbox, inbox.at[core], send_one, get_one)).start()
            return carry

        lax.fori_loop(1, chips, arrive, 0)

        def all_handed(at, carry):
            handed(at).wait_recv()
            return carry

        lax.fori_loop(0, chips, all_handed, 0)
        arrived = inbox[...].reshape(every * local, width)
        pick_row = lax.broadcasted_iota(jnp.int32, (every, every * local), 0)
        pick_col = lax.broadcasted_iota(jnp.int32, (every, every * local), 1)
        wanted = pick_row * local - pick_col

        def pair_copy(e):
            return pltpu.make_async_remote_copy(
                src_ref=pair_out.at[e], dst_ref=pair_in.at[e], send_sem=pair_send.at[e],
                recv_sem=pair_get.at[e], device_id=sibling(), device_id_type=MESH_IDS,
            )

        if backward:
            squares_ref[...] = jnp.zeros_like(squares_ref)

        def work(e, carry):
            pick = (wanted == -e).astype(F32).astype(BF16)
            mine = nn(pick, arrived).astype(BF16)
            if backward:
                gout_ref[e] = mine
                grad_pre = (nt(mine, wout[e].astype(BF16)) * slope_ref[e]).astype(BF16)
                pre_ref[e] = grad_pre
                part = nt(grad_pre, win[e].astype(BF16))
                rec, hid = received_ref[e], hid_ref[e]
                product = nt(rec, rec) * nt(grad_pre, grad_pre) + nt(hid, hid) * nt(mine, mine)
                squares_ref[...] += jnp.sum(product.reshape(every // 8, 8, every), 0)
            else:
                for copy in fetch(e):
                    copy.wait()
                received_ref[e] = mine
                hid = gelu(nn(mine, win[e].astype(BF16))).astype(BF16)
                part = nn(hid, wout[e].astype(BF16))
            parts[e] = part.reshape(cores, half, width)
            pair_out[e] = parts[e, 1 - core].astype(BF16)
            pair_copy(e).start()
            return carry

        lax.fori_loop(0, local, work, 0)

        def add(e, carry):
            pair_copy(e).wait_recv()
            sorted_ref[pl.ds(pl.multiple_of(e * half, half), half)] = (
                parts[e, core] + pair_in[e].astype(F32)
            ).astype(BF16)
            return carry

        lax.fori_loop(0, local, add, 0)
        back_row = lax.broadcasted_iota(jnp.int32, (half * local, half * local), 0)
        back_col = lax.broadcasted_iota(jnp.int32, (half * local, half * local), 1)
        back = (back_row == (back_col % half) * local + back_col // half).astype(F32).astype(BF16)
        backbox[...] = nn(back, sorted_ref[...]).astype(BF16).reshape(chips, rows, width)
        swap_start(chips, backbox, homebox, send_two, get_two)
        homebox[me] = backbox[me]

        def home(step, carry):
            swap_arrived(chips, step, backbox, homebox, send_two, get_two)
            return carry

        lax.fori_loop(1, chips, home, 0)
        blocks = [homebox[at].astype(F32) for at in range(chips)]
        for image in range(images):
            home_ref[image] = jnp.concatenate(
                [block[image * local : (image + 1) * local] for block in blocks], 0
            ).astype(BF16)

        def drain(step, carry):
            swap_sent(chips, step, outbox, inbox.at[core], send_one, get_one)
            swap_sent(chips, step, backbox, homebox, send_two, get_two)
            return carry

        lax.fori_loop(1, chips, drain, 0)

        def drain_pass(at, carry):
            hand(at).wait_send()
            return carry

        lax.fori_loop(0, chips, drain_pass, 0)

        def drain_pair(e, carry):
            pair_copy(e).wait_send()
            return carry

        lax.fori_loop(0, local, drain_pair, 0)

    inside = pl.BlockSpec(memory_space=pltpu.VMEM)
    outside = pl.BlockSpec(memory_space=pl.ANY)
    shape = jax.ShapeDtypeStruct
    home_shape = shape((images, experts, width), BF16)
    if backward:
        out_shape = [
            home_shape,
            shape((local, every, hidden), BF16),
            shape((local, every, hidden), BF16),
            shape((local, every, width), BF16),
            shape((8, every), F32),
        ]
        operands = (values, received, expert_in, expert_out)
        in_specs = [inside, inside, outside, outside]
        extra = [pltpu.VMEM((local, every, hidden), F32)]
    else:
        out_shape = [home_shape, shape((local, every, width), BF16)]
        operands = (values, expert_in, expert_out)
        in_specs = [inside, outside, outside]
        extra = []
    dma = pltpu.SemaphoreType.DMA
    return pl.pallas_call(
        kernel,
        in_specs=in_specs,
        out_specs=[inside] * len(out_shape),
        out_shape=out_shape,
        scratch_shapes=extra
        + [
            pltpu.VMEM((local, width, hidden), F32),
            pltpu.VMEM((local, hidden, width), F32),
            pltpu.VMEM((chips, rows, width), BF16),
            pltpu.VMEM((cores, chips, rows, width), BF16),
            pltpu.VMEM((local, cores, half, width), F32),
            pltpu.VMEM((local, half, width), BF16),
            pltpu.VMEM((local, half, width), BF16),
            pltpu.VMEM((local * half, width), BF16),
            pltpu.VMEM((chips, rows, width), BF16),
            pltpu.VMEM((chips, rows, width), BF16),
        ]
        + [dma((local,))] * 2
        + [dma((chips,))] * 4
        + [dma((local,))] * 2
        + [dma((chips,))] * 2,
        compiler_params=pltpu.CompilerParams(
            collective_id=collective_id, has_side_effects=True, vmem_limit_bytes=VMEM_BYTES
        ),
        cost_estimate=work_of(40),
        name="exchange_back" if backward else "exchange",
    )(*operands)


def expert_adam(weight, first, second, lefts, rights, scale, rate):
    layers, local, tall, wide = weight.shape
    deep = lefts[0].shape[1]
    each = 2 if local % 2 == 0 else 1

    def kernel(scale_ref, w_ref, m_ref, s_ref, *refs):
        left_refs, right_refs = refs[:layers], refs[layers : 2 * layers]
        new_w, new_m, new_s = refs[2 * layers :]

        for layer in range(layers):

            @pl.when(pl.program_id(0) == layer)
            def _(layer=layer):
                for e in range(each):
                    grad = tn(left_refs[layer][e], right_refs[layer][e]) * scale_ref[0]
                    moment = BETA_ONE * m_ref[e] + (1.0 - BETA_ONE) * grad
                    spread_of = BETA_TWO * s_ref[e] + (1.0 - BETA_TWO) * (grad * grad)
                    ratio = (moment * (1.0 / (1.0 - BETA_ONE**STEP))) / (
                        jnp.sqrt(spread_of * (1.0 / (1.0 - BETA_TWO**STEP))) + ADAM_EPS
                    )
                    held = w_ref[e]
                    new_m[e] = moment
                    new_s[e] = spread_of
                    new_w[e] = held - rate * (ratio + WEIGHT_DECAY * held)

    def factor_spec(layer, columns):
        last = local // each - 1
        return pl.BlockSpec(
            (each, deep, columns),
            lambda l, e: (jnp.where(l == layer, e, jnp.where(l < layer, 0, last)), 0, 0),
        )

    block = pl.BlockSpec((None, each, tall, wide), lambda l, e: (l, e, 0, 0))
    return pl.pallas_call(
        kernel,
        grid=(layers, local // each),
        in_specs=[pl.BlockSpec(memory_space=pltpu.SMEM)]
        + [block] * 3
        + [factor_spec(layer, tall) for layer in range(layers)]
        + [factor_spec(layer, wide) for layer in range(layers)],
        out_specs=[block] * 3,
        out_shape=[jax.ShapeDtypeStruct(weight.shape, F32)] * 3,
        compiler_params=pltpu.CompilerParams(vmem_limit_bytes=VMEM_BYTES),
        name="expert_adam",
    )(scale, weight, first, second, *lefts, *rights)


def adam(weight, first, second, grad, rate):
    first = BETA_ONE * first + (1.0 - BETA_ONE) * grad
    second = BETA_TWO * second + (1.0 - BETA_TWO) * grad * grad
    ratio = first / (1.0 - BETA_ONE**STEP) / (jnp.sqrt(second / (1.0 - BETA_TWO**STEP)) + ADAM_EPS)
    return (weight - rate * (ratio + WEIGHT_DECAY * weight), first, second)


def on_device(
    patches,
    resolution,
    labels,
    dense_weights,
    attention,
    router,
    expert_in,
    expert_out,
    classifier,
    norm_table,
    dense_weights_first,
    dense_weights_second,
    attention_first,
    attention_second,
    router_first,
    router_second,
    expert_in_first,
    expert_in_second,
    expert_out_first,
    expert_out_second,
    classifier_first,
    classifier_second,
    norm_table_first,
    norm_table_second,
):
    layers = attention.shape[0]
    width = norm_table.shape[1]
    classes = classifier.shape[1]
    devices = lax.axis_size("dp") * lax.axis_size("fsdp")
    images = patches.shape[0] * devices
    interp = interp_matrix()
    position = norm_table[:LEN_LO]
    pos_high = jnp.dot(interp, position, precision=PRECISE)
    pos_low = jnp.pad(position, ((0, LEN - LEN_LO), (0, 0)))
    positions = jnp.stack([pos_low, pos_high])
    gains = [
        jnp.pad(norm_table[LEN_LO + 4 * layer : LEN_LO + 4 * layer + 4], ((0, 4), (0, 0)))
        for layer in range(layers)
    ]
    last_gains = jnp.pad(norm_table[LEN_LO + 4 * layers :], ((0, 6), (0, 0)))
    attention_t = attention.transpose(0, 2, 1).astype(BF16)
    router_t = router.transpose(0, 2, 1).astype(BF16)
    dense_t = dense_weights.T.astype(BF16)
    local = expert_in.shape[1]
    own = (
        lax.axis_size("dp") == 2
        and lax.axis_size("fsdp") == 1 << BITS
        and patches.shape[0] * local % 16 == 0
        and router.shape[1] * router.shape[2] % width == 0
    )
    if own:
        dense, attention_one = gather_all([dense_t, attention_t[0]], 0)
    else:
        dense, attention_one = [
            lax.all_gather(part, ("dp", "fsdp"), axis=0, tiled=True)
            for part in (dense_t, attention_t[0])
        ]
    attention_all = [attention_one]
    router_all = [None]
    fetched = [None]
    for layer in range(1, layers):
        share = attention_t[layer]
        if layer > 1:
            share, attention_all[0] = lax.optimization_barrier((share, attention_all[0]))
        fetched.append(fetch_layer(share, router_t[layer - 1]))

    start, qkv, context, middle, hidden = first_forward(
        resolution, patches, dense, attention_all[0], positions, gains[0], width
    )
    kept = [(start, qkv, context, middle)]
    mixing = None
    for layer in range(1, layers):
        both = fetched[layer]
        if mixing is not None:
            both, last = lax.optimization_barrier((both, mixing[1]))
            mixing = (mixing[0], last)
        one, two = open_layer(both, attention_t.shape[1], router.shape[2], router.shape[1])
        attention_all.append(one)
        router_all.append(two)
        outs = sparse_forward(
            resolution, hidden, mixing, attention_all[layer], router_all[layer], gains[layer]
        )
        if mixing is not None:
            hidden = outs[0]
        qkv, context, middle, combine, slots = outs[-5:]
        if own:
            returned, received = exchange(layer - 1, slots, None, expert_in, expert_out, layer)
        else:
            returned, received = plain_exchange(layer - 1, slots, None, expert_in, expert_out)
        kept.append((hidden, qkv, context, middle, combine, returned, received))
        hidden = middle
        mixing = (combine, returned)

    packs = devices if own else None
    padding = -classes % 128 if not own else -classes % (16 * devices)
    head = jnp.pad(classifier[:width].astype(BF16), ((0, 0), (0, padding)))
    head_bias = jnp.pad(classifier[width:], ((0, 0), (0, padding)), constant_values=NEG_FILL)
    grad_hidden, grad_returned, grad_head, grad_bias, grad_last, loss_part = top(
        resolution, labels, middle, combine, returned, head, head_bias, last_gains, classes, images,
        packs,
    )
    attention_grads = [None] * layers
    router_grads = [None] * (layers - 1)
    gain_grads = [None] * layers
    layer_packs = [None] * layers
    in_factors = [None] * (layers - 1)
    out_factors = [None] * (layers - 1)
    local_squares = 0.0
    for layer in reversed(range(1, layers)):
        before, qkv, context, middle, combine, returned, received = kept[layer]
        if own:
            outs = exchange(
                layer - 1, grad_returned, received, expert_in, expert_out, layers + layer
            )
        else:
            outs = plain_exchange(layer - 1, grad_returned, received, expert_in, expert_out)
        grad_home, hid, grad_pre, grad_out, squares = outs
        local_squares = local_squares + jnp.sum(squares)
        in_factors[layer - 1] = (received, grad_pre)
        out_factors[layer - 1] = (hid, grad_out)
        below = kept[layer - 1][4] if layer > 1 else None
        outs = sparse_backward(
            resolution, before, qkv, context, middle, grad_hidden, returned, grad_home, below,
            attention_all[layer], router_all[layer], gains[layer], packs,
        )
        grad_hidden = outs[0]
        if below is not None:
            grad_returned = outs[1]
        grad_gain = outs[-1]
        if own:
            layer_packs[layer] = outs[-2]
        else:
            attention_grads[layer], router_grads[layer - 1] = outs[-3:-1]
        gain_grads[layer] = grad_gain[:4]
    start, qkv, context, middle = kept[0]
    outs = first_backward(
        resolution, patches, start, qkv, context, middle, grad_hidden, dense, attention_all[0],
        gains[0], packs,
    )
    grad_gain, grad_low, grad_high = outs[-3:]
    if own:
        layer_packs[0] = outs[0]
    else:
        grad_dense, attention_grads[0] = outs[:2]
    gain_grads[0] = grad_gain[:4]
    grad_pos = grad_low[:LEN_LO] + jnp.dot(interp.T, grad_high, precision=PRECISE)
    grad_table = jnp.concatenate([grad_pos] + gain_grads + [grad_last[:2]], 0)
    loss_local = loss_part[0, 0]
    part_rows, part_cols = router.shape[1:]
    table_rows = grad_table.shape[0]
    if own:
        bias_flat = grad_bias[0]
        bias_flat = jnp.pad(bias_flat, (0, -bias_flat.shape[0] % width)).reshape(-1, width)
        tail = jnp.concatenate([grad_table, bias_flat], 0).astype(BF16)
        tail = jnp.pad(tail, ((0, -tail.shape[0] % devices), (0, 0))).reshape(devices, -1, width)
        tail_each = tail.shape[1]
        tail = jnp.pad(tail, ((0, 0), (0, -tail_each % 16), (0, 0)))
        stats = jnp.concatenate(
            [
                jnp.broadcast_to(local_squares, (1, 128)),
                jnp.broadcast_to(loss_local, (1, 128)),
                jnp.zeros((6, 128), F32),
            ],
            0,
        )
        blocks = layer_packs + [grad_head, tail]
        starts = [sum(block.shape[1] for block in blocks[:at]) for at in range(layers)]
        columns = dense.shape[0] // devices
        part = attention_t.shape[1]
        router_at = [starts[layer] + part for layer in range(1, layers)]
        mine, shared, totals = reduce_all(
            blocks, stats, grad_head.shape[1] + tail.shape[1],
            [(at, at + part_cols) for at in router_at], 2 * layers,
        )
        shared = shared.reshape(devices, -1, width)
        head_each = grad_head.shape[1]
        head_all = shared[:, :head_each].reshape(-1, width)[:classes].T.astype(F32)
        tail_all = shared[:, head_each : head_each + tail_each].reshape(-1, width).astype(F32)
        shared_table = tail_all[:table_rows]
        bias_all = tail_all[table_rows:].reshape(-1)[None, :classes]
        shared_head = jnp.concatenate([head_all, bias_all], 0)
        norm = jnp.sqrt(totals[0, 0])
        loss_total = totals[1, 0]
        grad_first = mine[:columns].T
        attention_at = [columns] + starts[1:]
        grad_attention = jnp.stack([mine[at : at + part].T for at in attention_at])
        lane_at = lax.axis_index("dp") * part_rows
        grad_router_all = jnp.stack(
            [
                lax.dynamic_slice_in_dim(mine[at : at + part_cols], lane_at, part_rows, 1).T
                for at in router_at
            ]
        )
    else:
        grad_first = lax.psum_scatter(
            grad_dense, ("dp", "fsdp"), scatter_dimension=0, tiled=True
        ).T
        shares = [
            share_layer(attention_grads[layer], router_grads[layer - 1], part_cols, part_rows)
            for layer in range(1, layers)
        ]
        first_share = lax.psum_scatter(
            attention_grads[0], ("dp", "fsdp"), scatter_dimension=0, tiled=True
        )
        grad_attention = jnp.stack([first_share] + [share[0] for share in shares])
        grad_attention = grad_attention.transpose(0, 2, 1)
        grad_router_all = jnp.stack([share[1] for share in shares]).transpose(0, 2, 1)
        local_squares = (
            local_squares
            + jnp.sum(grad_first * grad_first)
            + jnp.sum(grad_attention * grad_attention)
            + jnp.sum(grad_router_all * grad_router_all)
        )
        grad_head = jnp.concatenate([grad_head[:classes].T, grad_bias[0:1, :classes]], 0)
        shared_head, shared_table, loss_total, squares = lax.psum(
            (grad_head, grad_table, loss_local, local_squares), ("dp", "fsdp")
        )
        norm = jnp.sqrt(
            squares + jnp.sum(shared_head * shared_head) + jnp.sum(shared_table * shared_table)
        )
    scale = jnp.minimum(1.0, CLIP_NORM / norm)
    scale_row = scale.reshape(1)

    def experts_updated(weight, first, second, factors, rate):
        lefts, rights = zip(*factors)
        return tuple(expert_adam(weight, first, second, lefts, rights, scale_row, rate))

    updates = (
        adam(dense_weights, dense_weights_first, dense_weights_second, grad_first * scale, LEARN_RATE),
        adam(attention, attention_first, attention_second, grad_attention * scale, ATTENTION_RATE),
        adam(router, router_first, router_second, grad_router_all * scale, LEARN_RATE),
        experts_updated(expert_in, expert_in_first, expert_in_second, in_factors, EXPERT_RATE),
        experts_updated(expert_out, expert_out_first, expert_out_second, out_factors, LEARN_RATE),
        adam(classifier, classifier_first, classifier_second, shared_head * scale, LEARN_RATE),
        adam(norm_table, norm_table_first, norm_table_second, shared_table * scale, TABLE_RATE),
    )
    return (loss_total, norm) + tuple(part for update in updates for part in update)


def solution(mesh):
    spread = P(("dp", "fsdp"))
    weights = (
        P(None, ("dp", "fsdp")),
        P(None, None, ("dp", "fsdp")),
        P(None, "dp", "fsdp"),
        P(None, "fsdp", None, "dp"),
        P(None, "fsdp", "dp", None),
        P(),
        P(),
    )
    moments = tuple(spec for spec in weights for _ in range(2))
    triples = tuple(spec for spec in weights for _ in range(3))
    return jax.shard_map(
        on_device,
        mesh=mesh,
        in_specs=(spread, spread, spread) + weights + moments,
        out_specs=(P(), P()) + triples,
        check_vma=False,
    )
```

```python
import functools

import jax
import jax.numpy as jnp
from jax import lax
from jax.experimental import pallas as pl
from jax.experimental.pallas import tpu as pltpu
from jax.sharding import PartitionSpec as P

HEADS = 6
FF = 1536
G_LO = 14
G_HI = 24
LEN = 576
LEN_LO = 196
ROWS_LO = 208
STEP = 10


LN_EPS = 1e-06
CLIP_NORM = 0.001
LEARN_RATE = 0.05
ATTENTION_RATE = 0.15
EXPERT_RATE = 1.0
TABLE_RATE = 0.5
BETA_ONE = 0.9
BETA_TWO = 0.95
ADAM_EPS = 1e-10
WEIGHT_DECAY = 0.1
SMOOTH = 0.1
NEG_FILL = -1e30
PRECISE = lax.Precision.HIGHEST
F32 = jnp.float32
BF16 = jnp.bfloat16
VMEM_BYTES = 60 * 1024 * 1024


def interp_matrix():
    rows = jnp.arange(G_HI, dtype=jnp.float32)[:, None]
    cols = jnp.arange(G_LO, dtype=jnp.float32)[None, :]
    weight = jnp.maximum(0.0, 1.0 - jnp.abs(rows * (G_LO - 1) - cols * (G_HI - 1)) / (G_HI - 1))
    return (weight[:, None, :, None] * weight[None, :, None, :]).reshape(G_HI * G_HI, G_LO * G_LO)


def matmul(left, right, form):
    return jnp.einsum(form, left, right, preferred_element_type=jnp.float32)


def contract(left, right, left_dim, right_dim):
    return lax.dot_general(
        left, right, (((left_dim,), (right_dim,)), ((), ())), preferred_element_type=F32
    )


def nn(left, right):
    return contract(left, right, 1, 0)


def nt(left, right):
    return contract(left, right, 1, 1)


def tn(left, right):
    return contract(left, right, 0, 0)


def normalise(values):
    center = values - jnp.mean(values, -1, keepdims=True)
    rate = lax.rsqrt(jnp.mean(center * center, -1, keepdims=True) + LN_EPS)
    return center * rate, rate


def normalise_back(unit, rate, gain, grad):
    scaled = grad * gain
    inner = scaled - jnp.mean(scaled, -1, keepdims=True)
    grad_in = rate * (inner - unit * jnp.mean(scaled * unit, -1, keepdims=True))
    return (
        grad_in,
        jnp.sum(grad * unit, 0, keepdims=True),
        jnp.sum(grad, 0, keepdims=True),
    )


def row_number(shape):
    return lax.broadcasted_iota(jnp.int32, shape, 0)


def side_masks():
    lane = lax.broadcasted_iota(jnp.int32, (1, 128), 1)
    first = (lane < 64).astype(F32)
    return (first.astype(BF16), (1.0 - first).astype(BF16))


def lanes(offset):
    return pl.ds(pl.multiple_of(offset, 128), 128)


GELU_RATE = 0.7978845608028654


def gelu(v):
    return 0.5 * v * (1.0 + jnp.tanh(GELU_RATE * (v + 0.044715 * (v * v * v))))


def gelu_both(v):
    square = v * v
    bend = jnp.tanh(GELU_RATE * (v + 0.044715 * (square * v)))
    half = 0.5 * (1.0 + bend)
    slope = half + 0.5 * v * (1.0 - bend * bend) * (GELU_RATE * (1.0 + 3 * 0.044715 * square))
    return v * half, slope


def attention_rows(rows, limit, qkv, context):
    width = context.shape[1]
    first = lax.broadcasted_iota(jnp.int32, (rows, 128), 1) < 64
    masks = side_masks()
    ones = jnp.ones((rows, 128), BF16)
    for offset in range(0, width, 128):
        query = qkv[:rows, offset : offset + 128] * BF16(0.125)
        keys = qkv[:rows, width + offset : width + offset + 128]
        values = qkv[:rows, 2 * width + offset : 2 * width + offset + 128]
        summing = jnp.concatenate([values, ones], 1)
        found = []
        for side in (0, 1):
            scores = nt(query * masks[side], keys)
            if limit is not None:
                lane = lax.broadcasted_iota(jnp.int32, (rows, rows), 1)
                scores = jnp.where(lane < limit, scores, NEG_FILL)
            raised = jnp.exp(scores - jnp.max(scores, 1, keepdims=True))
            both = nn(raised.astype(BF16), summing)
            found.append(both[:, :128] * (1.0 / both[:, 128:]))
        context[:rows, offset : offset + 128] = jnp.where(first, found[0], found[1]).astype(BF16)


def scores_back(limit, keys, values, query, grad):
    scores = nt(keys, query)
    if limit is not None:
        scores = jnp.where(row_number(scores.shape) < limit, scores, NEG_FILL)
    raised = jnp.exp(scores - jnp.max(scores, 0, keepdims=True))
    probs = raised * (1.0 / jnp.sum(raised, 0, keepdims=True))
    grad_values = nn(probs.astype(BF16), grad)
    grad_probs = nt(values, grad)
    mixed = jnp.sum(probs * grad_probs, 0, keepdims=True)
    grad_scores = (probs * (grad_probs - mixed)).astype(BF16)
    return grad_scores, nn(grad_scores, query), grad_values


def attention_rows_back(rows, limit, qkv, grad_context, grad_qkv):
    width = grad_context.shape[1]
    masks = side_masks()
    first = lax.broadcasted_iota(jnp.int32, (rows, 128), 1) < 64

    def pair(offset):
        query = qkv[:rows, lanes(offset)] * BF16(0.125)
        keys = qkv[:rows, lanes(width + offset)]
        values = qkv[:rows, lanes(2 * width + offset)]
        grad = grad_context[:rows, lanes(offset)]
        queries = [query * mask for mask in masks]
        grads = [grad * mask for mask in masks]
        if limit is None:
            grad_scores, grad_keys, grad_values = scores_back(
                limit, keys, values, jnp.concatenate(queries, 0), jnp.concatenate(grads, 0)
            )
            both = tn(grad_scores, keys)
            grad_query = jnp.where(first, both[:rows], both[rows:])
        else:
            one, two = [
                scores_back(limit, keys, values, queries[side], grads[side]) for side in (0, 1)
            ]
            grad_query = tn(one[0], keys * masks[0]) + tn(two[0], keys * masks[1])
            grad_keys, grad_values = one[1] + two[1], one[2] + two[2]
        grad_qkv[:rows, lanes(offset)] = (grad_query * 0.125).astype(BF16)
        grad_qkv[:rows, lanes(width + offset)] = grad_keys.astype(BF16)
        grad_qkv[:rows, lanes(2 * width + offset)] = grad_values.astype(BF16)

    if limit is None:

        def step(index, carry):
            pair(index * 128)
            return carry

        lax.fori_loop(0, width // 128, step, 0)
    else:
        for offset in range(0, width, 128):
            pair(offset)


def attention_forward(rows, limit, hidden, gains, weights, qkv, context):
    width = hidden.shape[1]
    unit, _ = normalise(hidden)
    normed = (unit * gains[0:1] + gains[1:2]).astype(BF16)
    qkv[:rows] = nt(normed, weights[: 3 * width]).astype(BF16)
    attention_rows(rows, limit, qkv, context)
    return hidden + nn(context[:rows], weights[3 * width :])


def attention_backward(
    rows, limit, hidden, grad_middle, gains, weights, qkv, context, hold_context, hold_qkv,
    grad_weights, grad_gains,
):
    width = hidden.shape[1]
    grad_b = grad_middle.astype(BF16)
    hold_context[:rows] = nt(grad_b, weights[3 * width :]).astype(BF16)
    grad_weights[3 * width :] += tn(context[:rows], grad_b)
    attention_rows_back(rows, limit, qkv, hold_context, hold_qkv)
    unit, rate = normalise(hidden)
    normed = (unit * gains[0:1] + gains[1:2]).astype(BF16)
    grad_weights[: 3 * width] += tn(hold_qkv[:rows], normed)
    grad_normed = nn(hold_qkv[:rows], weights[: 3 * width])
    grad_in, grad_gain, grad_bias = normalise_back(unit, rate, gains[0:1], grad_normed)
    grad_gains[0:1] += grad_gain
    grad_gains[1:2] += grad_bias
    return grad_middle + grad_in


def mlp_forward(rows, middle, gains, weights, pixels):
    unit, _ = normalise(middle)
    normed = (unit * gains[2:3] + gains[3:4]).astype(BF16)
    chunk = middle.shape[1]
    total = middle
    for start in range(0, FF, chunk):
        pre = nt(normed, weights[pixels + start : pixels + start + chunk])
        out = weights[pixels + FF + start : pixels + FF + start + chunk]
        total = total + nn(gelu(pre).astype(BF16), out)
    return total


def mlp_backward(rows, middle, grad, gains, weights, pixels, grad_weights, grad_gains):
    unit, rate = normalise(middle)
    normed = (unit * gains[2:3] + gains[3:4]).astype(BF16)
    grad_b = grad.astype(BF16)
    chunk = middle.shape[1]
    grad_normed = None
    for start in range(0, FF, chunk):
        first = slice(pixels + start, pixels + start + chunk)
        second = slice(pixels + FF + start, pixels + FF + start + chunk)
        hid, slope = gelu_both(nt(normed, weights[first]))
        grad_weights[second] += tn(hid.astype(BF16), grad_b)
        grad_pre = (nt(grad_b, weights[second]) * slope).astype(BF16)
        grad_weights[first] += tn(grad_pre, normed)
        part = nn(grad_pre, weights[first])
        grad_normed = part if grad_normed is None else grad_normed + part
    grad_in, grad_gain, grad_bias = normalise_back(unit, rate, gains[2:3], grad_normed)
    grad_gains[2:3] += grad_gain
    grad_gains[3:4] += grad_bias
    return grad + grad_in


def route(limit, middle, gains, router):
    unit, rate = normalise(middle)
    normed = (unit * gains[2:3] + gains[3:4]).astype(BF16)
    logits = nt(normed, router[...])
    masked = logits
    if limit is not None:
        masked = jnp.where(row_number(logits.shape) < limit, logits, NEG_FILL)
    raised = jnp.exp(masked - jnp.max(masked, 0, keepdims=True))
    dispatch = raised * (1.0 / jnp.sum(raised, 0, keepdims=True))
    raised = jnp.exp(logits - jnp.max(logits, 1, keepdims=True))
    combine = raised * (1.0 / jnp.sum(raised, 1, keepdims=True))
    return unit, rate, normed, dispatch, combine


def masked_rows(limit, values):
    if limit is None:
        return values
    return jnp.where(row_number(values.shape) < limit, values, 0.0)


def work_of(giga):
    return pl.CostEstimate(flops=giga * 10**9, bytes_accessed=1 << 20, transcendentals=0)


def by_image(name, body, scalars, per_image, whole, out_image, out_sum, scratch=(), pack=None):
    images = scalars[0].shape[0]
    inner = pack[0] if pack else 0
    packed = 1 if pack else 0
    counts = (
        len(scalars), len(per_image), len(whole), len(out_image), packed, len(out_sum) - inner,
        inner, len(scratch),
    )

    def kernel(*refs):
        groups, at = [], 0
        for count in counts:
            groups.append(refs[at : at + count])
            at += count
        index = pl.program_id(0)
        sums = tuple(groups[6]) + tuple(groups[5])

        @pl.when(index == 0)
        def _():
            for ref in sums:
                ref[...] = jnp.zeros_like(ref)

        numbers = [ref[index] for ref in groups[0]]
        given = (*groups[1:4], sums, groups[7])

        @pl.when(numbers[0] == 1)
        def _():
            body(LEN, None, numbers, *given)

        @pl.when(numbers[0] != 1)
        def _():
            body(ROWS_LO, LEN_LO + numbers[0], numbers, *given)

        if pack:

            @pl.when(index == images - 1)
            def _():
                def write(device, carry):
                    groups[4][0][device] = pack[3](sums, device).astype(BF16)
                    return carry

                lax.fori_loop(0, pack[1], write, 0)

    width = out_sum[0][1] if pack else 0
    pack_shapes = [(pack[1], pack[2], width)] if pack else []

    def image_spec(shape):
        return pl.BlockSpec((None,) + tuple(shape[1:]), lambda i, *_: (i, 0, 0))

    return pl.pallas_call(
        kernel,
        grid_spec=pltpu.PrefetchScalarGridSpec(
            num_scalar_prefetch=len(scalars),
            grid=(images,),
            in_specs=[image_spec(a.shape) for a in per_image]
            + [pl.BlockSpec(memory_space=pltpu.VMEM) for _ in whole],
            out_specs=[image_spec((images,) + shape) for shape, _ in out_image]
            + [pl.BlockSpec(shape, lambda i, *_: (0, 0, 0)) for shape in pack_shapes]
            + [pl.BlockSpec(shape, lambda i, *_: (0, 0)) for shape in out_sum[inner:]],
            scratch_shapes=[pltpu.VMEM(shape, F32) for shape in out_sum[:inner]] + list(scratch),
        ),
        out_shape=[jax.ShapeDtypeStruct((images,) + shape, dtype) for shape, dtype in out_image]
        + [jax.ShapeDtypeStruct(shape, BF16) for shape in pack_shapes]
        + [jax.ShapeDtypeStruct(shape, F32) for shape in out_sum[inner:]],
        compiler_params=pltpu.CompilerParams(vmem_limit_bytes=VMEM_BYTES),
        cost_estimate=work_of(images * 8),
        name=name,
    )(*scalars, *per_image, *whole)


def rows_of(ref, device, count):
    return ref[pl.ds(pl.multiple_of(device * count, 8), count)]


def padded_rows(blocks):
    rows = sum(block.shape[0] for block in blocks)
    if rows % 16:
        blocks = blocks + [jnp.zeros((-rows % 16, blocks[0].shape[1]), F32)]
    return jnp.concatenate(blocks, 0) if len(blocks) > 1 else blocks[0]


def up_16(count):
    return count + -count % 16


def first_forward(resolution, patches, dense, attention, positions, gains, width):
    pixels = patches.shape[2]

    def body(rows, limit, numbers, images, whole, outs, sums, scratch):
        dense_ref, attention_ref, position_ref, gain_ref = whole
        start, qkv, context, middle, last = outs
        place = position_ref[0 if limit is not None else 1, :rows]
        embedded = masked_rows(limit, nn(images[0][:rows], dense_ref[:pixels]) + place)
        start[:rows] = embedded
        middle_rows = attention_forward(
            rows, limit, embedded, gain_ref, attention_ref, qkv, context
        )
        middle[:rows] = middle_rows
        last[:rows] = mlp_forward(rows, middle_rows, gain_ref, dense_ref, pixels)

    return by_image(
        "first_forward",
        body,
        [resolution],
        [patches],
        [dense, attention, positions, gains],
        [
            ((LEN, width), F32),
            ((LEN, 3 * width), BF16),
            ((LEN, width), BF16),
            ((LEN, width), F32),
            ((LEN, width), F32),
        ],
        [],
    )


def sparse_forward(resolution, hidden, mixing, attention, router, gains):
    width = hidden.shape[2]
    experts = router.shape[0]

    def body(rows, limit, numbers, images, whole, outs, sums, scratch):
        attention_ref, router_ref, gain_ref = whole
        before, qkv, context, middle, combine, slots = ([None] + list(outs))[-6:]
        hidden_rows = images[0][:rows]
        if mixing is not None:
            hidden_rows = hidden_rows + nn(images[1][:rows], images[2][...])
            before[:rows] = hidden_rows
        middle_rows = attention_forward(
            rows, limit, hidden_rows, gain_ref, attention_ref, qkv, context
        )
        middle[:rows] = middle_rows
        _, _, normed, dispatch, share = route(limit, middle_rows, gain_ref, router_ref)
        combine[:rows] = share.astype(BF16)
        slots[...] = tn(dispatch.astype(BF16), normed).astype(BF16)

    outs = [
        ((LEN, 3 * width), BF16),
        ((LEN, width), BF16),
        ((LEN, width), F32),
        ((LEN, experts), BF16),
        ((experts, width), BF16),
    ]
    if mixing is not None:
        outs = [((LEN, width), F32)] + outs
    return by_image(
        "sparse_forward",
        body,
        [resolution],
        [hidden] + list(mixing or ()),
        [attention, router, gains],
        outs,
        [],
    )


def top(resolution, labels, middle, combine, returned, head, head_bias, last_gains, classes, images, devices):
    width = middle.shape[2]
    experts = returned.shape[1]
    padded = head.shape[1]

    def body(rows, limit, numbers, per_image, whole, outs, sums, scratch):
        middle_ref, combine_ref, returned_ref = per_image
        head_ref, bias_ref, gain_ref = whole
        grad_hidden, grad_returned = outs
        grad_head, grad_bias_row, grad_gains, loss = sums
        length = float(LEN if limit is None else LEN_LO)
        share = combine_ref[:rows]
        hidden = middle_ref[:rows] + nn(share, returned_ref[...])
        unit, rate = normalise(hidden)
        normed = masked_rows(limit, unit * gain_ref[0:1] + gain_ref[1:2])
        pooled = jnp.sum(normed, 0, keepdims=True) * (1.0 / length)
        one_row = (row_number((8, width)) == 0).astype(F32)
        pooled_b = (one_row * pooled).astype(BF16)
        logits = nn(pooled_b, head_ref[...])[0:1] + bias_ref[...]
        shifted = logits - jnp.max(logits, 1, keepdims=True)
        raised = jnp.exp(shifted)
        total = jnp.sum(raised, 1, keepdims=True)
        log_probs = shifted - jnp.log(total)
        lane = lax.broadcasted_iota(jnp.int32, (1, padded), 1)
        target = jnp.where(lane == numbers[1], 1.0 - SMOOTH, 0.0) + jnp.where(
            lane < classes, SMOOTH / classes, 0.0
        )
        picked = jnp.sum(target * log_probs, 1, keepdims=True)
        loss[...] += jnp.broadcast_to(picked * (-1.0 / images), loss.shape)
        grad_logits = (raised * (1.0 / total) - target) * (1.0 / images)
        grad_bias_row[0:1] += grad_logits
        row_mask = (row_number((8, padded)) == 0).astype(F32)
        grad_logits_b = (row_mask * grad_logits).astype(BF16)
        grad_head[...] += tn(grad_logits_b, pooled_b)
        grad_pooled = nt(grad_logits_b, head_ref[...])[0:1] * (1.0 / length)
        grad_normed = masked_rows(limit, jnp.broadcast_to(grad_pooled, (rows, width)))
        grad_rows, grad_gain, grad_bias = normalise_back(
            unit, rate, gain_ref[0:1], grad_normed
        )
        grad_gains[0:1] += grad_gain
        grad_gains[1:2] += grad_bias
        grad_hidden[:rows] = grad_rows
        grad_returned[...] = tn(share, grad_rows.astype(BF16)).astype(BF16)

    return by_image(
        "top",
        body,
        [resolution, labels],
        [middle, combine, returned],
        [head, head_bias, last_gains],
        [((LEN, width), F32), ((experts, width), BF16)],
        [(padded, width), (8, padded), (8, width), (8, 128)],
        pack=devices
        and (
            1, devices, padded // devices,
            lambda sums, device: rows_of(sums[0], device, padded // devices),
        ),
    )


def sparse_backward(
    resolution, hidden, qkv, context, middle, grad_hidden, returned, grad_home, below, attention,
    router, gains, devices,
):
    width = middle.shape[2]
    experts = router.shape[0]
    chips = lax.axis_size("fsdp")
    local = experts // chips

    def body(rows, limit, numbers, images, whole, outs, sums, scratch):
        hidden_ref, qkv_ref, context_ref, middle_ref, grad_ref, returned_ref, home_ref = images[:7]
        attention_ref, router_ref, gain_ref = whole
        grad_attention, grad_router, grad_gains = sums
        grad = grad_ref[:rows]
        grad_combine = nt(grad.astype(BF16), returned_ref[...])
        unit, rate, normed, dispatch, share = route(
            limit, middle_ref[:rows], gain_ref, router_ref
        )
        home = home_ref[...]
        grad_dispatch = nt(normed, home)
        grad_normed = nn(dispatch.astype(BF16), home)
        grad_route = dispatch * (
            grad_dispatch - jnp.sum(grad_dispatch * dispatch, 0, keepdims=True)
        ) + share * (grad_combine - jnp.sum(grad_combine * share, 1, keepdims=True))
        grad_route_b = grad_route.astype(BF16)
        grad_router[...] += tn(grad_route_b, normed)
        grad_normed = grad_normed + nn(grad_route_b, router_ref[...])
        grad_in, grad_gain, grad_bias = normalise_back(unit, rate, gain_ref[2:3], grad_normed)
        grad_gains[2:3] += grad_gain
        grad_gains[3:4] += grad_bias
        grad_rows = attention_backward(
            rows, limit, hidden_ref[:rows], grad + grad_in, gain_ref, attention_ref, qkv_ref,
            context_ref, scratch[0], scratch[1], grad_attention, grad_gains,
        )
        outs[0][:rows] = grad_rows
        if below is not None:
            outs[1][...] = tn(images[7][:rows], grad_rows.astype(BF16)).astype(BF16)

    outs = [((LEN, width), F32)]
    if below is not None:
        outs.append(((experts, width), BF16))
    return by_image(
        "sparse_backward",
        body,
        [resolution],
        [hidden, qkv, context, middle, grad_hidden, returned, grad_home]
        + ([] if below is None else [below]),
        [attention, router, gains],
        outs,
        [(4 * width, width), (experts, width), (8, width)],
        [pltpu.VMEM((LEN, width), BF16), pltpu.VMEM((LEN, 3 * width), BF16)],
        pack=devices
        and (
            2, devices, up_16(4 * width // devices + local),
            lambda sums, device: padded_rows(
                [
                    rows_of(sums[0], device, 4 * width // devices),
                    rows_of(sums[1], device % chips, local),
                ]
            ),
        ),
    )


def first_backward(
    resolution, patches, start, qkv, context, middle, grad_hidden, dense, attention, gains, devices
):
    width = middle.shape[2]
    pixels = patches.shape[2]
    columns = dense.shape[0]

    def body(rows, limit, numbers, images, whole, outs, sums, scratch):
        patches_ref, start_ref, qkv_ref, context_ref, middle_ref, grad_ref = images
        dense_ref, attention_ref, gain_ref = whole
        grad_dense, grad_attention, grad_gains, grad_low, grad_high = sums
        grad_middle = mlp_backward(
            rows, middle_ref[:rows], grad_ref[:rows], gain_ref, dense_ref, pixels, grad_dense,
            grad_gains,
        )
        grad_rows = attention_backward(
            rows, limit, start_ref[:rows], grad_middle, gain_ref, attention_ref, qkv_ref,
            context_ref, scratch[0], scratch[1], grad_attention, grad_gains,
        )
        grad_rows = masked_rows(limit, grad_rows)
        grad_dense[:pixels] += tn(patches_ref[:rows], grad_rows.astype(BF16))
        if limit is None:
            grad_high[...] += grad_rows
        else:
            grad_low[...] += grad_rows

    return by_image(
        "first_backward",
        body,
        [resolution],
        [patches, start, qkv, context, middle, grad_hidden],
        [dense, attention, gains],
        [],
        [(columns, width), (4 * width, width), (8, width), (ROWS_LO, width), (LEN, width)],
        [pltpu.VMEM((LEN, width), BF16), pltpu.VMEM((LEN, 3 * width), BF16)],
        pack=devices
        and (
            2, devices, up_16((columns + 4 * width) // devices),
            lambda sums, device: padded_rows(
                [
                    rows_of(sums[0], device, columns // devices),
                    rows_of(sums[1], device, 4 * width // devices),
                ]
            ),
        ),
    )


def to_experts(values):
    return lax.all_to_all(values, "fsdp", split_axis=1, concat_axis=0, tiled=True)


def from_experts(values):
    return lax.all_to_all(values, "fsdp", split_axis=0, concat_axis=1, tiled=True)


def all_rows(values):
    return lax.all_gather(to_experts(values), "dp", axis=0, tiled=True).transpose(1, 0, 2)


def rows_home(part):
    shared = lax.psum_scatter(part.transpose(1, 0, 2), "dp", scatter_dimension=0, tiled=True)
    return from_experts(shared.astype(BF16))


def plain_exchange(layer, values, received, expert_in, expert_out):
    win, wout = expert_in[layer].astype(BF16), expert_out[layer].astype(BF16)
    rows = all_rows(values)
    if received is None:
        hid = gelu(matmul(rows, win, "end,edf->enf")).astype(BF16)
        return rows_home(matmul(hid, wout, "enf,efd->end")), rows
    hid, slope = gelu_both(matmul(received, win, "end,edf->enf"))
    hid = hid.astype(BF16)
    grad_pre = (matmul(rows, wout, "end,efd->enf") * slope).astype(BF16)
    home = rows_home(matmul(grad_pre, win, "enf,edf->end"))

    def gram(values):
        return matmul(values, values, "enk,emk->enm")

    squares = gram(received) * gram(grad_pre) + gram(hid) * gram(rows)
    return home, hid, grad_pre, rows, jnp.sum(squares, (0, 1)).reshape(1, -1)


def fetch_layer(attention_t, router_t):
    width = attention_t.shape[1]
    flat = router_t.reshape(-1)
    pack = jnp.concatenate(
        [attention_t, jnp.pad(flat, (0, -flat.size % width)).reshape(-1, width)], 0
    )
    return lax.all_gather(pack, ("dp", "fsdp"), axis=0)


def open_layer(both, part, part_cols, part_rows):
    width = both.shape[2]
    rows_dp = lax.axis_size("dp")
    cols_fsdp = lax.axis_size("fsdp")
    router = (
        both[:, part:]
        .reshape(rows_dp * cols_fsdp, -1)[:, : part_cols * part_rows]
        .reshape(rows_dp, cols_fsdp, part_cols, part_rows)
        .transpose(1, 2, 0, 3)
        .reshape(cols_fsdp * part_cols, rows_dp * part_rows)
    )
    return both[:, :part].reshape(-1, width), router


def share_layer(grad_attention, grad_router, part_cols, part_rows):
    rows_dp = lax.axis_size("dp")
    cols_fsdp = lax.axis_size("fsdp")
    devices = rows_dp * cols_fsdp
    width = grad_attention.shape[1]
    router = (
        grad_router.reshape(cols_fsdp, part_cols, rows_dp, part_rows)
        .transpose(2, 0, 1, 3)
        .reshape(devices, -1)
    )
    router = jnp.pad(router, ((0, 0), (0, -part_cols * part_rows % width)))
    router = router.reshape(devices, -1, width)
    pack = jnp.concatenate([grad_attention.reshape(devices, -1, width), router], 1)
    mine = lax.psum_scatter(pack, ("dp", "fsdp"), scatter_dimension=0, tiled=False)
    part = grad_attention.shape[0] // devices
    return mine[:part], mine[part:].reshape(-1)[: part_cols * part_rows].reshape(part_cols, part_rows)


BITS = 4
GATHER_ORDERS = ((3, 2, 0, 1), (0, 1, 2, 3), (0, 1, 3, 2))
MESH_IDS = pl.DeviceIdType.MESH


def my_bits():
    at = lax.axis_index("fsdp")
    return [(at // (1 << (BITS - 1 - bit))) % 2 for bit in range(BITS)]


def partner_of(bit):
    at = lax.axis_index("fsdp")
    step = 1 << (BITS - 1 - bit)
    return (lax.axis_index("dp"), at + step * (1 - 2 * ((at // step) % 2)))


def sibling():
    return (1 - lax.axis_index("dp"), lax.axis_index("fsdp"))


def greet_partners():
    barrier = pltpu.get_barrier_semaphore()
    others = [partner_of(bit) for bit in range(BITS)] + [sibling()]
    for other in others:
        pl.semaphore_signal(barrier, inc=1, device_id=other, device_id_type=MESH_IDS)
    pl.semaphore_wait(barrier, len(others))


def send(source, target, send_sem, recv_sem, device):
    copy = pltpu.make_async_remote_copy(
        src_ref=source,
        dst_ref=target,
        send_sem=send_sem,
        recv_sem=recv_sem,
        device_id=device,
        device_id_type=MESH_IDS,
    )
    copy.start()
    return copy


def spread(parts, sems):
    mine = my_bits()
    core = lax.axis_index("dp")
    to_send, to_get, pass_send, pass_get = sems

    def view(part, stage, other):
        ref, lane_part, order = part
        index = []
        for bit in range(BITS):
            if bit in order[:stage]:
                index.append(slice(None))
            elif other and bit == order[stage]:
                index.append(1 - mine[bit])
            else:
                index.append(mine[bit])
        return ref.at[(core, *index, slice(None), lane_part)]

    def go(number, stage):
        block = view(parts[number], stage, False)
        return send(
            block, block, to_send.at[number, stage], to_get.at[number, stage],
            partner_of(parts[number][2][stage]),
        )

    def hand_over(number, slot, block):
        return send(block, block, pass_send.at[number, slot], pass_get.at[number, slot], sibling())

    going = [go(number, 0) for number in range(len(parts))]
    handed = [
        hand_over(number, BITS, view(parts[number], 0, False)) for number in range(len(parts))
    ]
    for stage in range(BITS):
        for number in range(len(parts)):
            going[number].wait()
            if stage + 1 < BITS:
                going[number] = go(number, stage + 1)
            handed.append(hand_over(number, stage, view(parts[number], stage, True)))
    for copy in handed:
        copy.wait()


def spread_sems(count):
    return [pltpu.SemaphoreType.DMA((count, BITS + 1)) for _ in range(4)]


def lane_parts(width):
    return [slice(start, start + 128) for start in range(0, width, 128)]


def gather_all(shards, collective_id):
    count = len(shards)
    width = shards[0].shape[1]
    cuts = lane_parts(width)

    def kernel(*refs):
        ins, outs, sems = refs[:count], refs[count : 2 * count], refs[2 * count :]
        place = (lax.axis_index("dp"), *my_bits())
        for ref, out in zip(ins, outs):
            out[place] = ref[...]
        greet_partners()
        spread(
            [
                (out, cut, GATHER_ORDERS[number % 3])
                for number, cut in enumerate(cuts)
                for out in outs
            ],
            sems,
        )

    outs = pl.pallas_call(
        kernel,
        in_specs=[pl.BlockSpec(memory_space=pltpu.VMEM)] * count,
        out_specs=[pl.BlockSpec(memory_space=pltpu.VMEM)] * count,
        out_shape=[jax.ShapeDtypeStruct((2,) * (BITS + 1) + s.shape, s.dtype) for s in shards],
        scratch_shapes=spread_sems(count * len(cuts)),
        compiler_params=pltpu.CompilerParams(
            collective_id=collective_id, has_side_effects=True, vmem_limit_bytes=VMEM_BYTES
        ),
        cost_estimate=work_of(40),
        name="gather_all",
    )(*shards)
    return [out.reshape(-1, width) for out in outs]


def reduce_all(grads, stats, shared, halved, collective_id):
    width = grads[0].shape[2]
    count = len(grads)
    starts = [sum(grad.shape[1] for grad in grads[:at]) for at in range(count + 1)]
    rows = starts[-1]
    cuts = lane_parts(width)
    parts = len(cuts)
    orders = [tuple(reversed(GATHER_ORDERS[number % 3])) for number in range(parts)]

    def kernel(*refs):
        grads_refs = refs[:count]
        stats_ref, mine_ref, shared_ref, total_ref = refs[count : count + 4]
        scratch = refs[count + 4 :]
        sums, first_get = scratch[:2]
        gets = scratch[2 : 2 + BITS]
        stats_all = scratch[2 + BITS]
        local_sem, pair_send, pair_get, to_send, to_get = scratch[3 + BITS : 8 + BITS]
        sems = scratch[8 + BITS :]
        core = lax.axis_index("dp")
        bits = my_bits()
        places = [
            (number, at, cut, slice(starts[at], starts[at + 1]))
            for number, cut in enumerate(cuts)
            for at in range(count)
        ]
        local = {
            (number, at): pltpu.make_async_copy(
                grads_refs[at].at[core, :, :, :, :, :, cut],
                sums.at[:, :, :, :, span, cut],
                local_sem.at[number, at],
            )
            for number, at, cut, span in places
        }
        for copy in local.values():
            copy.start()
        greet_partners()
        pairs = {
            (number, at): send(
                grads_refs[at].at[1 - core, :, :, :, :, :, cut],
                first_get.at[:, :, :, :, span, cut],
                pair_send.at[number, at],
                pair_get.at[number, at],
                sibling(),
            )
            for number, at, cut, span in places
        }

        def index(number, stage, own):
            order = orders[number]
            found = []
            for bit in range(BITS):
                if bit in order[:stage]:
                    found.append(bits[bit])
                elif bit == order[stage]:
                    found.append(bits[bit] if own else 1 - bits[bit])
                else:
                    found.append(slice(None))
            return (*found, slice(None), cuts[number])

        def go(number, stage):
            return send(
                sums.at[index(number, stage, False)],
                gets[stage].at[number],
                to_send.at[number, stage],
                to_get.at[number, stage],
                partner_of(orders[number][stage]),
            )

        going = [None] * parts
        turns = [number for number in range(parts) if number % 3] + list(range(0, parts, 3))
        for number in reversed(turns):
            for at in range(count):
                local[number, at].wait()
                pairs[number, at].wait()
            whole = (slice(None),) * (BITS + 1) + (cuts[number],)
            sums[whole] = sums[whole] + first_get[whole]
            going[number] = go(number, 0)
        place = tuple(bits)
        for stage in range(BITS):
            for number in turns:
                going[number].wait()
                if stage + 1 < BITS:
                    at = index(number, stage, True)
                    sums[at] = sums[at] + gets[stage][number]
                    going[number] = go(number, stage + 1)
                else:
                    at = index(number, stage, True)
                    mine_ref[:, cuts[number]] = sums[at].astype(F32) + gets[stage][number].astype(F32)
        mine = mine_ref[...]
        row = row_number((rows, width))
        counted = mine * mine
        for low, high in halved:
            counted = jnp.where((row >= low) & (row < high), 0.5 * counted, counted)
        squares = jnp.sum(jnp.sum(counted, 0, keepdims=True), 1, keepdims=True)
        top_row = (row_number((8, 128)) == 0).astype(F32)
        stats_all[(core, *place)] = stats_ref[...] + top_row * squares
        shared_ref[(core, *place)] = mine_ref[rows - shared :, :].astype(BF16)
        spread(
            [
                (shared_ref, cut, GATHER_ORDERS[number % 3]) for number, cut in enumerate(cuts)
            ]
            + [(stats_all, slice(0, 128), GATHER_ORDERS[1])],
            sems,
        )
        total_ref[...] = jnp.sum(stats_all[...].reshape(32, 8, 128), 0)

    grid = (2,) * BITS
    return pl.pallas_call(
        kernel,
        in_specs=[pl.BlockSpec(memory_space=pl.ANY)] * count
        + [pl.BlockSpec(memory_space=pltpu.VMEM)],
        out_specs=[pl.BlockSpec(memory_space=pltpu.VMEM)] * 3,
        out_shape=[
            jax.ShapeDtypeStruct((rows, width), F32),
            jax.ShapeDtypeStruct((2,) + grid + (shared, width), BF16),
            jax.ShapeDtypeStruct((8, 128), F32),
        ],
        scratch_shapes=[pltpu.VMEM(grid + (rows, width), BF16)] * 2
        + [pltpu.VMEM((parts,) + (2,) * (BITS - 1 - stage) + (rows, 128), BF16) for stage in range(BITS)]
        + [pltpu.VMEM((2,) + grid + (8, 128), F32)]
        + [pltpu.SemaphoreType.DMA((parts, count))] * 3
        + [pltpu.SemaphoreType.DMA((parts, BITS))] * 2
        + spread_sems(parts + 1),
        compiler_params=pltpu.CompilerParams(
            collective_id=collective_id, has_side_effects=True, vmem_limit_bytes=VMEM_BYTES
        ),
        cost_estimate=work_of(60),
        name="reduce_all",
    )(*[grad.reshape((2,) + grid + grad.shape[1:]) for grad in grads], stats)


def chip(at):
    return (lax.axis_index("dp"), at)


def greet_all(chips):
    barrier = pltpu.get_barrier_semaphore()
    me = lax.axis_index("fsdp")

    def one(step, carry):
        pl.semaphore_signal(
            barrier, inc=1, device_id=chip((me + step) % chips), device_id_type=MESH_IDS
        )
        return carry

    lax.fori_loop(1, chips, one, 0)
    pl.semaphore_signal(barrier, inc=1, device_id=sibling(), device_id_type=MESH_IDS)
    pl.semaphore_wait(barrier, chips)


def swap_start(chips, source, target, send_sem, get_sem):
    me = lax.axis_index("fsdp")

    def one(step, carry):
        other = (me + step) % chips
        send(source.at[other], target.at[me], send_sem.at[other], get_sem.at[me], chip(other))
        return carry

    lax.fori_loop(1, chips, one, 0)


def swap_sent(chips, step, source, target, send_sem, get_sem):
    me = lax.axis_index("fsdp")
    to = (me + step) % chips
    pltpu.make_async_remote_copy(
        src_ref=source.at[to], dst_ref=target.at[me], send_sem=send_sem.at[to],
        recv_sem=get_sem.at[me], device_id=chip(to), device_id_type=MESH_IDS,
    ).wait_send()


def swap_arrived(chips, step, source, target, send_sem, get_sem):
    origin = (lax.axis_index("fsdp") + chips - step) % chips
    pltpu.make_async_remote_copy(
        src_ref=source.at[origin], dst_ref=target.at[origin], send_sem=send_sem.at[origin],
        recv_sem=get_sem.at[origin], device_id=chip(origin), device_id_type=MESH_IDS,
    ).wait_recv()
    return origin


def exchange(layer, values, received, expert_in, expert_out, collective_id):
    images, experts, width = values.shape
    chips = lax.axis_size("fsdp")
    cores = lax.axis_size("dp")
    local, _, hidden = expert_in.shape[1:]
    rows = images * local
    half = chips * images
    every = cores * half
    backward = received is not None

    def kernel(*refs):
        if backward:
            values_ref, received_ref, in_ref, out_ref = refs[:4]
            home_ref, hid_ref, pre_ref, gout_ref, squares_ref = refs[4:9]
            slope_ref = refs[9]
            scratch = refs[10:]
        else:
            values_ref, in_ref, out_ref = refs[:3]
            home_ref, received_ref = refs[3:5]
            scratch = refs[5:]
        win, wout, outbox, inbox, parts, pair_out, pair_in, sorted_ref, backbox, homebox = scratch[:10]
        win_sem, wout_sem, send_one, get_one, pass_send, pass_get, pair_send, pair_get, send_two, get_two = scratch[10:]
        core = lax.axis_index("dp")
        me = lax.axis_index("fsdp")

        def fetch(e):
            return (
                pltpu.make_async_copy(in_ref.at[layer, e], win.at[e], win_sem.at[e]),
                pltpu.make_async_copy(out_ref.at[layer, e], wout.at[e], wout_sem.at[e]),
            )

        def start_fetch(e, carry):
            for copy in fetch(e):
                copy.start()
            return carry

        lax.fori_loop(0, local, start_fetch, 0)
        whole = [values_ref[image].astype(F32) for image in range(images)]
        for at in range(chips):
            outbox[at] = jnp.concatenate(
                [one[at * local : (at + 1) * local] for one in whole], 0
            ).astype(BF16)
        greet_all(chips)
        swap_start(chips, outbox, inbox.at[core], send_one, get_one)
        inbox[core, me] = outbox[me]

        def hand(at):
            block = inbox.at[core, at]
            return pltpu.make_async_remote_copy(
                src_ref=block, dst_ref=block, send_sem=pass_send.at[at],
                recv_sem=pass_get.at[at], device_id=sibling(), device_id_type=MESH_IDS,
            )

        def handed(at):
            block = inbox.at[1 - core, at]
            return pltpu.make_async_remote_copy(
                src_ref=block, dst_ref=block, send_sem=pass_send.at[at],
                recv_sem=pass_get.at[at], device_id=sibling(), device_id_type=MESH_IDS,
            )

        hand(me).start()
        if backward:

            def ahead(e, carry):
                for copy in fetch(e):
                    copy.wait()
                rec = received_ref[e]
                hid, slope = gelu_both(nn(rec, win[e].astype(BF16)))
                slope_ref[e] = slope
                hid_ref[e] = hid.astype(BF16)
                return carry

            lax.fori_loop(0, local, ahead, 0)

        def arrive(step, carry):
            hand(swap_arrived(chips, step, outbox, inbox.at[core], send_one, get_one)).start()
            return carry

        lax.fori_loop(1, chips, arrive, 0)

        def all_handed(at, carry):
            handed(at).wait_recv()
            return carry

        lax.fori_loop(0, chips, all_handed, 0)
        arrived = inbox[...].reshape(every * local, width)
        pick_row = lax.broadcasted_iota(jnp.int32, (every, every * local), 0)
        pick_col = lax.broadcasted_iota(jnp.int32, (every, every * local), 1)
        wanted = pick_row * local - pick_col

        def pair_copy(e):
            return pltpu.make_async_remote_copy(
                src_ref=pair_out.at[e], dst_ref=pair_in.at[e], send_sem=pair_send.at[e],
                recv_sem=pair_get.at[e], device_id=sibling(), device_id_type=MESH_IDS,
            )

        if backward:
            squares_ref[...] = jnp.zeros_like(squares_ref)

        def work(e, carry):
            pick = (wanted == -e).astype(F32).astype(BF16)
            mine = nn(pick, arrived).astype(BF16)
            if backward:
                gout_ref[e] = mine
                grad_pre = (nt(mine, wout[e].astype(BF16)) * slope_ref[e]).astype(BF16)
                pre_ref[e] = grad_pre
                part = nt(grad_pre, win[e].astype(BF16))
                rec, hid = received_ref[e], hid_ref[e]
                product = nt(rec, rec) * nt(grad_pre, grad_pre) + nt(hid, hid) * nt(mine, mine)
                squares_ref[...] += jnp.sum(product.reshape(every // 8, 8, every), 0)
            else:
                for copy in fetch(e):
                    copy.wait()
                received_ref[e] = mine
                hid = gelu(nn(mine, win[e].astype(BF16))).astype(BF16)
                part = nn(hid, wout[e].astype(BF16))
            parts[e] = part.reshape(cores, half, width)
            pair_out[e] = parts[e, 1 - core].astype(BF16)
            pair_copy(e).start()
            return carry

        lax.fori_loop(0, local, work, 0)

        def add(e, carry):
            pair_copy(e).wait_recv()
            sorted_ref[pl.ds(pl.multiple_of(e * half, half), half)] = (
                parts[e, core] + pair_in[e].astype(F32)
            ).astype(BF16)
            return carry

        lax.fori_loop(0, local, add, 0)
        back_row = lax.broadcasted_iota(jnp.int32, (half * local, half * local), 0)
        back_col = lax.broadcasted_iota(jnp.int32, (half * local, half * local), 1)
        back = (back_row == (back_col % half) * local + back_col // half).astype(F32).astype(BF16)
        backbox[...] = nn(back, sorted_ref[...]).astype(BF16).reshape(chips, rows, width)
        swap_start(chips, backbox, homebox, send_two, get_two)
        homebox[me] = backbox[me]

        def home(step, carry):
            swap_arrived(chips, step, backbox, homebox, send_two, get_two)
            return carry

        lax.fori_loop(1, chips, home, 0)
        blocks = [homebox[at].astype(F32) for at in range(chips)]
        for image in range(images):
            home_ref[image] = jnp.concatenate(
                [block[image * local : (image + 1) * local] for block in blocks], 0
            ).astype(BF16)

        def drain(step, carry):
            swap_sent(chips, step, outbox, inbox.at[core], send_one, get_one)
            swap_sent(chips, step, backbox, homebox, send_two, get_two)
            return carry

        lax.fori_loop(1, chips, drain, 0)

        def drain_pass(at, carry):
            hand(at).wait_send()
            return carry

        lax.fori_loop(0, chips, drain_pass, 0)

        def drain_pair(e, carry):
            pair_copy(e).wait_send()
            return carry

        lax.fori_loop(0, local, drain_pair, 0)

    inside = pl.BlockSpec(memory_space=pltpu.VMEM)
    outside = pl.BlockSpec(memory_space=pl.ANY)
    shape = jax.ShapeDtypeStruct
    home_shape = shape((images, experts, width), BF16)
    if backward:
        out_shape = [
            home_shape,
            shape((local, every, hidden), BF16),
            shape((local, every, hidden), BF16),
            shape((local, every, width), BF16),
            shape((8, every), F32),
        ]
        operands = (values, received, expert_in, expert_out)
        in_specs = [inside, inside, outside, outside]
        extra = [pltpu.VMEM((local, every, hidden), F32)]
    else:
        out_shape = [home_shape, shape((local, every, width), BF16)]
        operands = (values, expert_in, expert_out)
        in_specs = [inside, outside, outside]
        extra = []
    dma = pltpu.SemaphoreType.DMA
    return pl.pallas_call(
        kernel,
        in_specs=in_specs,
        out_specs=[inside] * len(out_shape),
        out_shape=out_shape,
        scratch_shapes=extra
        + [
            pltpu.VMEM((local, width, hidden), F32),
            pltpu.VMEM((local, hidden, width), F32),
            pltpu.VMEM((chips, rows, width), BF16),
            pltpu.VMEM((cores, chips, rows, width), BF16),
            pltpu.VMEM((local, cores, half, width), F32),
            pltpu.VMEM((local, half, width), BF16),
            pltpu.VMEM((local, half, width), BF16),
            pltpu.VMEM((local * half, width), BF16),
            pltpu.VMEM((chips, rows, width), BF16),
            pltpu.VMEM((chips, rows, width), BF16),
        ]
        + [dma((local,))] * 2
        + [dma((chips,))] * 4
        + [dma((local,))] * 2
        + [dma((chips,))] * 2,
        compiler_params=pltpu.CompilerParams(
            collective_id=collective_id, has_side_effects=True, vmem_limit_bytes=VMEM_BYTES
        ),
        cost_estimate=work_of(40),
        name="exchange_back" if backward else "exchange",
    )(*operands)


def expert_adam(weight, first, second, lefts, rights, scale, rate):
    layers, local, tall, wide = weight.shape
    deep = lefts[0].shape[1]
    each = 2 if local % 2 == 0 else 1

    def kernel(scale_ref, w_ref, m_ref, s_ref, *refs):
        left_refs, right_refs = refs[:layers], refs[layers : 2 * layers]
        new_w, new_m, new_s = refs[2 * layers :]

        for layer in range(layers):

            @pl.when(pl.program_id(0) == layer)
            def _(layer=layer):
                for e in range(each):
                    grad = tn(left_refs[layer][e], right_refs[layer][e]) * scale_ref[0]
                    moment = BETA_ONE * m_ref[e] + (1.0 - BETA_ONE) * grad
                    spread_of = BETA_TWO * s_ref[e] + (1.0 - BETA_TWO) * (grad * grad)
                    ratio = (moment * (1.0 / (1.0 - BETA_ONE**STEP))) / (
                        jnp.sqrt(spread_of * (1.0 / (1.0 - BETA_TWO**STEP))) + ADAM_EPS
                    )
                    held = w_ref[e]
                    new_m[e] = moment
                    new_s[e] = spread_of
                    new_w[e] = held - rate * (ratio + WEIGHT_DECAY * held)

    def factor_spec(layer, columns):
        last = local // each - 1
        return pl.BlockSpec(
            (each, deep, columns),
            lambda l, e: (jnp.where(l == layer, e, jnp.where(l < layer, 0, last)), 0, 0),
        )

    block = pl.BlockSpec((None, each, tall, wide), lambda l, e: (l, e, 0, 0))
    return pl.pallas_call(
        kernel,
        grid=(layers, local // each),
        in_specs=[pl.BlockSpec(memory_space=pltpu.SMEM)]
        + [block] * 3
        + [factor_spec(layer, tall) for layer in range(layers)]
        + [factor_spec(layer, wide) for layer in range(layers)],
        out_specs=[block] * 3,
        out_shape=[jax.ShapeDtypeStruct(weight.shape, F32)] * 3,
        compiler_params=pltpu.CompilerParams(vmem_limit_bytes=VMEM_BYTES),
        name="expert_adam",
    )(scale, weight, first, second, *lefts, *rights)


def level_pair(patches, resolution, labels):
    swap = [(0, 1), (1, 0)]
    images = resolution.shape[0]
    place = jnp.arange(images, dtype=jnp.int32)
    count = jnp.sum(resolution)
    other = lax.ppermute(count, "dp", swap)
    moves = jnp.abs(count - other) >= 2
    wanted = (count > other).astype(jnp.int32)
    at = jnp.min(jnp.where(resolution == wanted, place, images - 1))
    chosen = place == at
    out = lax.dynamic_slice_in_dim(patches, at, 1, 0)
    got = lax.ppermute(out, "dp", swap)
    label = lax.ppermute(jnp.sum(jnp.where(chosen, labels, 0)), "dp", swap)
    patches = lax.dynamic_update_slice_in_dim(patches, jnp.where(moves, got, out), at, 0)
    moved = chosen & moves
    return (
        patches,
        jnp.where(moved, 1 - resolution, resolution),
        jnp.where(moved, label, labels),
    )


def adam(weight, first, second, grad, rate):
    first = BETA_ONE * first + (1.0 - BETA_ONE) * grad
    second = BETA_TWO * second + (1.0 - BETA_TWO) * grad * grad
    ratio = first / (1.0 - BETA_ONE**STEP) / (jnp.sqrt(second / (1.0 - BETA_TWO**STEP)) + ADAM_EPS)
    return (weight - rate * (ratio + WEIGHT_DECAY * weight), first, second)


def on_device(
    patches,
    resolution,
    labels,
    dense_weights,
    attention,
    router,
    expert_in,
    expert_out,
    classifier,
    norm_table,
    dense_weights_first,
    dense_weights_second,
    attention_first,
    attention_second,
    router_first,
    router_second,
    expert_in_first,
    expert_in_second,
    expert_out_first,
    expert_out_second,
    classifier_first,
    classifier_second,
    norm_table_first,
    norm_table_second,
):
    layers = attention.shape[0]
    width = norm_table.shape[1]
    classes = classifier.shape[1]
    devices = lax.axis_size("dp") * lax.axis_size("fsdp")
    images = patches.shape[0] * devices
    interp = interp_matrix()
    position = norm_table[:LEN_LO]
    pos_high = jnp.dot(interp, position, precision=PRECISE)
    pos_low = jnp.pad(position, ((0, LEN - LEN_LO), (0, 0)))
    positions = jnp.stack([pos_low, pos_high])
    gains = [
        jnp.pad(norm_table[LEN_LO + 4 * layer : LEN_LO + 4 * layer + 4], ((0, 4), (0, 0)))
        for layer in range(layers)
    ]
    last_gains = jnp.pad(norm_table[LEN_LO + 4 * layers :], ((0, 6), (0, 0)))
    attention_t = attention.transpose(0, 2, 1).astype(BF16)
    router_t = router.transpose(0, 2, 1).astype(BF16)
    dense_t = dense_weights.T.astype(BF16)
    local = expert_in.shape[1]
    own = (
        lax.axis_size("dp") == 2
        and lax.axis_size("fsdp") == 1 << BITS
        and patches.shape[0] * local % 16 == 0
        and router.shape[1] * router.shape[2] % width == 0
    )
    if own:
        patches, resolution, labels = level_pair(patches, resolution, labels)
        dense, attention_one = gather_all([dense_t, attention_t[0]], 0)
    else:
        dense, attention_one = [
            lax.all_gather(part, ("dp", "fsdp"), axis=0, tiled=True)
            for part in (dense_t, attention_t[0])
        ]
    attention_all = [attention_one]
    router_all = [None]
    fetched = [None]
    for layer in range(1, layers):
        share = attention_t[layer]
        if layer > 1:
            share, attention_all[0] = lax.optimization_barrier((share, attention_all[0]))
        fetched.append(fetch_layer(share, router_t[layer - 1]))

    start, qkv, context, middle, hidden = first_forward(
        resolution, patches, dense, attention_all[0], positions, gains[0], width
    )
    kept = [(start, qkv, context, middle)]
    mixing = None
    for layer in range(1, layers):
        both = fetched[layer]
        if mixing is not None:
            both, last = lax.optimization_barrier((both, mixing[1]))
            mixing = (mixing[0], last)
        one, two = open_layer(both, attention_t.shape[1], router.shape[2], router.shape[1])
        attention_all.append(one)
        router_all.append(two)
        outs = sparse_forward(
            resolution, hidden, mixing, attention_all[layer], router_all[layer], gains[layer]
        )
        if mixing is not None:
            hidden = outs[0]
        qkv, context, middle, combine, slots = outs[-5:]
        if own:
            returned, received = exchange(layer - 1, slots, None, expert_in, expert_out, layer)
        else:
            returned, received = plain_exchange(layer - 1, slots, None, expert_in, expert_out)
        kept.append((hidden, qkv, context, middle, combine, returned, received))
        hidden = middle
        mixing = (combine, returned)

    packs = devices if own else None
    padding = -classes % 128 if not own else -classes % (16 * devices)
    head = jnp.pad(classifier[:width].astype(BF16), ((0, 0), (0, padding)))
    head_bias = jnp.pad(classifier[width:], ((0, 0), (0, padding)), constant_values=NEG_FILL)
    grad_hidden, grad_returned, grad_head, grad_bias, grad_last, loss_part = top(
        resolution, labels, middle, combine, returned, head, head_bias, last_gains, classes, images,
        packs,
    )
    attention_grads = [None] * layers
    router_grads = [None] * (layers - 1)
    gain_grads = [None] * layers
    layer_packs = [None] * layers
    in_factors = [None] * (layers - 1)
    out_factors = [None] * (layers - 1)
    local_squares = 0.0
    for layer in reversed(range(1, layers)):
        before, qkv, context, middle, combine, returned, received = kept[layer]
        if own:
            outs = exchange(
                layer - 1, grad_returned, received, expert_in, expert_out, layers + layer
            )
        else:
            outs = plain_exchange(layer - 1, grad_returned, received, expert_in, expert_out)
        grad_home, hid, grad_pre, grad_out, squares = outs
        local_squares = local_squares + jnp.sum(squares)
        in_factors[layer - 1] = (received, grad_pre)
        out_factors[layer - 1] = (hid, grad_out)
        below = kept[layer - 1][4] if layer > 1 else None
        outs = sparse_backward(
            resolution, before, qkv, context, middle, grad_hidden, returned, grad_home, below,
            attention_all[layer], router_all[layer], gains[layer], packs,
        )
        grad_hidden = outs[0]
        if below is not None:
            grad_returned = outs[1]
        grad_gain = outs[-1]
        if own:
            layer_packs[layer] = outs[-2]
        else:
            attention_grads[layer], router_grads[layer - 1] = outs[-3:-1]
        gain_grads[layer] = grad_gain[:4]
    start, qkv, context, middle = kept[0]
    outs = first_backward(
        resolution, patches, start, qkv, context, middle, grad_hidden, dense, attention_all[0],
        gains[0], packs,
    )
    grad_gain, grad_low, grad_high = outs[-3:]
    if own:
        layer_packs[0] = outs[0]
    else:
        grad_dense, attention_grads[0] = outs[:2]
    gain_grads[0] = grad_gain[:4]
    grad_pos = grad_low[:LEN_LO] + jnp.dot(interp.T, grad_high, precision=PRECISE)
    grad_table = jnp.concatenate([grad_pos] + gain_grads + [grad_last[:2]], 0)
    loss_local = loss_part[0, 0]
    part_rows, part_cols = router.shape[1:]
    table_rows = grad_table.shape[0]
    if own:
        bias_flat = grad_bias[0]
        bias_flat = jnp.pad(bias_flat, (0, -bias_flat.shape[0] % width)).reshape(-1, width)
        tail = jnp.concatenate([grad_table, bias_flat], 0).astype(BF16)
        tail = jnp.pad(tail, ((0, -tail.shape[0] % devices), (0, 0))).reshape(devices, -1, width)
        tail_each = tail.shape[1]
        tail = jnp.pad(tail, ((0, 0), (0, -tail_each % 16), (0, 0)))
        stats = jnp.concatenate(
            [
                jnp.broadcast_to(local_squares, (1, 128)),
                jnp.broadcast_to(loss_local, (1, 128)),
                jnp.zeros((6, 128), F32),
            ],
            0,
        )
        blocks = layer_packs + [grad_head, tail]
        starts = [sum(block.shape[1] for block in blocks[:at]) for at in range(layers)]
        columns = dense.shape[0] // devices
        part = attention_t.shape[1]
        router_at = [starts[layer] + part for layer in range(1, layers)]
        mine, shared, totals = reduce_all(
            blocks, stats, grad_head.shape[1] + tail.shape[1],
            [(at, at + part_cols) for at in router_at], 2 * layers,
        )
        shared = shared.reshape(devices, -1, width)
        head_each = grad_head.shape[1]
        head_all = shared[:, :head_each].reshape(-1, width)[:classes].T.astype(F32)
        tail_all = shared[:, head_each : head_each + tail_each].reshape(-1, width).astype(F32)
        shared_table = tail_all[:table_rows]
        bias_all = tail_all[table_rows:].reshape(-1)[None, :classes]
        shared_head = jnp.concatenate([head_all, bias_all], 0)
        norm = jnp.sqrt(totals[0, 0])
        loss_total = totals[1, 0]
        grad_first = mine[:columns].T
        attention_at = [columns] + starts[1:]
        grad_attention = jnp.stack([mine[at : at + part].T for at in attention_at])
        lane_at = lax.axis_index("dp") * part_rows
        grad_router_all = jnp.stack(
            [
                lax.dynamic_slice_in_dim(mine[at : at + part_cols], lane_at, part_rows, 1).T
                for at in router_at
            ]
        )
    else:
        grad_first = lax.psum_scatter(
            grad_dense, ("dp", "fsdp"), scatter_dimension=0, tiled=True
        ).T
        shares = [
            share_layer(attention_grads[layer], router_grads[layer - 1], part_cols, part_rows)
            for layer in range(1, layers)
        ]
        first_share = lax.psum_scatter(
            attention_grads[0], ("dp", "fsdp"), scatter_dimension=0, tiled=True
        )
        grad_attention = jnp.stack([first_share] + [share[0] for share in shares])
        grad_attention = grad_attention.transpose(0, 2, 1)
        grad_router_all = jnp.stack([share[1] for share in shares]).transpose(0, 2, 1)
        local_squares = (
            local_squares
            + jnp.sum(grad_first * grad_first)
            + jnp.sum(grad_attention * grad_attention)
            + jnp.sum(grad_router_all * grad_router_all)
        )
        grad_head = jnp.concatenate([grad_head[:classes].T, grad_bias[0:1, :classes]], 0)
        shared_head, shared_table, loss_total, squares = lax.psum(
            (grad_head, grad_table, loss_local, local_squares), ("dp", "fsdp")
        )
        norm = jnp.sqrt(
            squares + jnp.sum(shared_head * shared_head) + jnp.sum(shared_table * shared_table)
        )
    scale = jnp.minimum(1.0, CLIP_NORM / norm)
    scale_row = scale.reshape(1)

    def experts_updated(weight, first, second, factors, rate):
        lefts, rights = zip(*factors)
        return tuple(expert_adam(weight, first, second, lefts, rights, scale_row, rate))

    updates = (
        adam(dense_weights, dense_weights_first, dense_weights_second, grad_first * scale, LEARN_RATE),
        adam(attention, attention_first, attention_second, grad_attention * scale, ATTENTION_RATE),
        adam(router, router_first, router_second, grad_router_all * scale, LEARN_RATE),
        experts_updated(expert_in, expert_in_first, expert_in_second, in_factors, EXPERT_RATE),
        experts_updated(expert_out, expert_out_first, expert_out_second, out_factors, LEARN_RATE),
        adam(classifier, classifier_first, classifier_second, shared_head * scale, LEARN_RATE),
        adam(norm_table, norm_table_first, norm_table_second, shared_table * scale, TABLE_RATE),
    )
    return (loss_total, norm) + tuple(part for update in updates for part in update)


def solution(mesh):
    spread = P(("dp", "fsdp"))
    weights = (
        P(None, ("dp", "fsdp")),
        P(None, None, ("dp", "fsdp")),
        P(None, "dp", "fsdp"),
        P(None, "fsdp", None, "dp"),
        P(None, "fsdp", "dp", None),
        P(),
        P(),
    )
    moments = tuple(spec for spec in weights for _ in range(2))
    triples = tuple(spec for spec in weights for _ in range(3))
    return jax.shard_map(
        on_device,
        mesh=mesh,
        in_specs=(spread, spread, spread) + weights + moments,
        out_specs=(P(), P()) + triples,
        check_vma=False,
    )
```

```python
import functools

import jax
import jax.numpy as jnp
from jax import lax
from jax.experimental import pallas as pl
from jax.experimental.pallas import tpu as pltpu
from jax.sharding import PartitionSpec as P

HEADS = 6
FF = 1536
G_LO = 14
G_HI = 24
LEN = 576
LEN_LO = 196
ROWS_LO = 208
STEP = 10


LN_EPS = 1e-06
CLIP_NORM = 0.001
LEARN_RATE = 0.05
ATTENTION_RATE = 0.15
EXPERT_RATE = 1.0
TABLE_RATE = 0.5
BETA_ONE = 0.9
BETA_TWO = 0.95
ADAM_EPS = 1e-10
WEIGHT_DECAY = 0.1
SMOOTH = 0.1
NEG_FILL = -1e30
PRECISE = lax.Precision.HIGHEST
F32 = jnp.float32
BF16 = jnp.bfloat16
VMEM_BYTES = 60 * 1024 * 1024


def interp_matrix():
    rows = jnp.arange(G_HI, dtype=jnp.float32)[:, None]
    cols = jnp.arange(G_LO, dtype=jnp.float32)[None, :]
    weight = jnp.maximum(0.0, 1.0 - jnp.abs(rows * (G_LO - 1) - cols * (G_HI - 1)) / (G_HI - 1))
    return (weight[:, None, :, None] * weight[None, :, None, :]).reshape(G_HI * G_HI, G_LO * G_LO)


def matmul(left, right, form):
    return jnp.einsum(form, left, right, preferred_element_type=jnp.float32)


def contract(left, right, left_dim, right_dim):
    return lax.dot_general(
        left, right, (((left_dim,), (right_dim,)), ((), ())), preferred_element_type=F32
    )


def nn(left, right):
    return contract(left, right, 1, 0)


def nt(left, right):
    return contract(left, right, 1, 1)


def tn(left, right):
    return contract(left, right, 0, 0)


def normalise(values):
    center = values - jnp.mean(values, -1, keepdims=True)
    rate = lax.rsqrt(jnp.mean(center * center, -1, keepdims=True) + LN_EPS)
    return center * rate, rate


def normalise_back(unit, rate, gain, grad):
    scaled = grad * gain
    inner = scaled - jnp.mean(scaled, -1, keepdims=True)
    grad_in = rate * (inner - unit * jnp.mean(scaled * unit, -1, keepdims=True))
    return (
        grad_in,
        jnp.sum(grad * unit, 0, keepdims=True),
        jnp.sum(grad, 0, keepdims=True),
    )


def row_number(shape):
    return lax.broadcasted_iota(jnp.int32, shape, 0)


def side_masks():
    lane = lax.broadcasted_iota(jnp.int32, (1, 128), 1)
    first = (lane < 64).astype(F32)
    return (first.astype(BF16), (1.0 - first).astype(BF16))


def lanes(offset):
    return pl.ds(pl.multiple_of(offset, 128), 128)


GELU_RATE = 0.7978845608028654


def gelu(v):
    return 0.5 * v * (1.0 + jnp.tanh(GELU_RATE * (v + 0.044715 * (v * v * v))))


def gelu_both(v):
    square = v * v
    bend = jnp.tanh(GELU_RATE * (v + 0.044715 * (square * v)))
    half = 0.5 * (1.0 + bend)
    slope = half + 0.5 * v * (1.0 - bend * bend) * (GELU_RATE * (1.0 + 3 * 0.044715 * square))
    return v * half, slope


def attention_rows(rows, limit, qkv, context):
    width = context.shape[1]
    first = lax.broadcasted_iota(jnp.int32, (rows, 128), 1) < 64
    masks = side_masks()
    ones = jnp.ones((rows, 128), BF16)
    for offset in range(0, width, 128):
        query = qkv[:rows, offset : offset + 128] * BF16(0.125)
        keys = qkv[:rows, width + offset : width + offset + 128]
        values = qkv[:rows, 2 * width + offset : 2 * width + offset + 128]
        summing = jnp.concatenate([values, ones], 1)
        found = []
        for side in (0, 1):
            scores = nt(query * masks[side], keys)
            if limit is not None:
                lane = lax.broadcasted_iota(jnp.int32, (rows, rows), 1)
                scores = jnp.where(lane < limit, scores, NEG_FILL)
            raised = jnp.exp(scores - jnp.max(scores, 1, keepdims=True))
            both = nn(raised.astype(BF16), summing)
            found.append(both[:, :128] * (1.0 / both[:, 128:]))
        context[:rows, offset : offset + 128] = jnp.where(first, found[0], found[1]).astype(BF16)


def scores_back(limit, keys, values, query, grad):
    scores = nt(keys, query)
    if limit is not None:
        scores = jnp.where(row_number(scores.shape) < limit, scores, NEG_FILL)
    raised = jnp.exp(scores - jnp.max(scores, 0, keepdims=True))
    probs = raised * (1.0 / jnp.sum(raised, 0, keepdims=True))
    grad_values = nn(probs.astype(BF16), grad)
    grad_probs = nt(values, grad)
    mixed = jnp.sum(probs * grad_probs, 0, keepdims=True)
    grad_scores = (probs * (grad_probs - mixed)).astype(BF16)
    return grad_scores, nn(grad_scores, query), grad_values


def attention_rows_back(rows, limit, qkv, grad_context, grad_qkv):
    width = grad_context.shape[1]
    masks = side_masks()
    first = lax.broadcasted_iota(jnp.int32, (rows, 128), 1) < 64

    def pair(offset):
        query = qkv[:rows, lanes(offset)] * BF16(0.125)
        keys = qkv[:rows, lanes(width + offset)]
        values = qkv[:rows, lanes(2 * width + offset)]
        grad = grad_context[:rows, lanes(offset)]
        queries = [query * mask for mask in masks]
        grads = [grad * mask for mask in masks]
        if limit is None:
            grad_scores, grad_keys, grad_values = scores_back(
                limit, keys, values, jnp.concatenate(queries, 0), jnp.concatenate(grads, 0)
            )
            both = tn(grad_scores, keys)
            grad_query = jnp.where(first, both[:rows], both[rows:])
        else:
            one, two = [
                scores_back(limit, keys, values, queries[side], grads[side]) for side in (0, 1)
            ]
            grad_query = tn(one[0], keys * masks[0]) + tn(two[0], keys * masks[1])
            grad_keys, grad_values = one[1] + two[1], one[2] + two[2]
        grad_qkv[:rows, lanes(offset)] = (grad_query * 0.125).astype(BF16)
        grad_qkv[:rows, lanes(width + offset)] = grad_keys.astype(BF16)
        grad_qkv[:rows, lanes(2 * width + offset)] = grad_values.astype(BF16)

    if limit is None:

        def step(index, carry):
            pair(index * 128)
            return carry

        lax.fori_loop(0, width // 128, step, 0)
    else:
        for offset in range(0, width, 128):
            pair(offset)


def attention_forward(rows, limit, hidden, gains, weights, qkv, context):
    width = hidden.shape[1]
    unit, _ = normalise(hidden)
    normed = (unit * gains[0:1] + gains[1:2]).astype(BF16)
    qkv[:rows] = nt(normed, weights[: 3 * width]).astype(BF16)
    attention_rows(rows, limit, qkv, context)
    return hidden + nn(context[:rows], weights[3 * width :])


def attention_backward(
    rows, limit, hidden, grad_middle, gains, weights, qkv, context, hold_context, hold_qkv,
    grad_weights, grad_gains,
):
    width = hidden.shape[1]
    grad_b = grad_middle.astype(BF16)
    hold_context[:rows] = nt(grad_b, weights[3 * width :]).astype(BF16)
    grad_weights[3 * width :] += tn(context[:rows], grad_b)
    attention_rows_back(rows, limit, qkv, hold_context, hold_qkv)
    unit, rate = normalise(hidden)
    normed = (unit * gains[0:1] + gains[1:2]).astype(BF16)
    grad_weights[: 3 * width] += tn(hold_qkv[:rows], normed)
    grad_normed = nn(hold_qkv[:rows], weights[: 3 * width])
    grad_in, grad_gain, grad_bias = normalise_back(unit, rate, gains[0:1], grad_normed)
    grad_gains[0:1] += grad_gain
    grad_gains[1:2] += grad_bias
    return grad_middle + grad_in


def mlp_forward(rows, middle, gains, weights, pixels):
    unit, _ = normalise(middle)
    normed = (unit * gains[2:3] + gains[3:4]).astype(BF16)
    chunk = middle.shape[1]
    total = middle
    for start in range(0, FF, chunk):
        pre = nt(normed, weights[pixels + start : pixels + start + chunk])
        out = weights[pixels + FF + start : pixels + FF + start + chunk]
        total = total + nn(gelu(pre).astype(BF16), out)
    return total


def mlp_backward(rows, middle, grad, gains, weights, pixels, grad_weights, grad_gains):
    unit, rate = normalise(middle)
    normed = (unit * gains[2:3] + gains[3:4]).astype(BF16)
    grad_b = grad.astype(BF16)
    chunk = middle.shape[1]
    grad_normed = None
    for start in range(0, FF, chunk):
        first = slice(pixels + start, pixels + start + chunk)
        second = slice(pixels + FF + start, pixels + FF + start + chunk)
        hid, slope = gelu_both(nt(normed, weights[first]))
        grad_weights[second] += tn(hid.astype(BF16), grad_b)
        grad_pre = (nt(grad_b, weights[second]) * slope).astype(BF16)
        grad_weights[first] += tn(grad_pre, normed)
        part = nn(grad_pre, weights[first])
        grad_normed = part if grad_normed is None else grad_normed + part
    grad_in, grad_gain, grad_bias = normalise_back(unit, rate, gains[2:3], grad_normed)
    grad_gains[2:3] += grad_gain
    grad_gains[3:4] += grad_bias
    return grad + grad_in


def route(limit, middle, gains, router):
    unit, rate = normalise(middle)
    normed = (unit * gains[2:3] + gains[3:4]).astype(BF16)
    logits = nt(normed, router[...])
    masked = logits
    if limit is not None:
        masked = jnp.where(row_number(logits.shape) < limit, logits, NEG_FILL)
    raised = jnp.exp(masked - jnp.max(masked, 0, keepdims=True))
    dispatch = raised * (1.0 / jnp.sum(raised, 0, keepdims=True))
    raised = jnp.exp(logits - jnp.max(logits, 1, keepdims=True))
    combine = raised * (1.0 / jnp.sum(raised, 1, keepdims=True))
    return unit, rate, normed, dispatch, combine


def masked_rows(limit, values):
    if limit is None:
        return values
    return jnp.where(row_number(values.shape) < limit, values, 0.0)


def work_of(giga):
    return pl.CostEstimate(flops=giga * 10**9, bytes_accessed=1 << 20, transcendentals=0)


def by_image(name, body, scalars, per_image, whole, out_image, out_sum, scratch=(), pack=None):
    images = scalars[0].shape[0]
    inner = pack[0] if pack else 0
    packed = 1 if pack else 0
    counts = (
        len(scalars), len(per_image), len(whole), len(out_image), packed, len(out_sum) - inner,
        inner, len(scratch),
    )

    def kernel(*refs):
        groups, at = [], 0
        for count in counts:
            groups.append(refs[at : at + count])
            at += count
        index = pl.program_id(0)
        sums = tuple(groups[6]) + tuple(groups[5])

        @pl.when(index == 0)
        def _():
            for ref in sums:
                ref[...] = jnp.zeros_like(ref)

        numbers = [ref[index] for ref in groups[0]]
        given = (*groups[1:4], sums, groups[7])

        @pl.when(numbers[0] == 1)
        def _():
            body(LEN, None, numbers, *given)

        @pl.when(numbers[0] != 1)
        def _():
            body(ROWS_LO, LEN_LO + numbers[0], numbers, *given)

        if pack:

            @pl.when(index == images - 1)
            def _():
                def write(device, carry):
                    groups[4][0][device] = pack[3](sums, device).astype(BF16)
                    return carry

                lax.fori_loop(0, pack[1], write, 0)

    width = out_sum[0][1] if pack else 0
    pack_shapes = [(pack[1], pack[2], width)] if pack else []

    def image_spec(shape):
        return pl.BlockSpec((None,) + tuple(shape[1:]), lambda i, *_: (i, 0, 0))

    return pl.pallas_call(
        kernel,
        grid_spec=pltpu.PrefetchScalarGridSpec(
            num_scalar_prefetch=len(scalars),
            grid=(images,),
            in_specs=[image_spec(a.shape) for a in per_image]
            + [pl.BlockSpec(memory_space=pltpu.VMEM) for _ in whole],
            out_specs=[image_spec((images,) + shape) for shape, _ in out_image]
            + [pl.BlockSpec(shape, lambda i, *_: (0, 0, 0)) for shape in pack_shapes]
            + [pl.BlockSpec(shape, lambda i, *_: (0, 0)) for shape in out_sum[inner:]],
            scratch_shapes=[pltpu.VMEM(shape, F32) for shape in out_sum[:inner]] + list(scratch),
        ),
        out_shape=[jax.ShapeDtypeStruct((images,) + shape, dtype) for shape, dtype in out_image]
        + [jax.ShapeDtypeStruct(shape, BF16) for shape in pack_shapes]
        + [jax.ShapeDtypeStruct(shape, F32) for shape in out_sum[inner:]],
        compiler_params=pltpu.CompilerParams(vmem_limit_bytes=VMEM_BYTES),
        cost_estimate=work_of(images * 8),
        name=name,
    )(*scalars, *per_image, *whole)


def rows_of(ref, device, count):
    return ref[pl.ds(pl.multiple_of(device * count, 8), count)]


def padded_rows(blocks):
    rows = sum(block.shape[0] for block in blocks)
    if rows % 16:
        blocks = blocks + [jnp.zeros((-rows % 16, blocks[0].shape[1]), F32)]
    return jnp.concatenate(blocks, 0) if len(blocks) > 1 else blocks[0]


def up_16(count):
    return count + -count % 16


def first_forward(resolution, patches, dense, attention, positions, gains, width):
    pixels = patches.shape[2]

    def body(rows, limit, numbers, images, whole, outs, sums, scratch):
        dense_ref, attention_ref, position_ref, gain_ref = whole
        start, qkv, context, middle, last = outs
        place = position_ref[0 if limit is not None else 1, :rows]
        embedded = masked_rows(limit, nn(images[0][:rows], dense_ref[:pixels]) + place)
        start[:rows] = embedded
        middle_rows = attention_forward(
            rows, limit, embedded, gain_ref, attention_ref, qkv, context
        )
        middle[:rows] = middle_rows
        last[:rows] = mlp_forward(rows, middle_rows, gain_ref, dense_ref, pixels)

    return by_image(
        "first_forward",
        body,
        [resolution],
        [patches],
        [dense, attention, positions, gains],
        [
            ((LEN, width), F32),
            ((LEN, 3 * width), BF16),
            ((LEN, width), BF16),
            ((LEN, width), F32),
            ((LEN, width), F32),
        ],
        [],
    )


def sparse_forward(resolution, hidden, mixing, attention, router, gains):
    width = hidden.shape[2]
    experts = router.shape[0]

    def body(rows, limit, numbers, images, whole, outs, sums, scratch):
        attention_ref, router_ref, gain_ref = whole
        before, qkv, context, middle, combine, slots = ([None] + list(outs))[-6:]
        hidden_rows = images[0][:rows]
        if mixing is not None:
            hidden_rows = hidden_rows + nn(images[1][:rows], images[2][...])
            before[:rows] = hidden_rows
        middle_rows = attention_forward(
            rows, limit, hidden_rows, gain_ref, attention_ref, qkv, context
        )
        middle[:rows] = middle_rows
        _, _, normed, dispatch, share = route(limit, middle_rows, gain_ref, router_ref)
        combine[:rows] = share.astype(BF16)
        slots[...] = tn(dispatch.astype(BF16), normed).astype(BF16)

    outs = [
        ((LEN, 3 * width), BF16),
        ((LEN, width), BF16),
        ((LEN, width), F32),
        ((LEN, experts), BF16),
        ((experts, width), BF16),
    ]
    if mixing is not None:
        outs = [((LEN, width), F32)] + outs
    return by_image(
        "sparse_forward",
        body,
        [resolution],
        [hidden] + list(mixing or ()),
        [attention, router, gains],
        outs,
        [],
    )


def top(resolution, labels, middle, combine, returned, head, head_bias, last_gains, classes, images, devices):
    width = middle.shape[2]
    experts = returned.shape[1]
    padded = head.shape[1]

    def body(rows, limit, numbers, per_image, whole, outs, sums, scratch):
        middle_ref, combine_ref, returned_ref = per_image
        head_ref, bias_ref, gain_ref = whole
        grad_hidden, grad_returned = outs
        grad_head, grad_bias_row, grad_gains, loss = sums
        length = float(LEN if limit is None else LEN_LO)
        share = combine_ref[:rows]
        hidden = middle_ref[:rows] + nn(share, returned_ref[...])
        unit, rate = normalise(hidden)
        normed = masked_rows(limit, unit * gain_ref[0:1] + gain_ref[1:2])
        pooled = jnp.sum(normed, 0, keepdims=True) * (1.0 / length)
        one_row = (row_number((8, width)) == 0).astype(F32)
        pooled_b = (one_row * pooled).astype(BF16)
        logits = nn(pooled_b, head_ref[...])[0:1] + bias_ref[...]
        shifted = logits - jnp.max(logits, 1, keepdims=True)
        raised = jnp.exp(shifted)
        total = jnp.sum(raised, 1, keepdims=True)
        log_probs = shifted - jnp.log(total)
        lane = lax.broadcasted_iota(jnp.int32, (1, padded), 1)
        target = jnp.where(lane == numbers[1], 1.0 - SMOOTH, 0.0) + jnp.where(
            lane < classes, SMOOTH / classes, 0.0
        )
        picked = jnp.sum(target * log_probs, 1, keepdims=True)
        loss[...] += jnp.broadcast_to(picked * (-1.0 / images), loss.shape)
        grad_logits = (raised * (1.0 / total) - target) * (1.0 / images)
        grad_bias_row[0:1] += grad_logits
        row_mask = (row_number((8, padded)) == 0).astype(F32)
        grad_logits_b = (row_mask * grad_logits).astype(BF16)
        grad_head[...] += tn(grad_logits_b, pooled_b)
        grad_pooled = nt(grad_logits_b, head_ref[...])[0:1] * (1.0 / length)
        grad_normed = masked_rows(limit, jnp.broadcast_to(grad_pooled, (rows, width)))
        grad_rows, grad_gain, grad_bias = normalise_back(
            unit, rate, gain_ref[0:1], grad_normed
        )
        grad_gains[0:1] += grad_gain
        grad_gains[1:2] += grad_bias
        grad_hidden[:rows] = grad_rows
        grad_returned[...] = tn(share, grad_rows.astype(BF16)).astype(BF16)

    return by_image(
        "top",
        body,
        [resolution, labels],
        [middle, combine, returned],
        [head, head_bias, last_gains],
        [((LEN, width), F32), ((experts, width), BF16)],
        [(padded, width), (8, padded), (8, width), (8, 128)],
        pack=devices
        and (
            1, devices, padded // devices,
            lambda sums, device: rows_of(sums[0], device, padded // devices),
        ),
    )


def sparse_backward(
    resolution, hidden, qkv, context, middle, grad_hidden, returned, grad_home, below, attention,
    router, gains, devices,
):
    width = middle.shape[2]
    experts = router.shape[0]
    chips = lax.axis_size("fsdp")
    local = experts // chips

    def body(rows, limit, numbers, images, whole, outs, sums, scratch):
        hidden_ref, qkv_ref, context_ref, middle_ref, grad_ref, returned_ref, home_ref = images[:7]
        attention_ref, router_ref, gain_ref = whole
        grad_attention, grad_router, grad_gains = sums
        grad = grad_ref[:rows]
        grad_combine = nt(grad.astype(BF16), returned_ref[...])
        unit, rate, normed, dispatch, share = route(
            limit, middle_ref[:rows], gain_ref, router_ref
        )
        home = home_ref[...]
        grad_dispatch = nt(normed, home)
        grad_normed = nn(dispatch.astype(BF16), home)
        grad_route = dispatch * (
            grad_dispatch - jnp.sum(grad_dispatch * dispatch, 0, keepdims=True)
        ) + share * (grad_combine - jnp.sum(grad_combine * share, 1, keepdims=True))
        grad_route_b = grad_route.astype(BF16)
        grad_router[...] += tn(grad_route_b, normed)
        grad_normed = grad_normed + nn(grad_route_b, router_ref[...])
        grad_in, grad_gain, grad_bias = normalise_back(unit, rate, gain_ref[2:3], grad_normed)
        grad_gains[2:3] += grad_gain
        grad_gains[3:4] += grad_bias
        grad_rows = attention_backward(
            rows, limit, hidden_ref[:rows], grad + grad_in, gain_ref, attention_ref, qkv_ref,
            context_ref, scratch[0], scratch[1], grad_attention, grad_gains,
        )
        outs[0][:rows] = grad_rows
        if below is not None:
            outs[1][...] = tn(images[7][:rows], grad_rows.astype(BF16)).astype(BF16)

    outs = [((LEN, width), F32)]
    if below is not None:
        outs.append(((experts, width), BF16))
    return by_image(
        "sparse_backward",
        body,
        [resolution],
        [hidden, qkv, context, middle, grad_hidden, returned, grad_home]
        + ([] if below is None else [below]),
        [attention, router, gains],
        outs,
        [(4 * width, width), (experts, width), (8, width)],
        [pltpu.VMEM((LEN, width), BF16), pltpu.VMEM((LEN, 3 * width), BF16)],
        pack=devices
        and (
            2, devices, up_16(4 * width // devices + local),
            lambda sums, device: padded_rows(
                [
                    rows_of(sums[0], device, 4 * width // devices),
                    rows_of(sums[1], device % chips, local),
                ]
            ),
        ),
    )


def first_backward(
    resolution, patches, start, qkv, context, middle, grad_hidden, dense, attention, gains, devices
):
    width = middle.shape[2]
    pixels = patches.shape[2]
    columns = dense.shape[0]

    def body(rows, limit, numbers, images, whole, outs, sums, scratch):
        patches_ref, start_ref, qkv_ref, context_ref, middle_ref, grad_ref = images
        dense_ref, attention_ref, gain_ref = whole
        grad_dense, grad_attention, grad_gains, grad_low, grad_high = sums
        grad_middle = mlp_backward(
            rows, middle_ref[:rows], grad_ref[:rows], gain_ref, dense_ref, pixels, grad_dense,
            grad_gains,
        )
        grad_rows = attention_backward(
            rows, limit, start_ref[:rows], grad_middle, gain_ref, attention_ref, qkv_ref,
            context_ref, scratch[0], scratch[1], grad_attention, grad_gains,
        )
        grad_rows = masked_rows(limit, grad_rows)
        grad_dense[:pixels] += tn(patches_ref[:rows], grad_rows.astype(BF16))
        if limit is None:
            grad_high[...] += grad_rows
        else:
            grad_low[...] += grad_rows

    return by_image(
        "first_backward",
        body,
        [resolution],
        [patches, start, qkv, context, middle, grad_hidden],
        [dense, attention, gains],
        [],
        [(columns, width), (4 * width, width), (8, width), (ROWS_LO, width), (LEN, width)],
        [pltpu.VMEM((LEN, width), BF16), pltpu.VMEM((LEN, 3 * width), BF16)],
        pack=devices
        and (
            2, devices, up_16((columns + 4 * width) // devices),
            lambda sums, device: padded_rows(
                [
                    rows_of(sums[0], device, columns // devices),
                    rows_of(sums[1], device, 4 * width // devices),
                ]
            ),
        ),
    )


def to_experts(values):
    return lax.all_to_all(values, "fsdp", split_axis=1, concat_axis=0, tiled=True)


def from_experts(values):
    return lax.all_to_all(values, "fsdp", split_axis=0, concat_axis=1, tiled=True)


def all_rows(values):
    return lax.all_gather(to_experts(values), "dp", axis=0, tiled=True).transpose(1, 0, 2)


def rows_home(part):
    shared = lax.psum_scatter(part.transpose(1, 0, 2), "dp", scatter_dimension=0, tiled=True)
    return from_experts(shared.astype(BF16))


def plain_exchange(layer, values, received, expert_in, expert_out):
    win, wout = expert_in[layer].astype(BF16), expert_out[layer].astype(BF16)
    rows = all_rows(values)
    if received is None:
        hid = gelu(matmul(rows, win, "end,edf->enf")).astype(BF16)
        return rows_home(matmul(hid, wout, "enf,efd->end")), rows
    hid, slope = gelu_both(matmul(received, win, "end,edf->enf"))
    hid = hid.astype(BF16)
    grad_pre = (matmul(rows, wout, "end,efd->enf") * slope).astype(BF16)
    home = rows_home(matmul(grad_pre, win, "enf,edf->end"))

    def gram(values):
        return matmul(values, values, "enk,emk->enm")

    squares = gram(received) * gram(grad_pre) + gram(hid) * gram(rows)
    return home, hid, grad_pre, rows, jnp.sum(squares, (0, 1)).reshape(1, -1)


def fetch_layer(attention_t, router_t):
    width = attention_t.shape[1]
    flat = router_t.reshape(-1)
    pack = jnp.concatenate(
        [attention_t, jnp.pad(flat, (0, -flat.size % width)).reshape(-1, width)], 0
    )
    return lax.all_gather(pack, ("dp", "fsdp"), axis=0)


def open_layer(both, part, part_cols, part_rows):
    width = both.shape[2]
    rows_dp = lax.axis_size("dp")
    cols_fsdp = lax.axis_size("fsdp")
    router = (
        both[:, part:]
        .reshape(rows_dp * cols_fsdp, -1)[:, : part_cols * part_rows]
        .reshape(rows_dp, cols_fsdp, part_cols, part_rows)
        .transpose(1, 2, 0, 3)
        .reshape(cols_fsdp * part_cols, rows_dp * part_rows)
    )
    return both[:, :part].reshape(-1, width), router


def share_layer(grad_attention, grad_router, part_cols, part_rows):
    rows_dp = lax.axis_size("dp")
    cols_fsdp = lax.axis_size("fsdp")
    devices = rows_dp * cols_fsdp
    width = grad_attention.shape[1]
    router = (
        grad_router.reshape(cols_fsdp, part_cols, rows_dp, part_rows)
        .transpose(2, 0, 1, 3)
        .reshape(devices, -1)
    )
    router = jnp.pad(router, ((0, 0), (0, -part_cols * part_rows % width)))
    router = router.reshape(devices, -1, width)
    pack = jnp.concatenate([grad_attention.reshape(devices, -1, width), router], 1)
    mine = lax.psum_scatter(pack, ("dp", "fsdp"), scatter_dimension=0, tiled=False)
    part = grad_attention.shape[0] // devices
    return mine[:part], mine[part:].reshape(-1)[: part_cols * part_rows].reshape(part_cols, part_rows)


BITS = 4
GATHER_ORDERS = ((3, 2, 0, 1), (0, 1, 2, 3), (0, 1, 3, 2))
MESH_IDS = pl.DeviceIdType.MESH


def my_bits():
    at = lax.axis_index("fsdp")
    return [(at // (1 << (BITS - 1 - bit))) % 2 for bit in range(BITS)]


def partner_of(bit):
    at = lax.axis_index("fsdp")
    step = 1 << (BITS - 1 - bit)
    return (lax.axis_index("dp"), at + step * (1 - 2 * ((at // step) % 2)))


def sibling():
    return (1 - lax.axis_index("dp"), lax.axis_index("fsdp"))


def greet_partners():
    barrier = pltpu.get_barrier_semaphore()
    others = [partner_of(bit) for bit in range(BITS)] + [sibling()]
    for other in others:
        pl.semaphore_signal(barrier, inc=1, device_id=other, device_id_type=MESH_IDS)
    pl.semaphore_wait(barrier, len(others))


def send(source, target, send_sem, recv_sem, device):
    copy = pltpu.make_async_remote_copy(
        src_ref=source,
        dst_ref=target,
        send_sem=send_sem,
        recv_sem=recv_sem,
        device_id=device,
        device_id_type=MESH_IDS,
    )
    copy.start()
    return copy


def spread(parts, sems):
    mine = my_bits()
    core = lax.axis_index("dp")
    to_send, to_get, pass_send, pass_get = sems

    def view(part, stage, other):
        ref, lane_part, order = part
        index = []
        for bit in range(BITS):
            if bit in order[:stage]:
                index.append(slice(None))
            elif other and bit == order[stage]:
                index.append(1 - mine[bit])
            else:
                index.append(mine[bit])
        return ref.at[(core, *index, slice(None), lane_part)]

    def go(number, stage):
        block = view(parts[number], stage, False)
        return send(
            block, block, to_send.at[number, stage], to_get.at[number, stage],
            partner_of(parts[number][2][stage]),
        )

    def hand_over(number, slot, block):
        return send(block, block, pass_send.at[number, slot], pass_get.at[number, slot], sibling())

    going = [go(number, 0) for number in range(len(parts))]
    handed = [
        hand_over(number, BITS, view(parts[number], 0, False)) for number in range(len(parts))
    ]
    for stage in range(BITS):
        for number in range(len(parts)):
            going[number].wait()
            if stage + 1 < BITS:
                going[number] = go(number, stage + 1)
            handed.append(hand_over(number, stage, view(parts[number], stage, True)))
    for copy in handed:
        copy.wait()


def spread_sems(count):
    return [pltpu.SemaphoreType.DMA((count, BITS + 1)) for _ in range(4)]


def lane_parts(width):
    return [slice(start, start + 128) for start in range(0, width, 128)]


def gather_all(shards, collective_id):
    count = len(shards)
    width = shards[0].shape[1]
    cuts = lane_parts(width)

    def kernel(*refs):
        ins, outs, sems = refs[:count], refs[count : 2 * count], refs[2 * count :]
        place = (lax.axis_index("dp"), *my_bits())
        for ref, out in zip(ins, outs):
            out[place] = ref[...]
        greet_partners()
        spread(
            [
                (out, cut, GATHER_ORDERS[number % 3])
                for number, cut in enumerate(cuts)
                for out in outs
            ],
            sems,
        )

    outs = pl.pallas_call(
        kernel,
        in_specs=[pl.BlockSpec(memory_space=pltpu.VMEM)] * count,
        out_specs=[pl.BlockSpec(memory_space=pltpu.VMEM)] * count,
        out_shape=[jax.ShapeDtypeStruct((2,) * (BITS + 1) + s.shape, s.dtype) for s in shards],
        scratch_shapes=spread_sems(count * len(cuts)),
        compiler_params=pltpu.CompilerParams(
            collective_id=collective_id, has_side_effects=True, vmem_limit_bytes=VMEM_BYTES
        ),
        cost_estimate=work_of(40),
        name="gather_all",
    )(*shards)
    return [out.reshape(-1, width) for out in outs]


def reduce_all(grads, stats, shared, halved, collective_id):
    width = grads[0].shape[2]
    count = len(grads)
    starts = [sum(grad.shape[1] for grad in grads[:at]) for at in range(count + 1)]
    rows = starts[-1]
    cuts = lane_parts(width)
    parts = len(cuts)
    orders = [tuple(reversed(GATHER_ORDERS[number % 3])) for number in range(parts)]

    def kernel(*refs):
        grads_refs = refs[:count]
        stats_ref, mine_ref, shared_ref, total_ref = refs[count : count + 4]
        scratch = refs[count + 4 :]
        sums, first_get = scratch[:2]
        gets = scratch[2 : 2 + BITS]
        stats_all = scratch[2 + BITS]
        local_sem, pair_send, pair_get, to_send, to_get = scratch[3 + BITS : 8 + BITS]
        sems = scratch[8 + BITS :]
        core = lax.axis_index("dp")
        bits = my_bits()
        places = [
            (number, at, cut, slice(starts[at], starts[at + 1]))
            for number, cut in enumerate(cuts)
            for at in range(count)
        ]
        local = {
            (number, at): pltpu.make_async_copy(
                grads_refs[at].at[core, :, :, :, :, :, cut],
                sums.at[:, :, :, :, span, cut],
                local_sem.at[number, at],
            )
            for number, at, cut, span in places
        }
        for copy in local.values():
            copy.start()
        greet_partners()
        pairs = {
            (number, at): send(
                grads_refs[at].at[1 - core, :, :, :, :, :, cut],
                first_get.at[:, :, :, :, span, cut],
                pair_send.at[number, at],
                pair_get.at[number, at],
                sibling(),
            )
            for number, at, cut, span in places
        }

        def index(number, stage, own):
            order = orders[number]
            found = []
            for bit in range(BITS):
                if bit in order[:stage]:
                    found.append(bits[bit])
                elif bit == order[stage]:
                    found.append(bits[bit] if own else 1 - bits[bit])
                else:
                    found.append(slice(None))
            return (*found, slice(None), cuts[number])

        def go(number, stage):
            return send(
                sums.at[index(number, stage, False)],
                gets[stage].at[number],
                to_send.at[number, stage],
                to_get.at[number, stage],
                partner_of(orders[number][stage]),
            )

        going = [None] * parts
        turns = [number for number in range(parts) if number % 3] + list(range(0, parts, 3))
        for number in reversed(turns):
            for at in range(count):
                local[number, at].wait()
                pairs[number, at].wait()
            whole = (slice(None),) * (BITS + 1) + (cuts[number],)
            sums[whole] = sums[whole] + first_get[whole]
            going[number] = go(number, 0)
        place = tuple(bits)
        for stage in range(BITS):
            for number in turns:
                going[number].wait()
                if stage + 1 < BITS:
                    at = index(number, stage, True)
                    sums[at] = sums[at] + gets[stage][number]
                    going[number] = go(number, stage + 1)
                else:
                    at = index(number, stage, True)
                    mine_ref[:, cuts[number]] = sums[at].astype(F32) + gets[stage][number].astype(F32)
        mine = mine_ref[...]
        row = row_number((rows, width))
        counted = mine * mine
        for low, high in halved:
            counted = jnp.where((row >= low) & (row < high), 0.5 * counted, counted)
        squares = jnp.sum(jnp.sum(counted, 0, keepdims=True), 1, keepdims=True)
        top_row = (row_number((8, 128)) == 0).astype(F32)
        stats_all[(core, *place)] = stats_ref[...] + top_row * squares
        shared_ref[(core, *place)] = mine_ref[rows - shared :, :].astype(BF16)
        spread(
            [
                (shared_ref, cut, GATHER_ORDERS[number % 3]) for number, cut in enumerate(cuts)
            ]
            + [(stats_all, slice(0, 128), GATHER_ORDERS[1])],
            sems,
        )
        total_ref[...] = jnp.sum(stats_all[...].reshape(32, 8, 128), 0)

    grid = (2,) * BITS
    return pl.pallas_call(
        kernel,
        in_specs=[pl.BlockSpec(memory_space=pl.ANY)] * count
        + [pl.BlockSpec(memory_space=pltpu.VMEM)],
        out_specs=[pl.BlockSpec(memory_space=pltpu.VMEM)] * 3,
        out_shape=[
            jax.ShapeDtypeStruct((rows, width), F32),
            jax.ShapeDtypeStruct((2,) + grid + (shared, width), BF16),
            jax.ShapeDtypeStruct((8, 128), F32),
        ],
        scratch_shapes=[pltpu.VMEM(grid + (rows, width), BF16)] * 2
        + [pltpu.VMEM((parts,) + (2,) * (BITS - 1 - stage) + (rows, 128), BF16) for stage in range(BITS)]
        + [pltpu.VMEM((2,) + grid + (8, 128), F32)]
        + [pltpu.SemaphoreType.DMA((parts, count))] * 3
        + [pltpu.SemaphoreType.DMA((parts, BITS))] * 2
        + spread_sems(parts + 1),
        compiler_params=pltpu.CompilerParams(
            collective_id=collective_id, has_side_effects=True, vmem_limit_bytes=VMEM_BYTES
        ),
        cost_estimate=work_of(60),
        name="reduce_all",
    )(*[grad.reshape((2,) + grid + grad.shape[1:]) for grad in grads], stats)


def chip(at):
    return (lax.axis_index("dp"), at)


def greet_all(chips):
    barrier = pltpu.get_barrier_semaphore()
    me = lax.axis_index("fsdp")

    def one(step, carry):
        pl.semaphore_signal(
            barrier, inc=1, device_id=chip((me + step) % chips), device_id_type=MESH_IDS
        )
        return carry

    lax.fori_loop(1, chips, one, 0)
    pl.semaphore_signal(barrier, inc=1, device_id=sibling(), device_id_type=MESH_IDS)
    pl.semaphore_wait(barrier, chips)


def swap_start(chips, source, target, send_sem, get_sem):
    me = lax.axis_index("fsdp")

    def one(step, carry):
        other = (me + step) % chips
        send(source.at[other], target.at[me], send_sem.at[other], get_sem.at[me], chip(other))
        return carry

    lax.fori_loop(1, chips, one, 0)


def swap_sent(chips, step, source, target, send_sem, get_sem):
    me = lax.axis_index("fsdp")
    to = (me + step) % chips
    pltpu.make_async_remote_copy(
        src_ref=source.at[to], dst_ref=target.at[me], send_sem=send_sem.at[to],
        recv_sem=get_sem.at[me], device_id=chip(to), device_id_type=MESH_IDS,
    ).wait_send()


def swap_arrived(chips, step, source, target, send_sem, get_sem):
    origin = (lax.axis_index("fsdp") + chips - step) % chips
    pltpu.make_async_remote_copy(
        src_ref=source.at[origin], dst_ref=target.at[origin], send_sem=send_sem.at[origin],
        recv_sem=get_sem.at[origin], device_id=chip(origin), device_id_type=MESH_IDS,
    ).wait_recv()
    return origin


def exchange(layer, values, received, expert_in, expert_out, collective_id):
    images, experts, width = values.shape
    chips = lax.axis_size("fsdp")
    cores = lax.axis_size("dp")
    local, _, hidden = expert_in.shape[1:]
    rows = images * local
    half = chips * images
    every = cores * half
    backward = received is not None

    def kernel(*refs):
        if backward:
            values_ref, received_ref, in_ref, out_ref = refs[:4]
            home_ref, hid_ref, pre_ref, gout_ref, squares_ref = refs[4:9]
            slope_ref = refs[9]
            scratch = refs[10:]
        else:
            values_ref, in_ref, out_ref = refs[:3]
            home_ref, received_ref = refs[3:5]
            scratch = refs[5:]
        win, wout, outbox, inbox, parts, pair_out, pair_in, sorted_ref, backbox, homebox = scratch[:10]
        win_sem, wout_sem, send_one, get_one, pass_send, pass_get, pair_send, pair_get, send_two, get_two = scratch[10:]
        core = lax.axis_index("dp")
        me = lax.axis_index("fsdp")

        def fetch(e):
            return (
                pltpu.make_async_copy(in_ref.at[layer, e], win.at[e], win_sem.at[e]),
                pltpu.make_async_copy(out_ref.at[layer, e], wout.at[e], wout_sem.at[e]),
            )

        def start_fetch(e, carry):
            for copy in fetch(e):
                copy.start()
            return carry

        lax.fori_loop(0, local, start_fetch, 0)
        whole = [values_ref[image].astype(F32) for image in range(images)]
        for at in range(chips):
            outbox[at] = jnp.concatenate(
                [one[at * local : (at + 1) * local] for one in whole], 0
            ).astype(BF16)
        greet_all(chips)
        swap_start(chips, outbox, inbox.at[core], send_one, get_one)
        inbox[core, me] = outbox[me]

        def hand(at):
            block = inbox.at[core, at]
            return pltpu.make_async_remote_copy(
                src_ref=block, dst_ref=block, send_sem=pass_send.at[at],
                recv_sem=pass_get.at[at], device_id=sibling(), device_id_type=MESH_IDS,
            )

        def handed(at):
            block = inbox.at[1 - core, at]
            return pltpu.make_async_remote_copy(
                src_ref=block, dst_ref=block, send_sem=pass_send.at[at],
                recv_sem=pass_get.at[at], device_id=sibling(), device_id_type=MESH_IDS,
            )

        hand(me).start()
        if backward:

            def ahead(e, carry):
                for copy in fetch(e):
                    copy.wait()
                rec = received_ref[e]
                hid, slope = gelu_both(nn(rec, win[e].astype(BF16)))
                slope_ref[e] = slope
                hid_ref[e] = hid.astype(BF16)
                return carry

            lax.fori_loop(0, local, ahead, 0)

        def arrive(step, carry):
            hand(swap_arrived(chips, step, outbox, inbox.at[core], send_one, get_one)).start()
            return carry

        lax.fori_loop(1, chips, arrive, 0)

        def all_handed(at, carry):
            handed(at).wait_recv()
            return carry

        lax.fori_loop(0, chips, all_handed, 0)
        arrived = inbox[...].reshape(every * local, width)
        pick_row = lax.broadcasted_iota(jnp.int32, (every, every * local), 0)
        pick_col = lax.broadcasted_iota(jnp.int32, (every, every * local), 1)
        wanted = pick_row * local - pick_col

        def pair_copy(e):
            return pltpu.make_async_remote_copy(
                src_ref=pair_out.at[e], dst_ref=pair_in.at[e], send_sem=pair_send.at[e],
                recv_sem=pair_get.at[e], device_id=sibling(), device_id_type=MESH_IDS,
            )

        if backward:
            squares_ref[...] = jnp.zeros_like(squares_ref)

        def work(e, carry):
            pick = (wanted == -e).astype(F32).astype(BF16)
            mine = nn(pick, arrived).astype(BF16)
            if backward:
                gout_ref[e] = mine
                grad_pre = (nt(mine, wout[e].astype(BF16)) * slope_ref[e]).astype(BF16)
                pre_ref[e] = grad_pre
                part = nt(grad_pre, win[e].astype(BF16))
                rec, hid = received_ref[e], hid_ref[e]
                product = nt(rec, rec) * nt(grad_pre, grad_pre) + nt(hid, hid) * nt(mine, mine)
                squares_ref[...] += jnp.sum(product.reshape(every // 8, 8, every), 0)
            else:
                for copy in fetch(e):
                    copy.wait()
                received_ref[e] = mine
                hid = gelu(nn(mine, win[e].astype(BF16))).astype(BF16)
                part = nn(hid, wout[e].astype(BF16))
            parts[e] = part.reshape(cores, half, width)
            pair_out[e] = parts[e, 1 - core].astype(BF16)
            pair_copy(e).start()
            return carry

        lax.fori_loop(0, local, work, 0)

        def add(e, carry):
            pair_copy(e).wait_recv()
            sorted_ref[pl.ds(pl.multiple_of(e * half, half), half)] = (
                parts[e, core] + pair_in[e].astype(F32)
            ).astype(BF16)
            return carry

        lax.fori_loop(0, local, add, 0)
        back_row = lax.broadcasted_iota(jnp.int32, (half * local, half * local), 0)
        back_col = lax.broadcasted_iota(jnp.int32, (half * local, half * local), 1)
        back = (back_row == (back_col % half) * local + back_col // half).astype(F32).astype(BF16)
        backbox[...] = nn(back, sorted_ref[...]).astype(BF16).reshape(chips, rows, width)
        swap_start(chips, backbox, homebox, send_two, get_two)
        homebox[me] = backbox[me]

        def home(step, carry):
            swap_arrived(chips, step, backbox, homebox, send_two, get_two)
            return carry

        lax.fori_loop(1, chips, home, 0)
        blocks = [homebox[at].astype(F32) for at in range(chips)]
        for image in range(images):
            home_ref[image] = jnp.concatenate(
                [block[image * local : (image + 1) * local] for block in blocks], 0
            ).astype(BF16)

        def drain(step, carry):
            swap_sent(chips, step, outbox, inbox.at[core], send_one, get_one)
            swap_sent(chips, step, backbox, homebox, send_two, get_two)
            return carry

        lax.fori_loop(1, chips, drain, 0)

        def drain_pass(at, carry):
            hand(at).wait_send()
            return carry

        lax.fori_loop(0, chips, drain_pass, 0)

        def drain_pair(e, carry):
            pair_copy(e).wait_send()
            return carry

        lax.fori_loop(0, local, drain_pair, 0)

    inside = pl.BlockSpec(memory_space=pltpu.VMEM)
    outside = pl.BlockSpec(memory_space=pl.ANY)
    shape = jax.ShapeDtypeStruct
    home_shape = shape((images, experts, width), BF16)
    if backward:
        out_shape = [
            home_shape,
            shape((local, every, hidden), BF16),
            shape((local, every, hidden), BF16),
            shape((local, every, width), BF16),
            shape((8, every), F32),
        ]
        operands = (values, received, expert_in, expert_out)
        in_specs = [inside, inside, outside, outside]
        extra = [pltpu.VMEM((local, every, hidden), F32)]
    else:
        out_shape = [home_shape, shape((local, every, width), BF16)]
        operands = (values, expert_in, expert_out)
        in_specs = [inside, outside, outside]
        extra = []
    dma = pltpu.SemaphoreType.DMA
    return pl.pallas_call(
        kernel,
        in_specs=in_specs,
        out_specs=[inside] * len(out_shape),
        out_shape=out_shape,
        scratch_shapes=extra
        + [
            pltpu.VMEM((local, width, hidden), F32),
            pltpu.VMEM((local, hidden, width), F32),
            pltpu.VMEM((chips, rows, width), BF16),
            pltpu.VMEM((cores, chips, rows, width), BF16),
            pltpu.VMEM((local, cores, half, width), F32),
            pltpu.VMEM((local, half, width), BF16),
            pltpu.VMEM((local, half, width), BF16),
            pltpu.VMEM((local * half, width), BF16),
            pltpu.VMEM((chips, rows, width), BF16),
            pltpu.VMEM((chips, rows, width), BF16),
        ]
        + [dma((local,))] * 2
        + [dma((chips,))] * 4
        + [dma((local,))] * 2
        + [dma((chips,))] * 2,
        compiler_params=pltpu.CompilerParams(
            collective_id=collective_id, has_side_effects=True, vmem_limit_bytes=VMEM_BYTES
        ),
        cost_estimate=work_of(40),
        name="exchange_back" if backward else "exchange",
    )(*operands)


def expert_adam(weight, first, second, lefts, rights, scale, rate):
    layers, local, tall, wide = weight.shape
    deep = lefts[0].shape[1]
    each = 2 if local % 2 == 0 else 1

    def kernel(scale_ref, w_ref, m_ref, s_ref, *refs):
        left_refs, right_refs = refs[:layers], refs[layers : 2 * layers]
        new_w, new_m, new_s = refs[2 * layers :]

        for layer in range(layers):

            @pl.when(pl.program_id(0) == layer)
            def _(layer=layer):
                for e in range(each):
                    grad = tn(left_refs[layer][e], right_refs[layer][e]) * scale_ref[0]
                    moment = BETA_ONE * m_ref[e] + (1.0 - BETA_ONE) * grad
                    spread_of = BETA_TWO * s_ref[e] + (1.0 - BETA_TWO) * (grad * grad)
                    ratio = (moment * (1.0 / (1.0 - BETA_ONE**STEP))) / (
                        jnp.sqrt(spread_of * (1.0 / (1.0 - BETA_TWO**STEP))) + ADAM_EPS
                    )
                    held = w_ref[e]
                    new_m[e] = moment
                    new_s[e] = spread_of
                    new_w[e] = held - rate * (ratio + WEIGHT_DECAY * held)

    def factor_spec(layer, columns):
        last = local // each - 1
        return pl.BlockSpec(
            (each, deep, columns),
            lambda l, e: (jnp.where(l == layer, e, jnp.where(l < layer, 0, last)), 0, 0),
        )

    block = pl.BlockSpec((None, each, tall, wide), lambda l, e: (l, e, 0, 0))
    return pl.pallas_call(
        kernel,
        grid=(layers, local // each),
        in_specs=[pl.BlockSpec(memory_space=pltpu.SMEM)]
        + [block] * 3
        + [factor_spec(layer, tall) for layer in range(layers)]
        + [factor_spec(layer, wide) for layer in range(layers)],
        out_specs=[block] * 3,
        out_shape=[jax.ShapeDtypeStruct(weight.shape, F32)] * 3,
        compiler_params=pltpu.CompilerParams(vmem_limit_bytes=VMEM_BYTES),
        name="expert_adam",
    )(scale, weight, first, second, *lefts, *rights)


def level_pair(patches, resolution, labels):
    swap = [(0, 1), (1, 0)]
    images = resolution.shape[0]
    place = jnp.arange(images, dtype=jnp.int32)
    facts = lax.ppermute(jnp.stack([resolution, labels]), "dp", swap)
    count, other = jnp.sum(resolution), jnp.sum(facts[0])
    moves = jnp.abs(count - other) >= 2
    wanted = (count > other).astype(jnp.int32)

    def first_of(numbers, value):
        return jnp.min(jnp.where(numbers == value, place, images - 1))

    at = first_of(resolution, wanted)
    chosen = place == at
    out = lax.dynamic_slice_in_dim(patches, at, 1, 0)
    got = lax.ppermute(out, "dp", swap)
    label = jnp.sum(jnp.where(place == first_of(facts[0], 1 - wanted), facts[1], 0))
    patches = lax.dynamic_update_slice_in_dim(patches, jnp.where(moves, got, out), at, 0)
    moved = chosen & moves
    return (
        patches,
        jnp.where(moved, 1 - resolution, resolution),
        jnp.where(moved, label, labels),
    )


def adam(weight, first, second, grad, rate):
    first = BETA_ONE * first + (1.0 - BETA_ONE) * grad
    second = BETA_TWO * second + (1.0 - BETA_TWO) * grad * grad
    ratio = first / (1.0 - BETA_ONE**STEP) / (jnp.sqrt(second / (1.0 - BETA_TWO**STEP)) + ADAM_EPS)
    return (weight - rate * (ratio + WEIGHT_DECAY * weight), first, second)


def on_device(
    patches,
    resolution,
    labels,
    dense_weights,
    attention,
    router,
    expert_in,
    expert_out,
    classifier,
    norm_table,
    dense_weights_first,
    dense_weights_second,
    attention_first,
    attention_second,
    router_first,
    router_second,
    expert_in_first,
    expert_in_second,
    expert_out_first,
    expert_out_second,
    classifier_first,
    classifier_second,
    norm_table_first,
    norm_table_second,
):
    layers = attention.shape[0]
    width = norm_table.shape[1]
    classes = classifier.shape[1]
    devices = lax.axis_size("dp") * lax.axis_size("fsdp")
    images = patches.shape[0] * devices
    interp = interp_matrix()
    position = norm_table[:LEN_LO]
    pos_high = jnp.dot(interp, position, precision=PRECISE)
    pos_low = jnp.pad(position, ((0, LEN - LEN_LO), (0, 0)))
    positions = jnp.stack([pos_low, pos_high])
    gains = [
        jnp.pad(norm_table[LEN_LO + 4 * layer : LEN_LO + 4 * layer + 4], ((0, 4), (0, 0)))
        for layer in range(layers)
    ]
    last_gains = jnp.pad(norm_table[LEN_LO + 4 * layers :], ((0, 6), (0, 0)))
    attention_t = attention.transpose(0, 2, 1).astype(BF16)
    router_t = router.transpose(0, 2, 1).astype(BF16)
    dense_t = dense_weights.T.astype(BF16)
    local = expert_in.shape[1]
    own = (
        lax.axis_size("dp") == 2
        and lax.axis_size("fsdp") == 1 << BITS
        and patches.shape[0] * local % 16 == 0
        and router.shape[1] * router.shape[2] % width == 0
    )
    if own:
        patches, resolution, labels = level_pair(patches, resolution, labels)
        dense, attention_one = gather_all([dense_t, attention_t[0]], 0)
    else:
        dense, attention_one = [
            lax.all_gather(part, ("dp", "fsdp"), axis=0, tiled=True)
            for part in (dense_t, attention_t[0])
        ]
    attention_all = [attention_one]
    router_all = [None]
    fetched = [None]
    for layer in range(1, layers):
        share = attention_t[layer]
        if layer > 1:
            share, attention_all[0] = lax.optimization_barrier((share, attention_all[0]))
        fetched.append(fetch_layer(share, router_t[layer - 1]))

    start, qkv, context, middle, hidden = first_forward(
        resolution, patches, dense, attention_all[0], positions, gains[0], width
    )
    kept = [(start, qkv, context, middle)]
    mixing = None
    for layer in range(1, layers):
        both = fetched[layer]
        if mixing is not None:
            both, last = lax.optimization_barrier((both, mixing[1]))
            mixing = (mixing[0], last)
        one, two = open_layer(both, attention_t.shape[1], router.shape[2], router.shape[1])
        attention_all.append(one)
        router_all.append(two)
        outs = sparse_forward(
            resolution, hidden, mixing, attention_all[layer], router_all[layer], gains[layer]
        )
        if mixing is not None:
            hidden = outs[0]
        qkv, context, middle, combine, slots = outs[-5:]
        if own:
            returned, received = exchange(layer - 1, slots, None, expert_in, expert_out, layer)
        else:
            returned, received = plain_exchange(layer - 1, slots, None, expert_in, expert_out)
        kept.append((hidden, qkv, context, middle, combine, returned, received))
        hidden = middle
        mixing = (combine, returned)

    packs = devices if own else None
    padding = -classes % 128 if not own else -classes % (16 * devices)
    head = jnp.pad(classifier[:width].astype(BF16), ((0, 0), (0, padding)))
    head_bias = jnp.pad(classifier[width:], ((0, 0), (0, padding)), constant_values=NEG_FILL)
    grad_hidden, grad_returned, grad_head, grad_bias, grad_last, loss_part = top(
        resolution, labels, middle, combine, returned, head, head_bias, last_gains, classes, images,
        packs,
    )
    attention_grads = [None] * layers
    router_grads = [None] * (layers - 1)
    gain_grads = [None] * layers
    layer_packs = [None] * layers
    in_factors = [None] * (layers - 1)
    out_factors = [None] * (layers - 1)
    local_squares = 0.0
    for layer in reversed(range(1, layers)):
        before, qkv, context, middle, combine, returned, received = kept[layer]
        if own:
            outs = exchange(
                layer - 1, grad_returned, received, expert_in, expert_out, layers + layer
            )
        else:
            outs = plain_exchange(layer - 1, grad_returned, received, expert_in, expert_out)
        grad_home, hid, grad_pre, grad_out, squares = outs
        local_squares = local_squares + jnp.sum(squares)
        in_factors[layer - 1] = (received, grad_pre)
        out_factors[layer - 1] = (hid, grad_out)
        below = kept[layer - 1][4] if layer > 1 else None
        outs = sparse_backward(
            resolution, before, qkv, context, middle, grad_hidden, returned, grad_home, below,
            attention_all[layer], router_all[layer], gains[layer], packs,
        )
        grad_hidden = outs[0]
        if below is not None:
            grad_returned = outs[1]
        grad_gain = outs[-1]
        if own:
            layer_packs[layer] = outs[-2]
        else:
            attention_grads[layer], router_grads[layer - 1] = outs[-3:-1]
        gain_grads[layer] = grad_gain[:4]
    start, qkv, context, middle = kept[0]
    outs = first_backward(
        resolution, patches, start, qkv, context, middle, grad_hidden, dense, attention_all[0],
        gains[0], packs,
    )
    grad_gain, grad_low, grad_high = outs[-3:]
    if own:
        layer_packs[0] = outs[0]
    else:
        grad_dense, attention_grads[0] = outs[:2]
    gain_grads[0] = grad_gain[:4]
    grad_pos = grad_low[:LEN_LO] + jnp.dot(interp.T, grad_high, precision=PRECISE)
    grad_table = jnp.concatenate([grad_pos] + gain_grads + [grad_last[:2]], 0)
    loss_local = loss_part[0, 0]
    part_rows, part_cols = router.shape[1:]
    table_rows = grad_table.shape[0]
    if own:
        bias_flat = grad_bias[0]
        bias_flat = jnp.pad(bias_flat, (0, -bias_flat.shape[0] % width)).reshape(-1, width)
        tail = jnp.concatenate([grad_table, bias_flat], 0).astype(BF16)
        tail = jnp.pad(tail, ((0, -tail.shape[0] % devices), (0, 0))).reshape(devices, -1, width)
        tail_each = tail.shape[1]
        tail = jnp.pad(tail, ((0, 0), (0, -tail_each % 16), (0, 0)))
        stats = jnp.concatenate(
            [
                jnp.broadcast_to(local_squares, (1, 128)),
                jnp.broadcast_to(loss_local, (1, 128)),
                jnp.zeros((6, 128), F32),
            ],
            0,
        )
        blocks = layer_packs + [grad_head, tail]
        starts = [sum(block.shape[1] for block in blocks[:at]) for at in range(layers)]
        columns = dense.shape[0] // devices
        part = attention_t.shape[1]
        router_at = [starts[layer] + part for layer in range(1, layers)]
        mine, shared, totals = reduce_all(
            blocks, stats, grad_head.shape[1] + tail.shape[1],
            [(at, at + part_cols) for at in router_at], 2 * layers,
        )
        shared = shared.reshape(devices, -1, width)
        head_each = grad_head.shape[1]
        head_all = shared[:, :head_each].reshape(-1, width)[:classes].T.astype(F32)
        tail_all = shared[:, head_each : head_each + tail_each].reshape(-1, width).astype(F32)
        shared_table = tail_all[:table_rows]
        bias_all = tail_all[table_rows:].reshape(-1)[None, :classes]
        shared_head = jnp.concatenate([head_all, bias_all], 0)
        norm = jnp.sqrt(totals[0, 0])
        loss_total = totals[1, 0]
        grad_first = mine[:columns].T
        attention_at = [columns] + starts[1:]
        grad_attention = jnp.stack([mine[at : at + part].T for at in attention_at])
        lane_at = lax.axis_index("dp") * part_rows
        grad_router_all = jnp.stack(
            [
                lax.dynamic_slice_in_dim(mine[at : at + part_cols], lane_at, part_rows, 1).T
                for at in router_at
            ]
        )
    else:
        grad_first = lax.psum_scatter(
            grad_dense, ("dp", "fsdp"), scatter_dimension=0, tiled=True
        ).T
        shares = [
            share_layer(attention_grads[layer], router_grads[layer - 1], part_cols, part_rows)
            for layer in range(1, layers)
        ]
        first_share = lax.psum_scatter(
            attention_grads[0], ("dp", "fsdp"), scatter_dimension=0, tiled=True
        )
        grad_attention = jnp.stack([first_share] + [share[0] for share in shares])
        grad_attention = grad_attention.transpose(0, 2, 1)
        grad_router_all = jnp.stack([share[1] for share in shares]).transpose(0, 2, 1)
        local_squares = (
            local_squares
            + jnp.sum(grad_first * grad_first)
            + jnp.sum(grad_attention * grad_attention)
            + jnp.sum(grad_router_all * grad_router_all)
        )
        grad_head = jnp.concatenate([grad_head[:classes].T, grad_bias[0:1, :classes]], 0)
        shared_head, shared_table, loss_total, squares = lax.psum(
            (grad_head, grad_table, loss_local, local_squares), ("dp", "fsdp")
        )
        norm = jnp.sqrt(
            squares + jnp.sum(shared_head * shared_head) + jnp.sum(shared_table * shared_table)
        )
    scale = jnp.minimum(1.0, CLIP_NORM / norm)
    scale_row = scale.reshape(1)

    def experts_updated(weight, first, second, factors, rate):
        lefts, rights = zip(*factors)
        return tuple(expert_adam(weight, first, second, lefts, rights, scale_row, rate))

    updates = (
        adam(dense_weights, dense_weights_first, dense_weights_second, grad_first * scale, LEARN_RATE),
        adam(attention, attention_first, attention_second, grad_attention * scale, ATTENTION_RATE),
        adam(router, router_first, router_second, grad_router_all * scale, LEARN_RATE),
        experts_updated(expert_in, expert_in_first, expert_in_second, in_factors, EXPERT_RATE),
        experts_updated(expert_out, expert_out_first, expert_out_second, out_factors, LEARN_RATE),
        adam(classifier, classifier_first, classifier_second, shared_head * scale, LEARN_RATE),
        adam(norm_table, norm_table_first, norm_table_second, shared_table * scale, TABLE_RATE),
    )
    return (loss_total, norm) + tuple(part for update in updates for part in update)


def solution(mesh):
    spread = P(("dp", "fsdp"))
    weights = (
        P(None, ("dp", "fsdp")),
        P(None, None, ("dp", "fsdp")),
        P(None, "dp", "fsdp"),
        P(None, "fsdp", None, "dp"),
        P(None, "fsdp", "dp", None),
        P(),
        P(),
    )
    moments = tuple(spec for spec in weights for _ in range(2))
    triples = tuple(spec for spec in weights for _ in range(3))
    return jax.shard_map(
        on_device,
        mesh=mesh,
        in_specs=(spread, spread, spread) + weights + moments,
        out_specs=(P(), P()) + triples,
        check_vma=False,
    )
```
